32 devices in a mesh: grp: 2 (over x), clu: 16 (over z, y, core).
Axes of the slice: x: 2, y: 2, z: 4, core: 2. Of those that a mesh axis runs over, the one named last changes fastest.
Arguments:
- raw_rows: bfloat16 [262144, 256], P(('grp', 'clu')), parts along dimension 0, may hold values from -6 to 6
- enc_weight: bfloat16 [256, 256], replicated, may hold values from -0.375 to 0.375
- counts: int32 [32, 256], P(('grp', 'clu')), parts along dimension 0, may hold values from 1 to 64, 8192 in all within a row
- member_rows: int32 [32, 8192], P(('grp', 'clu')), parts along dimension 0, may hold values from 0 to 8191, each once within a row
- pool: int32 [32, 1024], P(('grp', 'clu')), parts along dimension 0, may hold values from 0 to 4095, as said below
- picks: int32 [4096, 100], P(('grp', 'clu')), parts along dimension 0, may hold values from 0 to 1023, all different within a row
- queries: bfloat16 [4096, 256], P(('grp', 'clu')), parts along dimension 0, may hold values from -6 to 6
- attn_weights: bfloat16 [4, 256, 256], replicated, may hold values from -0.375 to 0.375
- out_grad: bfloat16 [4096, 256], P(('grp', 'clu')), parts along dimension 0, may hold values from -6 to 6
Outputs:
- grad_query: bfloat16 [4096, 256], P(('grp', 'clu')), parts along dimension 0
- grad_rows: bfloat16 [262144, 256], P(('grp', 'clu')), parts along dimension 0
- grad_attn: float32 [8, 256, 256], P('grp'), parts along dimension 0
- grad_encoder: float32 [512, 256], P('grp'), parts along dimension 0
The draws below stay inside these ranges and needn't reach their ends.
There are 2 independent parts, one for each index of `grp`. The reference program is written for one: setup_inputs(seed, part) draws one part's arguments, and reference() takes and returns one part's arrays. A program takes and returns all parts, laid end to end along the dimension named above; an argument that names none is the same for every part. Nothing has to cross between parts.
Inputs may be any that keep to these rules, and one draw needn't show every extreme that they name: `counts`: row o sums to 8192. `member_rows`: each row holds every number of 0 to 8191 once. `pool`: in each row, entries 64 * o to 64 * o + 63 are 64 different clusters of owner o, that is of o * 256 to o * 256 + 255. `picks`: the 100 entries of a row are different.
All inputs are finite; a program needn't handle non-finite values.
Results may differ from the reference program's by a relative error of at most 0.012.
Values may be sent and summed in bfloat16 or wider, within the bound.
No kernel may reach another device: no remote copies, remote signals or barrier semaphores. Data moves between devices by JAX's collectives and lax.ppermute only.
A program may use at most 128 MiB of HBM per device.

```python
import math
import jax
import jax.numpy as jnp
import numpy as np
from jax import lax

D = 256
D_RAW = 256
HEADS = 4
K = 100
MEMB = 64
CL_DEV = 256
TGT_DEV = 128
P_SIZE = 64
ROW_DEV = 8192
CLUSTERS = 4096
ROWS = 131072
TARGETS = 2048
N_CLU = 16


def draw_pool(key, part):
    key = jax.random.fold_in(key, 7)
    pair_keys = jax.random.split(key, N_CLU * N_CLU)
    local = jax.vmap(lambda single: jax.random.permutation(single, CL_DEV)[:P_SIZE])(pair_keys)
    owners = jnp.tile(jnp.arange(N_CLU, dtype=jnp.int32), N_CLU)
    chosen = local.astype(jnp.int32) + (owners * CL_DEV)[:, None]
    return chosen.reshape(N_CLU, N_CLU * P_SIZE).astype(jnp.int32)


def levels(key, shape, cuts, low, largest):
    gain = 1.0
    for axis_at, shards_of in cuts:
        draws = jax.random.uniform(jax.random.fold_in(jax.random.fold_in(key, 6), axis_at), (shards_of,), jnp.float32, low / len(cuts), largest / len(cuts))
        gain = gain * jnp.repeat(jnp.exp(draws), shape[axis_at] // shards_of).reshape((-1,) + (1,) * (len(shape) - 1 - axis_at))
    return gain


def distinct(own_key, rows, count, top, lift):
    ranking = jax.random.permutation(jax.random.fold_in(own_key, 1), count)
    favour = ranking
    for power in range(3):
        favour = favour * favour // count
    favour = favour * lift // count
    lots = jax.random.randint(jax.random.fold_in(own_key, 2), (rows, count), 0, 4096) + favour
    sure = jax.random.permutation(jax.random.fold_in(own_key, 3), rows)[jnp.arange(count) % rows]
    lots = jnp.where(jnp.arange(rows)[:, None] == sure[None, :], 1 << 14, lots)
    score = lots * count + jnp.arange(count)
    return lax.top_k(score.astype(jnp.int32), top)[1].astype(jnp.int32)


def profile(number_of, total, bound, skew):
    weights = [(1 << 20) // math.isqrt(grade ** skew) + 1 for grade in range(2, number_of + 1)]
    surplus, holding = total - bound - (number_of - 1), [1] * (number_of - 1)
    while surplus > 0:
        free = [i for i in range(number_of - 1) if holding[i] < bound]
        mass, left = sum([weights[i] for i in free]), surplus
        for i in free:
            addition = min(bound - holding[i], max(1, left * weights[i] // mass), surplus)
            holding[i] = holding[i] + addition
            surplus = surplus - addition
    return np.array([bound] + holding)


def uneven_parts(rng, number_of, total, bound, skew):
    if number_of == 2:
        one = jax.random.randint(rng, (), max(1, total - bound), min(bound, total - 1) + 1)
        return jnp.stack([one, total - one])
    tallies = jnp.asarray(profile(number_of, total, bound, skew), jnp.int32)
    pairs = (number_of - 1) // 2
    source_of, receiver = tallies[1:1 + 2 * pairs:2], tallies[2:2 + 2 * pairs:2]
    room = jnp.minimum(source_of - 1, bound - receiver)
    passed = jax.random.randint(jax.random.fold_in(rng, 1), (pairs,), 0, 1 << 20) % (room + 1)
    tallies = tallies.at[1:1 + 2 * pairs:2].set(source_of - passed).at[2:2 + 2 * pairs:2].set(receiver + passed)
    return tallies[jax.random.permutation(jax.random.fold_in(rng, 2), number_of)]


def centred(own_key, extent, scale, bound, cuts=(), kind=jnp.bfloat16):
    values = scale * jax.random.normal(own_key, extent, jnp.float32)
    if cuts:
        values = values * levels(own_key, extent, cuts, -0.22, 0.18)
    return jnp.clip(values, -bound, bound).astype(kind)


def setup_inputs(seed: int = 0, part: int = 0) -> dict:
    key_of = jax.random.split(jax.random.key(seed), 10)
    part_splits = jax.random.split(jax.random.fold_in(key_of[9], part), 10)
    raw_rows = centred(part_splits[0], (ROWS, D_RAW), 1.0, 6.0, ((0, 16),))
    enc_weight = centred(key_of[1], (D_RAW, D), D_RAW ** -0.5, 0.375)
    counts = jax.vmap(lambda own: uneven_parts(own, CL_DEV, ROW_DEV, MEMB, 2))(jax.random.split(part_splits[2], N_CLU)).reshape((N_CLU, CL_DEV)).astype(jnp.int32)
    member_rows = jax.vmap(lambda own: jax.random.permutation(own, ROW_DEV))(jax.random.split(part_splits[3], N_CLU)).reshape((N_CLU, ROW_DEV)).astype(jnp.int32)
    pool = draw_pool(jax.random.fold_in(jax.random.fold_in(key_of[9], part), 71), part)
    picks = distinct(part_splits[5], TARGETS, N_CLU * P_SIZE, K, 800)
    queries = centred(part_splits[6], (TARGETS, D), 1.0, 6.0, ((0, 16),))
    attn_weights = centred(key_of[7], (4, D, D), D ** -0.5, 0.375)
    out_grad = centred(part_splits[8], (TARGETS, D), 1.0, 6.0, ((0, 16),))
    return {"raw_rows": raw_rows, "enc_weight": enc_weight, "counts": counts, "member_rows": member_rows, "pool": pool, "picks": picks, "queries": queries, "attn_weights": attn_weights, "out_grad": out_grad}


highest = lax.Precision.HIGHEST

def cluster_means(behavior, counts_row, members):
    row_count = members.shape[0]
    cluster_count = counts_row.shape[0]
    owner_of = jnp.repeat(jnp.arange(cluster_count, dtype=jnp.int32), counts_row, total_repeat_length=row_count)
    totals = jax.ops.segment_sum(behavior[members].astype(jnp.float32), owner_of, cluster_count)
    return ((totals / counts_row[:, None].astype(jnp.float32)).astype(jnp.bfloat16), owner_of)

def expand_rows(cluster_grad, counts_row, members, owner_of):
    shares = cluster_grad[owner_of] / counts_row[owner_of][:, None].astype(jnp.float32)
    return jnp.zeros(shares.shape, jnp.bfloat16).at[members].set(shares.astype(jnp.bfloat16))

def backward_block(query_rows, key_rows, value_rows, grad_out, weights):
    targets = query_rows.shape[0]
    pick_count = key_rows.shape[1]
    width = query_rows.shape[1]
    head_size = width // HEADS
    scale = 1.0 / math.sqrt(head_size)
    query_proj = jnp.dot(query_rows, weights[0], preferred_element_type=jnp.float32).astype(jnp.bfloat16)
    query_heads = query_proj.astype(jnp.float32).reshape(targets, HEADS, head_size)
    key_heads = key_rows.astype(jnp.float32).reshape(targets, pick_count, HEADS, head_size)
    value_heads = value_rows.astype(jnp.float32).reshape(targets, pick_count, HEADS, head_size)
    scores = jnp.einsum('thd,tkhd->thk', query_heads, key_heads) * scale
    attend = jax.nn.softmax(scores, axis=-1)
    attend_low = attend.astype(jnp.bfloat16)
    mixed = jnp.einsum('thk,tkhd->thd', attend_low.astype(jnp.float32), value_heads)
    mixed = mixed.reshape(targets, width).astype(jnp.bfloat16)
    grad_wo = jnp.dot(mixed.T, grad_out, preferred_element_type=jnp.float32)
    grad_mixed = jnp.dot(grad_out, weights[3].T, preferred_element_type=jnp.float32).astype(jnp.bfloat16)
    mixed_heads = grad_mixed.astype(jnp.float32).reshape(targets, HEADS, head_size)
    grad_attend = jnp.einsum('thd,tkhd->thk', mixed_heads, value_heads)
    grad_values = jnp.einsum('thk,thd->tkhd', attend_low.astype(jnp.float32), mixed_heads)
    grad_scores = attend * (grad_attend - lax.optimization_barrier(jnp.sum(attend * grad_attend, axis=-1, keepdims=True)))
    score_low = (grad_scores * scale).astype(jnp.bfloat16)
    grad_qproj = jnp.einsum('thk,tkhd->thd', score_low.astype(jnp.float32), key_heads)
    grad_qproj = grad_qproj.reshape(targets, width).astype(jnp.bfloat16)
    grad_keys = jnp.einsum('thk,thd->tkhd', score_low.astype(jnp.float32), query_heads)
    grad_wq = jnp.dot(query_rows.T, grad_qproj, preferred_element_type=jnp.float32)
    grad_query = jnp.dot(grad_qproj, weights[0].T, preferred_element_type=jnp.float32).astype(jnp.bfloat16)
    return (grad_query, grad_keys.reshape(targets * pick_count, width), grad_values.reshape(targets * pick_count, width), grad_wq, grad_wo)

def reference(raw_rows, enc_weight, counts, member_rows, pool, picks, queries, attn_weights, out_grad):
    behavior = jnp.dot(raw_rows, enc_weight, preferred_element_type=jnp.float32).astype(jnp.bfloat16)
    cluster_emb, owner_of = jax.vmap(cluster_means)(behavior.reshape(N_CLU, ROW_DEV, D), counts, member_rows)
    cluster_emb = cluster_emb.reshape(CLUSTERS, D)
    key_table = jnp.dot(cluster_emb, attn_weights[1], preferred_element_type=jnp.float32).astype(jnp.bfloat16)
    value_table = jnp.dot(cluster_emb, attn_weights[2], preferred_element_type=jnp.float32).astype(jnp.bfloat16)

    def step(carry, block):
        key_grad, value_grad, grad_wq, grad_wo = carry
        query_rows, grad_out, pool_row, pick_rows = block
        chosen = pool_row[pick_rows]
        result = backward_block(query_rows, key_table[chosen], value_table[chosen], grad_out, attn_weights)
        flat_ids = chosen.reshape(-1)
        key_grad = key_grad.at[flat_ids].add(result[1])
        value_grad = value_grad.at[flat_ids].add(result[2])
        return ((key_grad, value_grad, grad_wq + result[3], grad_wo + result[4]), result[0])
    start = (jnp.zeros((CLUSTERS, D), jnp.float32), jnp.zeros((CLUSTERS, D), jnp.float32), jnp.zeros((D, D), jnp.float32), jnp.zeros((D, D), jnp.float32))
    blocks = (queries.reshape(N_CLU, TGT_DEV, D), out_grad.reshape(N_CLU, TGT_DEV, D), pool, picks.reshape(N_CLU, TGT_DEV, K))
    carry, grad_blocks = lax.scan(step, start, blocks)
    key_grad, value_grad, grad_wq, grad_wo = carry
    emb_wide = cluster_emb.astype(jnp.float32)
    grad_wk = jnp.dot(emb_wide.T, key_grad, precision=highest)
    grad_wv = jnp.dot(emb_wide.T, value_grad, precision=highest)
    cluster_grad = jnp.dot(key_grad, attn_weights[1].astype(jnp.float32).T, precision=highest) + jnp.dot(value_grad, attn_weights[2].astype(jnp.float32).T, precision=highest)
    grad_rows = jax.vmap(expand_rows)(cluster_grad.reshape(N_CLU, CL_DEV, D), counts, member_rows, owner_of)
    grad_rows = grad_rows.reshape(ROWS, D)
    grad_encoder = jnp.dot(raw_rows.T, grad_rows, preferred_element_type=jnp.float32)
    grad_attn = jnp.stack([grad_wq, grad_wk, grad_wv, grad_wo])
    return (grad_blocks.reshape(TARGETS, D), grad_rows, grad_attn, grad_encoder)
```

```python
import functools

import jax
import jax.numpy as jnp
from jax import lax
from jax.experimental import pallas as pl
from jax.experimental.pallas import tpu as pltpu
from jax.sharding import PartitionSpec as P

HEADS = 4
LANES = 128
F32 = jnp.float32
BF16 = jnp.bfloat16
VMEM_LIMIT = 48 * 1024 * 1024


def dot(a, b):
    return jnp.dot(a, b, preferred_element_type=F32)


def dot_nt(a, b):
    return lax.dot_general(a, b, (((1,), (1,)), ((), ())), preferred_element_type=F32)


def dot_tn(a, b):
    return lax.dot_general(a, b, (((0,), (0,)), ((), ())), preferred_element_type=F32)


def iota(shape, dim):
    return lax.broadcasted_iota(jnp.int32, shape, dim)


def ones_where(cond):
    return jnp.where(cond, 1.0, 0.0).astype(BF16)


def column_of(row):
    n = row.shape[1]
    wide = jnp.where(iota((n, n), 0) == iota((n, n), 1), row, 0.0)
    return jnp.sum(wide, axis=1, keepdims=True)


def member_onehot(table_ref, at, clusters):
    sub = iota((clusters, LANES), 0).astype(F32)
    parts = [ones_where(table_ref[pl.ds(at + k, 1), :] == sub) for k in range(2)]
    return jnp.concatenate(parts, axis=1)


def means_kernel(counts_s, counts_v, members, raw, mean_out, table, acc):
    step = pl.program_id(0)
    clusters = counts_v.shape[1]
    groups = members.shape[0]

    @pl.when(step == 0)
    def _():
        place = iota((groups, LANES), 0) * LANES + iota((groups, LANES), 1)

        def body(j, carry):
            end, cluster = carry
            end = end + counts_s[0, j]
            return end, cluster + jnp.where(place >= end, 1, 0)

        _, cluster = lax.fori_loop(
            0, clusters, body, (jnp.int32(0), jnp.zeros((groups, LANES), jnp.int32)), unroll=8
        )
        cluster = cluster.astype(F32)
        rows = members[...]
        high = rows // LANES
        low = rows % LANES
        total = jnp.zeros((groups, LANES), F32)
        high_iota = iota((groups, LANES), 0)
        low_iota = iota((LANES, LANES), 0)
        for k in range(0, groups, 2):
            a_parts, b_parts = [], []
            for m in (k, k + 1):
                a_parts.append(
                    jnp.where(high[m : m + 1] == high_iota, cluster[m : m + 1], 0.0).astype(BF16)
                )
                b_parts.append(ones_where(low[m : m + 1] == low_iota))
            total = total + dot_nt(
                jnp.concatenate(a_parts, axis=1), jnp.concatenate(b_parts, axis=1)
            )
        table[...] = total
        acc[...] = jnp.zeros_like(acc)

    blocks = raw.shape[0] // 256
    total = acc[...]
    for k in range(blocks):
        onehot = member_onehot(table, (step * blocks + k) * 2, clusters)
        total = total + dot(onehot, raw[k * 256 : k * 256 + 256, :])
    acc[...] = total

    @pl.when(step == pl.num_programs(0) - 1)
    def _():
        mean_out[...] = (acc[...] / column_of(counts_v[...].astype(F32))).astype(BF16)


def cluster_means(counts, members, raw_rows):
    clusters = counts.shape[1]
    rows, width = raw_rows.shape
    groups = rows // LANES
    block = 1024
    return pl.pallas_call(
        means_kernel,
        grid=(rows // block,),
        in_specs=[
            pl.BlockSpec(memory_space=pltpu.SMEM),
            pl.BlockSpec((1, clusters), lambda i: (0, 0)),
            pl.BlockSpec((groups, LANES), lambda i: (0, 0)),
            pl.BlockSpec((block, width), lambda i: (i, 0)),
        ],
        out_specs=[
            pl.BlockSpec((clusters, width), lambda i: (0, 0)),
            pl.BlockSpec((groups, LANES), lambda i: (0, 0)),
        ],
        out_shape=[
            jax.ShapeDtypeStruct((clusters, width), BF16),
            jax.ShapeDtypeStruct((groups, LANES), F32),
        ],
        scratch_shapes=[pltpu.VMEM((clusters, width), F32)],
        compiler_params=pltpu.CompilerParams(vmem_limit_bytes=VMEM_LIMIT),
        cost_estimate=pl.CostEstimate(
            flops=2 * rows * clusters * width, bytes_accessed=2 * rows * width, transcendentals=0
        ),
    )(counts, counts, members.reshape(groups, LANES), raw_rows)


def spread_heads(rows):
    head = iota(rows.shape, 1) // (rows.shape[1] // HEADS)
    return jnp.concatenate([jnp.where(head == h, rows, 0.0) for h in range(HEADS)], axis=0).astype(
        BF16
    )


def targets_kernel(scale, picks, queries, out_grad, weights, bias, query_heads, mixed_heads):
    query_proj = dot(queries[...], weights[0]).astype(BF16)
    query_heads[...] = spread_heads(query_proj.astype(F32) * scale)
    grad_mixed = dot_nt(out_grad[...], weights[3]).astype(BF16)
    mixed_heads[...] = spread_heads(grad_mixed.astype(F32))
    count, targets = picks.shape
    block = 128

    def body(b, carry):
        at = pl.multiple_of(b * block, block)
        slot = iota((block, targets), 0) + at
        found = jnp.zeros((block, targets), F32)
        for i in range(count):
            found = jnp.where(picks[i : i + 1, :] == slot, 1.0, found)
        bias[pl.ds(at, block), :] = jnp.where(found > 0.5, 0.0, -1e30)
        return carry

    lax.fori_loop(0, bias.shape[0] // block, body, 0)


def target_terms(scale, picks_t, queries, out_grad, weights, pooled):
    targets, width = queries.shape
    return pl.pallas_call(
        functools.partial(targets_kernel, scale),
        out_shape=[
            jax.ShapeDtypeStruct((pooled, targets), F32),
            jax.ShapeDtypeStruct((HEADS * targets, width), BF16),
            jax.ShapeDtypeStruct((HEADS * targets, width), BF16),
        ],
        compiler_params=pltpu.CompilerParams(vmem_limit_bytes=VMEM_LIMIT),
        cost_estimate=pl.CostEstimate(
            flops=4 * targets * pooled * picks_t.shape[0],
            bytes_accessed=4 * pooled * targets,
            transcendentals=0,
        ),
    )(picks_t, queries, out_grad, weights)


def attention_kernel(
    scale, owners, raw, enc, weights, queries, out_grad, bias, query_heads, mixed_heads, send, grad_query, grads
):
    pooled, width = raw.shape
    targets = queries.shape[0]
    raw_pool = raw[...]
    emb = dot(raw_pool, enc[...]).astype(BF16)
    key = dot(emb, weights[1]).astype(BF16)
    value = dot(emb, weights[2]).astype(BF16)
    key_t = dot_nt(weights[1].T, emb).astype(BF16)
    value_t = dot_nt(weights[2].T, emb).astype(BF16)
    pair_bias = jnp.concatenate([bias[...], bias[...]], axis=1)
    head_of_row = iota((width, targets), 0) // (width // HEADS)
    key_grad = jnp.zeros((pooled, width), F32)
    value_grad = jnp.zeros((pooled, width), F32)
    mixed_t = jnp.zeros((width, targets), F32)
    qproj_t = jnp.zeros((width, targets), F32)
    for pair in range(HEADS // 2):
        rows = slice(pair * 2 * targets, (pair + 1) * 2 * targets)
        query_pair = query_heads[rows, :]
        mixed_pair = mixed_heads[rows, :]
        scores = dot_nt(key, query_pair) + pair_bias
        raised = jnp.exp(scores - jnp.max(scores, axis=0, keepdims=True))
        attend = raised * (1.0 / jnp.sum(raised, axis=0, keepdims=True))
        attend_low = attend.astype(BF16)
        weighted = attend * dot_nt(value, mixed_pair)
        score_low = (weighted - attend * jnp.sum(weighted, axis=0, keepdims=True)).astype(BF16)
        value_grad = value_grad + dot(attend_low, mixed_pair)
        key_grad = key_grad + dot(score_low, query_pair)
        mixed_both = dot(value_t, attend_low)
        qproj_both = dot(key_t, score_low)
        for k in range(2):
            own = head_of_row == pair * 2 + k
            cols = slice(k * targets, (k + 1) * targets)
            mixed_t = jnp.where(own, mixed_both[:, cols], mixed_t)
            qproj_t = jnp.where(own, qproj_both[:, cols], qproj_t)
    grad_qproj = (qproj_t * scale).T.astype(BF16)
    grad_query[...] = dot_nt(grad_qproj, weights[0]).astype(BF16)
    key_low = key_grad.astype(BF16)
    value_low = value_grad.astype(BF16)
    emb_grad = (dot_nt(key_low, weights[1]) + dot_nt(value_low, weights[2])).astype(BF16)
    grads[0:width, :] = dot_tn(queries[...], grad_qproj)
    grads[width : 2 * width, :] = dot_tn(emb, key_low)
    grads[2 * width : 3 * width, :] = dot_tn(emb, value_low)
    grads[3 * width : 4 * width, :] = dot(mixed_t.astype(BF16), out_grad[...])
    grads[4 * width : 5 * width, :] = dot_tn(raw_pool, emb_grad)
    if grads.shape[0] > 5 * width:
        grads[5 * width :, :] = jnp.zeros((grads.shape[0] - 5 * width, width), F32)
    per_owner = pooled // owners
    chunk = grads.shape[0] // owners
    for o in range(owners):
        send[o, 0:per_owner, :] = emb_grad[o * per_owner : (o + 1) * per_owner, :]
        send[o, per_owner:, :] = grads[o * chunk : (o + 1) * chunk, :].astype(BF16)


def attention(scale, owners, chunk, raw_pool, enc, weights, queries, out_grad, bias, query_heads, mixed_heads):
    pooled, width = raw_pool.shape
    return pl.pallas_call(
        functools.partial(attention_kernel, scale, owners),
        out_shape=[
            jax.ShapeDtypeStruct((owners, pooled // owners + chunk, width), BF16),
            jax.ShapeDtypeStruct(queries.shape, BF16),
        ],
        scratch_shapes=[pltpu.VMEM((owners * chunk, width), F32)],
        compiler_params=pltpu.CompilerParams(vmem_limit_bytes=VMEM_LIMIT),
    )(raw_pool, enc, weights, queries, out_grad, bias, query_heads, mixed_heads)


def rows_kernel(counts, ids, table, back, out, share):
    step = pl.program_id(0)
    clusters = counts.shape[1]
    owners, _, width = back.shape
    per_owner = ids.shape[1] // owners

    @pl.when(step == 0)
    def _():
        total = jnp.zeros((clusters, width), F32)
        many = 256 // per_owner
        for o in range(0, owners, many):
            at = o * per_owner
            onehot = ones_where(ids[:, at : at + 256] == iota((clusters, 256), 0))
            terms = jnp.concatenate([back[o + k, 0:per_owner, :] for k in range(many)], axis=0)
            total = total + dot(onehot, terms)
        share[...] = (total / column_of(counts[...].astype(F32))).astype(BF16)

    blocks = out.shape[0] // 256
    for k in range(blocks):
        onehot = member_onehot(table, (step * blocks + k) * 2, clusters)
        out[k * 256 : k * 256 + 256, :] = dot_tn(onehot, share[...]).astype(BF16)


def member_grads(counts, ids, table, back, rows):
    clusters = counts.shape[1]
    width = back.shape[2]
    block = 1024
    return pl.pallas_call(
        rows_kernel,
        grid=(rows // block,),
        in_specs=[
            pl.BlockSpec((1, clusters), lambda i: (0, 0)),
            pl.BlockSpec(ids.shape, lambda i: (0, 0)),
            pl.BlockSpec(table.shape, lambda i: (0, 0)),
            pl.BlockSpec(back.shape, lambda i: (0, 0, 0)),
        ],
        out_specs=pl.BlockSpec((block, width), lambda i: (i, 0)),
        out_shape=jax.ShapeDtypeStruct((rows, width), BF16),
        scratch_shapes=[pltpu.VMEM((clusters, width), BF16)],
        compiler_params=pltpu.CompilerParams(vmem_limit_bytes=VMEM_LIMIT),
        cost_estimate=pl.CostEstimate(
            flops=2 * rows * clusters * width, bytes_accessed=2 * rows * width, transcendentals=0
        ),
    )(counts, ids, table, back)


def swap(blocks):
    return lax.all_to_all(blocks, "clu", split_axis=0, concat_axis=0, tiled=True)


def local(raw_rows, enc_weight, counts, member_rows, pool, picks, queries, attn_weights, out_grad):
    clusters = counts.shape[1]
    rows, width = raw_rows.shape
    owners = lax.axis_size("clu")
    pooled = pool.shape[1]
    per_owner = pooled // owners
    scale = (width // HEADS) ** -0.5
    chunk = -(-5 * width // (owners * 16)) * 16

    wanted = swap(pool.reshape(owners, per_owner))
    ids = (wanted % clusters).reshape(1, pooled)
    means, table = cluster_means(counts, member_rows, raw_rows)
    asked = (ids[0][:, None] == jnp.arange(clusters, dtype=jnp.int32)[None, :]).astype(BF16)
    sent = jnp.dot(asked, means, preferred_element_type=F32).astype(BF16)
    raw_pool = swap(sent.reshape(owners, per_owner, width)).reshape(pooled, width)
    bias, query_heads, mixed_heads = target_terms(
        scale, picks.T, queries, out_grad, attn_weights, pooled
    )
    send, grad_query = attention(
        scale, owners, chunk, raw_pool, enc_weight, attn_weights, queries, out_grad, bias, query_heads, mixed_heads
    )
    back = swap(send)
    summed = jnp.sum(back[:, per_owner:, :].astype(F32), axis=0).astype(BF16)
    grads = swap(jnp.broadcast_to(summed[None], (owners, chunk, width)))
    grads = grads.reshape(owners * chunk, width)[: 5 * width].astype(F32)
    grad_rows = member_grads(counts, ids, table, back, rows)
    grad_attn = grads[: 4 * width].reshape(4, width, width)
    return grad_query, grad_rows, grad_attn, grads[4 * width :]


def solution(mesh):
    split = P(("grp", "clu"), None)
    in_specs = (split, P(), split, split, split, split, split, P(), split)
    out_specs = (split, split, P("grp", None, None), P("grp", None))
    return jax.shard_map(local, mesh=mesh, in_specs=in_specs, out_specs=out_specs, check_vma=False)
```

```python
import functools

import jax
import jax.numpy as jnp
from jax import lax
from jax.experimental import pallas as pl
from jax.experimental.pallas import tpu as pltpu
from jax.sharding import PartitionSpec as P

HEADS = 4
MATRICES = 5
LANES = 128
F32 = jnp.float32
BF16 = jnp.bfloat16
VMEM_LIMIT = 48 * 1024 * 1024


def dot(a, b):
    return jnp.dot(a, b, preferred_element_type=F32)


def dot_nt(a, b):
    return lax.dot_general(a, b, (((1,), (1,)), ((), ())), preferred_element_type=F32)


def dot_tn(a, b):
    return lax.dot_general(a, b, (((0,), (0,)), ((), ())), preferred_element_type=F32)


def iota(shape, dim):
    return lax.broadcasted_iota(jnp.int32, shape, dim)


def ones_where(cond):
    return jnp.where(cond, 1.0, 0.0).astype(BF16)


def column_of(row):
    n = row.shape[1]
    wide = jnp.where(iota((n, n), 0) == iota((n, n), 1), row, 0.0)
    return jnp.sum(wide, axis=1, keepdims=True)


def member_onehot(table_ref, at, clusters):
    sub = iota((clusters, LANES), 0).astype(F32)
    parts = [ones_where(table_ref[pl.ds(at + k, 1), :] == sub) for k in range(2)]
    return jnp.concatenate(parts, axis=1)


def means_kernel(
    counts_h, members_h, raw_h, mean_out, table, counts_s, counts_v, members, raw, small_sem, raw_sem
):
    clusters = counts_v.shape[1]
    groups = members.shape[0]
    parts = raw_sem.shape[0]
    part = raw.shape[0] // parts
    small = [
        pltpu.make_async_copy(counts_h, counts_s, small_sem.at[0]),
        pltpu.make_async_copy(members_h, members, small_sem.at[1]),
        pltpu.make_async_copy(counts_h, counts_v, small_sem.at[2]),
    ]
    large = [
        pltpu.make_async_copy(
            raw_h.at[pl.ds(k * part, part)], raw.at[pl.ds(k * part, part)], raw_sem.at[k]
        )
        for k in range(parts)
    ]
    for copy in small + large:
        copy.start()
    place = iota((groups, LANES), 0) * LANES + iota((groups, LANES), 1)
    small[0].wait()

    def body(j, carry):
        end, cluster = carry
        end = end + counts_s[0, j]
        return end, cluster + jnp.where(place >= end, 1, 0)

    _, cluster = lax.fori_loop(
        0, clusters, body, (jnp.int32(0), jnp.zeros((groups, LANES), jnp.int32)), unroll=8
    )
    cluster = cluster.astype(F32)
    small[1].wait()
    rows = members[...]
    high = rows // LANES
    low = rows % LANES
    total = jnp.zeros((groups, LANES), F32)
    high_iota = iota((groups, LANES), 0)
    low_iota = iota((LANES, LANES), 0)
    for k in range(0, groups, 2):
        a_parts, b_parts = [], []
        for m in (k, k + 1):
            a_parts.append(
                jnp.where(high[m : m + 1] == high_iota, cluster[m : m + 1], 0.0).astype(BF16)
            )
            b_parts.append(ones_where(low[m : m + 1] == low_iota))
        total = total + dot_nt(jnp.concatenate(a_parts, axis=1), jnp.concatenate(b_parts, axis=1))
    table[...] = total
    small[2].wait()
    count_column = column_of(counts_v[...].astype(F32))
    sums = jnp.zeros((clusters, raw.shape[1]), F32)
    for p in range(parts):
        large[p].wait()
        for k in range(part // 256):
            at = p * part + k * 256
            onehot = member_onehot(table, at // LANES, clusters)
            sums = sums + dot(onehot, raw[at : at + 256, :])
    mean_out[...] = (sums / count_column).astype(BF16)


def cluster_means(counts, members, raw_rows):
    clusters = counts.shape[1]
    rows, width = raw_rows.shape
    groups = rows // LANES
    parts = 8
    return pl.pallas_call(
        means_kernel,
        in_specs=[pl.BlockSpec(memory_space=pltpu.HBM)] * 3,
        out_shape=[
            jax.ShapeDtypeStruct((clusters, width), BF16),
            jax.ShapeDtypeStruct((groups, LANES), F32),
        ],
        scratch_shapes=[
            pltpu.SMEM((1, clusters), jnp.int32),
            pltpu.VMEM((1, clusters), jnp.int32),
            pltpu.VMEM((groups, LANES), jnp.int32),
            pltpu.VMEM((rows, width), BF16),
            pltpu.SemaphoreType.DMA((3,)),
            pltpu.SemaphoreType.DMA((parts,)),
        ],
        compiler_params=pltpu.CompilerParams(vmem_limit_bytes=VMEM_LIMIT),
        cost_estimate=pl.CostEstimate(
            flops=2 * rows * clusters * width, bytes_accessed=2 * rows * width, transcendentals=0
        ),
    )(counts, members.reshape(groups, LANES), raw_rows)


def select_kernel(got, means, onehot_t, sent):
    clusters = means.shape[0]
    parity = lax.axis_index("clu") % 2
    half = LANES // 2
    wanted = lax.rem(got[...], clusters)
    turned = pltpu.roll(wanted, half, 1)
    first = jnp.where(parity == 0, wanted, turned)
    second = jnp.where(parity == 0, turned, wanted)
    left = iota((1, LANES), 1) < half
    for k in range(got.shape[0] // 2):
        row = jnp.where(left, first[2 * k : 2 * k + 1], second[2 * k + 1 : 2 * k + 2])
        onehot_t[:, k * LANES : (k + 1) * LANES] = ones_where(row == iota((clusters, LANES), 0))
    sent[...] = dot_tn(onehot_t[...], means[...]).astype(BF16)


def select_rows(got, means, pooled):
    clusters, width = means.shape
    return pl.pallas_call(
        select_kernel,
        out_shape=[
            jax.ShapeDtypeStruct((clusters, pooled), BF16),
            jax.ShapeDtypeStruct((pooled, width), BF16),
        ],
        compiler_params=pltpu.CompilerParams(vmem_limit_bytes=VMEM_LIMIT),
    )(got, means)


def spread_heads(rows):
    head = iota(rows.shape, 1) // (rows.shape[1] // HEADS)
    return jnp.concatenate([jnp.where(head == h, rows, 0.0) for h in range(HEADS)], axis=0).astype(
        BF16
    )


def targets_kernel(scale, picks, queries, out_grad, weights, bias, query_heads, mixed_heads):
    query_proj = dot(queries[...], weights[0]).astype(BF16)
    query_heads[...] = spread_heads(query_proj.astype(F32) * scale)
    grad_mixed = dot_nt(out_grad[...], weights[3]).astype(BF16)
    mixed_heads[...] = spread_heads(grad_mixed.astype(F32))
    count, targets = picks.shape
    block = 128

    def body(b, carry):
        at = pl.multiple_of(b * block, block)
        slot = iota((block, targets), 0) + at
        found = jnp.zeros((block, targets), F32)
        for i in range(count):
            found = jnp.where(picks[i : i + 1, :] == slot, 1.0, found)
        bias[pl.ds(at, block), :] = jnp.where(found > 0.5, 0.0, -1e30)
        return carry

    lax.fori_loop(0, bias.shape[0] // block, body, 0)


def target_terms(scale, picks_t, queries, out_grad, weights, pooled):
    targets, width = queries.shape
    return pl.pallas_call(
        functools.partial(targets_kernel, scale),
        out_shape=[
            jax.ShapeDtypeStruct((pooled, targets), F32),
            jax.ShapeDtypeStruct((HEADS * targets, width), BF16),
            jax.ShapeDtypeStruct((HEADS * targets, width), BF16),
        ],
        compiler_params=pltpu.CompilerParams(vmem_limit_bytes=VMEM_LIMIT),
        cost_estimate=pl.CostEstimate(
            flops=4 * targets * pooled * picks_t.shape[0],
            bytes_accessed=4 * pooled * targets,
            transcendentals=0,
        ),
    )(picks_t, queries, out_grad, weights)


def attention_kernel(
    scale, owners, raw, enc, weights, queries, out_grad, bias, query_heads, mixed_heads, back, grad_query, keep, send, grads
):
    pooled, width = raw.shape
    targets = queries.shape[0]
    raw_pool = raw[...]
    emb = dot(raw_pool, enc[...]).astype(BF16)
    key = dot(emb, weights[1]).astype(BF16)
    value = dot(emb, weights[2]).astype(BF16)
    key_t = dot_nt(weights[1].T, emb).astype(BF16)
    value_t = dot_nt(weights[2].T, emb).astype(BF16)
    pair_bias = jnp.concatenate([bias[...], bias[...]], axis=1)
    head_of_row = iota((width, targets), 0) // (width // HEADS)
    key_grad = jnp.zeros((pooled, width), F32)
    value_grad = jnp.zeros((pooled, width), F32)
    mixed_t = jnp.zeros((width, targets), F32)
    qproj_t = jnp.zeros((width, targets), F32)
    for pair in range(HEADS // 2):
        rows = slice(pair * 2 * targets, (pair + 1) * 2 * targets)
        query_pair = query_heads[rows, :]
        mixed_pair = mixed_heads[rows, :]
        scores = dot_nt(key, query_pair) + pair_bias
        raised = jnp.exp(scores - jnp.max(scores, axis=0, keepdims=True))
        attend = raised * (1.0 / jnp.sum(raised, axis=0, keepdims=True))
        attend_low = attend.astype(BF16)
        weighted = attend * dot_nt(value, mixed_pair)
        score_low = (weighted - attend * jnp.sum(weighted, axis=0, keepdims=True)).astype(BF16)
        value_grad = value_grad + dot(attend_low, mixed_pair)
        key_grad = key_grad + dot(score_low, query_pair)
        mixed_both = dot(value_t, attend_low)
        qproj_both = dot(key_t, score_low)
        for k in range(2):
            own = head_of_row == pair * 2 + k
            cols = slice(k * targets, (k + 1) * targets)
            mixed_t = jnp.where(own, mixed_both[:, cols], mixed_t)
            qproj_t = jnp.where(own, qproj_both[:, cols], qproj_t)
    grad_qproj = (qproj_t * scale).T.astype(BF16)
    grad_query[...] = dot_nt(grad_qproj, weights[0]).astype(BF16)
    key_low = key_grad.astype(BF16)
    value_low = value_grad.astype(BF16)
    emb_grad = (dot_nt(key_low, weights[1]) + dot_nt(value_low, weights[2])).astype(BF16)
    grads[0:width, :] = dot_tn(queries[...], grad_qproj)
    grads[width : 2 * width, :] = dot_tn(emb, key_low)
    grads[2 * width : 3 * width, :] = dot_tn(emb, value_low)
    grads[3 * width : 4 * width, :] = dot(mixed_t.astype(BF16), out_grad[...])
    grads[4 * width : 5 * width, :] = dot_tn(raw_pool, emb_grad)
    back[...] = emb_grad
    core = lax.axis_index("clu") % 2
    part = width // owners
    deep = owners // 4
    for y in range(2):
        for z in range(deep):
            for m in range(MATRICES):
                at = m * width + (z * 4 + y * 2) * part
                kept = pl.ds(pl.multiple_of(at + core * part, part), part)
                given = pl.ds(pl.multiple_of(at + (1 - core) * part, part), part)
                keep[y * deep + z, m] = grads[kept, :].astype(BF16)
                send[y * deep + z, m] = grads[given, :].astype(BF16)


def attention(scale, owners, raw_pool, enc, weights, queries, out_grad, bias, query_heads, mixed_heads):
    pooled, width = raw_pool.shape
    half = jax.ShapeDtypeStruct((owners // 2, MATRICES, width // owners, width), BF16)
    return pl.pallas_call(
        functools.partial(attention_kernel, scale, owners),
        out_shape=[
            jax.ShapeDtypeStruct((pooled, width), BF16),
            jax.ShapeDtypeStruct(queries.shape, BF16),
            half,
            half,
        ],
        scratch_shapes=[pltpu.VMEM((MATRICES * width, width), F32)],
        compiler_params=pltpu.CompilerParams(vmem_limit_bytes=VMEM_LIMIT),
    )(raw_pool, enc, weights, queries, out_grad, bias, query_heads, mixed_heads)


def add_low(a, b):
    return (a.astype(F32) + b.astype(F32)).astype(BF16)


def split_y_kernel(keep, got, kept, given):
    y = lax.axis_index("clu") // 2 % 2
    deep = kept.shape[0]
    for i in range(deep):
        own = y * deep + i
        other = (1 - y) * deep + i
        kept[i] = add_low(keep[own], got[own])
        given[i] = add_low(keep[other], got[other])


def split_y(keep, got):
    half = jax.ShapeDtypeStruct((keep.shape[0] // 2,) + keep.shape[1:], BF16)
    return pl.pallas_call(split_y_kernel, out_shape=[half, half])(keep, got)


def split_z_kernel(keep, got, *outs):
    z = lax.axis_index("clu") // 4
    deep = keep.shape[0]
    for k in range(deep):
        at = lax.rem(z + k, deep)
        outs[k][...] = add_low(keep[at], got[at])


def split_z(keep, got):
    one = jax.ShapeDtypeStruct(keep.shape[1:], BF16)
    return pl.pallas_call(split_z_kernel, out_shape=[one] * keep.shape[0])(keep, got)


def place_kernel(own, beside, own_core, beside_core, attn, enc):
    me = lax.axis_index("clu")
    deep, matrices, part, _ = own.shape
    for k in range(deep):
        z = lax.rem(me // 4 + deep - k, deep)
        low = me % 4
        for source, flip in ((own, 0), (beside, 2), (own_core, 1), (beside_core, 3)):
            at = pl.multiple_of((z * 4 + (low ^ flip)) * part, part)
            for m in range(matrices - 1):
                attn[m, pl.ds(at, part), :] = source[k, m].astype(F32)
            enc[pl.ds(at, part), :] = source[k, matrices - 1].astype(F32)


def place(own, beside, own_core, beside_core):
    width = own.shape[3]
    return pl.pallas_call(
        place_kernel,
        out_shape=[
            jax.ShapeDtypeStruct((MATRICES - 1, width, width), F32),
            jax.ShapeDtypeStruct((width, width), F32),
        ],
    )(own, beside, own_core, beside_core)


def rows_kernel(counts, onehot_t, table, back, out, share):
    step = pl.program_id(0)
    clusters = counts.shape[1]

    @pl.when(step == 0)
    def _():
        total = dot(onehot_t[...], back[...])
        share[...] = (total / column_of(counts[...].astype(F32))).astype(BF16)

    blocks = out.shape[0] // 256
    for k in range(blocks):
        onehot = member_onehot(table, (step * blocks + k) * 2, clusters)
        out[k * 256 : k * 256 + 256, :] = dot_tn(onehot, share[...]).astype(BF16)


def member_grads(counts, onehot_t, table, back, rows):
    clusters = counts.shape[1]
    width = back.shape[1]
    block = 1024
    return pl.pallas_call(
        rows_kernel,
        grid=(rows // block,),
        in_specs=[
            pl.BlockSpec((1, clusters), lambda i: (0, 0)),
            pl.BlockSpec(onehot_t.shape, lambda i: (0, 0)),
            pl.BlockSpec(table.shape, lambda i: (0, 0)),
            pl.BlockSpec(back.shape, lambda i: (0, 0)),
        ],
        out_specs=pl.BlockSpec((block, width), lambda i: (i, 0)),
        out_shape=jax.ShapeDtypeStruct((rows, width), BF16),
        scratch_shapes=[pltpu.VMEM((clusters, width), BF16)],
        compiler_params=pltpu.CompilerParams(vmem_limit_bytes=VMEM_LIMIT),
        cost_estimate=pl.CostEstimate(
            flops=2 * rows * clusters * width, bytes_accessed=2 * rows * width, transcendentals=0
        ),
    )(counts, onehot_t, table, back)


def swap(blocks):
    return lax.all_to_all(blocks, "clu", split_axis=0, concat_axis=0, tiled=True)


def local(raw_rows, enc_weight, counts, member_rows, pool, picks, queries, attn_weights, out_grad):
    rows, width = raw_rows.shape
    owners = lax.axis_size("clu")
    deep = owners // 4
    pooled = pool.shape[1]
    scale = (width // HEADS) ** -0.5

    def permute(block, target):
        return lax.ppermute(block, "clu", [(d, target(d)) for d in range(owners)])

    def along_z(k):
        return lambda d: (d // 4 + k) % deep * 4 + d % 4

    def flip(bit):
        return lambda d: d ^ bit

    pairs = pool.reshape(owners // 2, 1, 1, LANES)
    asking = jnp.broadcast_to(pairs, (owners // 2, 2, 1, LANES)).reshape(owners, 1, LANES)
    got = swap(asking).reshape(owners, LANES)
    means, table = cluster_means(counts, member_rows, raw_rows)
    onehot_t, sent = select_rows(got, means, pooled)
    raw_pool = swap(sent.reshape(owners, pooled // owners, width)).reshape(pooled, width)
    bias, query_heads, mixed_heads = target_terms(
        scale, picks.T, queries, out_grad, attn_weights, pooled
    )
    back, grad_query, keep, given = attention(
        scale, owners, raw_pool, enc_weight, attn_weights, queries, out_grad, bias, query_heads, mixed_heads
    )
    keep, given = split_y(keep, permute(given, flip(1)))
    back = swap(back.reshape(owners, pooled // owners, width)).reshape(pooled, width)
    terms = split_z(keep, permute(given, flip(2)))
    total = terms[0].astype(F32)
    for k in range(1, deep):
        total = total + permute(terms[k], along_z(k)).astype(F32)
    total = total.astype(BF16)
    own = jnp.stack([total] + [permute(total, along_z(k)) for k in range(1, deep)])
    beside = permute(own, flip(2))
    grad_attn, grad_encoder = place(own, beside, permute(own, flip(1)), permute(beside, flip(1)))
    grad_rows = member_grads(counts, onehot_t, table, back, rows)
    return grad_query, grad_rows, grad_attn, grad_encoder


def solution(mesh):
    split = P(("grp", "clu"), None)
    in_specs = (split, P(), split, split, split, split, split, P(), split)
    out_specs = (split, split, P("grp", None, None), P("grp", None))
    return jax.shard_map(local, mesh=mesh, in_specs=in_specs, out_specs=out_specs, check_vma=False)
```

```python
import functools

import jax
import jax.numpy as jnp
from jax import lax
from jax.experimental import pallas as pl
from jax.experimental.pallas import tpu as pltpu
from jax.sharding import PartitionSpec as P

HEADS = 4
MATRICES = 5
LANES = 128
F32 = jnp.float32
BF16 = jnp.bfloat16
VMEM_LIMIT = 32 * 1024 * 1024
SMALL = pltpu.CompilerParams(vmem_limit_bytes=8 * 1024 * 1024)


def dot(a, b):
    return jnp.dot(a, b, preferred_element_type=F32)


def dot_nt(a, b):
    return lax.dot_general(a, b, (((1,), (1,)), ((), ())), preferred_element_type=F32)


def dot_tn(a, b):
    return lax.dot_general(a, b, (((0,), (0,)), ((), ())), preferred_element_type=F32)


def iota(shape, dim):
    return lax.broadcasted_iota(jnp.int32, shape, dim)


def ones_where(cond):
    return jnp.where(cond, 1.0, 0.0).astype(BF16)


def column_of(row):
    n = row.shape[1]
    wide = jnp.where(iota((n, n), 0) == iota((n, n), 1), row, 0.0)
    return jnp.sum(wide, axis=1, keepdims=True)


def member_onehot(table_ref, at, clusters):
    sub = iota((clusters, LANES), 0).astype(F32)
    parts = [ones_where(table_ref[pl.ds(at + k, 1), :] == sub) for k in range(2)]
    return jnp.concatenate(parts, axis=1)


def means_kernel(
    counts_h, members_h, raw_h, mean_out, table, counts_s, counts_v, members, raw, small_sem, raw_sem
):
    clusters = counts_v.shape[1]
    groups = members.shape[0]
    parts = raw_sem.shape[0]
    part = raw.shape[0] // parts
    small = [
        pltpu.make_async_copy(counts_h, counts_s, small_sem.at[0]),
        pltpu.make_async_copy(members_h, members, small_sem.at[1]),
        pltpu.make_async_copy(counts_h, counts_v, small_sem.at[2]),
    ]
    large = [
        pltpu.make_async_copy(
            raw_h.at[pl.ds(k * part, part)], raw.at[pl.ds(k * part, part)], raw_sem.at[k]
        )
        for k in range(parts)
    ]
    for copy in small + large:
        copy.start()
    place = iota((groups, LANES), 0) * LANES + iota((groups, LANES), 1)
    small[0].wait()

    def body(j, carry):
        end, cluster = carry
        end = end + counts_s[0, j]
        return end, cluster + jnp.where(place >= end, 1, 0)

    _, cluster = lax.fori_loop(
        0, clusters, body, (jnp.int32(0), jnp.zeros((groups, LANES), jnp.int32)), unroll=8
    )
    cluster = cluster.astype(F32)
    small[1].wait()
    rows = members[...]
    high = rows // LANES
    low = rows % LANES
    total = jnp.zeros((groups, LANES), F32)
    high_iota = iota((groups, LANES), 0)
    low_iota = iota((LANES, LANES), 0)
    for k in range(0, groups, 2):
        a_parts, b_parts = [], []
        for m in (k, k + 1):
            a_parts.append(
                jnp.where(high[m : m + 1] == high_iota, cluster[m : m + 1], 0.0).astype(BF16)
            )
            b_parts.append(ones_where(low[m : m + 1] == low_iota))
        total = total + dot_nt(jnp.concatenate(a_parts, axis=1), jnp.concatenate(b_parts, axis=1))
    table[...] = total
    small[2].wait()
    count_column = column_of(counts_v[...].astype(F32))
    sums = jnp.zeros((clusters, raw.shape[1]), F32)
    for p in range(parts):
        large[p].wait()
        for k in range(part // 256):
            at = p * part + k * 256
            onehot = member_onehot(table, at // LANES, clusters)
            sums = sums + dot(onehot, raw[at : at + 256, :])
    mean_out[...] = (sums / count_column).astype(BF16)


def cluster_means(counts, members, raw_rows):
    clusters = counts.shape[1]
    rows, width = raw_rows.shape
    groups = rows // LANES
    parts = 8
    return pl.pallas_call(
        means_kernel,
        in_specs=[pl.BlockSpec(memory_space=pltpu.HBM)] * 3,
        out_shape=[
            jax.ShapeDtypeStruct((clusters, width), BF16),
            jax.ShapeDtypeStruct((groups, LANES), F32),
        ],
        scratch_shapes=[
            pltpu.SMEM((1, clusters), jnp.int32),
            pltpu.VMEM((1, clusters), jnp.int32),
            pltpu.VMEM((groups, LANES), jnp.int32),
            pltpu.VMEM((rows, width), BF16),
            pltpu.SemaphoreType.DMA((3,)),
            pltpu.SemaphoreType.DMA((parts,)),
        ],
        compiler_params=pltpu.CompilerParams(vmem_limit_bytes=51 * 1024 * 1024),
        cost_estimate=pl.CostEstimate(
            flops=2 * rows * clusters * width, bytes_accessed=2 * rows * width, transcendentals=0
        ),
    )(counts, members.reshape(groups, LANES), raw_rows)


def select_kernel(got, means, onehot_t, sent):
    clusters = means.shape[0]
    parity = lax.axis_index("clu") % 2
    half = LANES // 2
    wanted = lax.rem(got[...], clusters)
    turned = pltpu.roll(wanted, half, 1)
    first = jnp.where(parity == 0, wanted, turned)
    second = jnp.where(parity == 0, turned, wanted)
    left = iota((1, LANES), 1) < half
    for k in range(got.shape[0] // 2):
        row = jnp.where(left, first[2 * k : 2 * k + 1], second[2 * k + 1 : 2 * k + 2])
        onehot_t[:, k * LANES : (k + 1) * LANES] = ones_where(row == iota((clusters, LANES), 0))
    sent[...] = dot_tn(onehot_t[...], means[...]).astype(BF16)


def select_rows(got, means, pooled):
    clusters, width = means.shape
    return pl.pallas_call(
        select_kernel,
        out_shape=[
            jax.ShapeDtypeStruct((clusters, pooled), BF16),
            jax.ShapeDtypeStruct((pooled, width), BF16),
        ],
        compiler_params=pltpu.CompilerParams(vmem_limit_bytes=VMEM_LIMIT),
    )(got, means)


def spread_heads(rows):
    head = iota(rows.shape, 1) // (rows.shape[1] // HEADS)
    return jnp.concatenate([jnp.where(head == h, rows, 0.0) for h in range(HEADS)], axis=0).astype(
        BF16
    )


def targets_kernel(scale, picks, queries, out_grad, weights, bias, query_heads, mixed_heads):
    query_proj = dot(queries[...], weights[0]).astype(BF16)
    query_heads[...] = spread_heads(query_proj.astype(F32) * scale)
    grad_mixed = dot_nt(out_grad[...], weights[3]).astype(BF16)
    mixed_heads[...] = spread_heads(grad_mixed.astype(F32))
    count, targets = picks.shape
    block = 128

    def body(b, carry):
        at = pl.multiple_of(b * block, block)
        slot = iota((block, targets), 0) + at
        found = jnp.zeros((block, targets), F32)
        for i in range(count):
            found = jnp.where(picks[i : i + 1, :] == slot, 1.0, found)
        bias[pl.ds(at, block), :] = jnp.where(found > 0.5, 0.0, -1e30)
        return carry

    lax.fori_loop(0, bias.shape[0] // block, body, 0)


def target_terms(scale, picks_t, queries, out_grad, weights, pooled):
    targets, width = queries.shape
    return pl.pallas_call(
        functools.partial(targets_kernel, scale),
        out_shape=[
            jax.ShapeDtypeStruct((pooled, targets), F32),
            jax.ShapeDtypeStruct((HEADS * targets, width), BF16),
            jax.ShapeDtypeStruct((HEADS * targets, width), BF16),
        ],
        compiler_params=pltpu.CompilerParams(vmem_limit_bytes=VMEM_LIMIT),
        cost_estimate=pl.CostEstimate(
            flops=4 * targets * pooled * picks_t.shape[0],
            bytes_accessed=4 * pooled * targets,
            transcendentals=0,
        ),
    )(picks_t, queries, out_grad, weights)


def attention_kernel(
    scale, owners, raw, enc, weights, queries, out_grad, bias, query_heads, mixed_heads, back, grad_query, keep, send, grads
):
    pooled, width = raw.shape
    targets = queries.shape[0]
    raw_pool = raw[...]
    emb = dot(raw_pool, enc[...]).astype(BF16)
    key = dot(emb, weights[1]).astype(BF16)
    value = dot(emb, weights[2]).astype(BF16)
    key_t = dot_nt(weights[1].T, emb).astype(BF16)
    value_t = dot_nt(weights[2].T, emb).astype(BF16)
    pair_bias = jnp.concatenate([bias[...], bias[...]], axis=1)
    head_of_row = iota((width, targets), 0) // (width // HEADS)
    key_grad = jnp.zeros((pooled, width), F32)
    value_grad = jnp.zeros((pooled, width), F32)
    mixed_t = jnp.zeros((width, targets), F32)
    qproj_t = jnp.zeros((width, targets), F32)
    for pair in range(HEADS // 2):
        rows = slice(pair * 2 * targets, (pair + 1) * 2 * targets)
        query_pair = query_heads[rows, :]
        mixed_pair = mixed_heads[rows, :]
        scores = dot_nt(key, query_pair) + pair_bias
        raised = jnp.exp(scores - jnp.max(scores, axis=0, keepdims=True))
        attend = raised * (1.0 / jnp.sum(raised, axis=0, keepdims=True))
        attend_low = attend.astype(BF16)
        weighted = attend * dot_nt(value, mixed_pair)
        score_low = (weighted - attend * jnp.sum(weighted, axis=0, keepdims=True)).astype(BF16)
        value_grad = value_grad + dot(attend_low, mixed_pair)
        key_grad = key_grad + dot(score_low, query_pair)
        mixed_both = dot(value_t, attend_low)
        qproj_both = dot(key_t, score_low)
        for k in range(2):
            own = head_of_row == pair * 2 + k
            cols = slice(k * targets, (k + 1) * targets)
            mixed_t = jnp.where(own, mixed_both[:, cols], mixed_t)
            qproj_t = jnp.where(own, qproj_both[:, cols], qproj_t)
    grad_qproj = (qproj_t * scale).T.astype(BF16)
    grad_query[...] = dot_nt(grad_qproj, weights[0]).astype(BF16)
    key_low = key_grad.astype(BF16)
    value_low = value_grad.astype(BF16)
    emb_grad = (dot_nt(key_low, weights[1]) + dot_nt(value_low, weights[2])).astype(BF16)
    grads[0:width, :] = dot_tn(queries[...], grad_qproj)
    grads[width : 2 * width, :] = dot_tn(emb, key_low)
    grads[2 * width : 3 * width, :] = dot_tn(emb, value_low)
    grads[3 * width : 4 * width, :] = dot(mixed_t.astype(BF16), out_grad[...])
    grads[4 * width : 5 * width, :] = dot_tn(raw_pool, emb_grad)
    back[...] = emb_grad
    core = lax.axis_index("clu") % 2
    part = width // owners
    deep = owners // 4
    for y in range(2):
        for z in range(deep):
            for m in range(MATRICES):
                at = m * width + (z * 4 + y * 2) * part
                kept = pl.ds(pl.multiple_of(at + core * part, part), part)
                given = pl.ds(pl.multiple_of(at + (1 - core) * part, part), part)
                keep[y * deep + z, m] = grads[kept, :].astype(BF16)
                send[y * deep + z, m] = grads[given, :].astype(BF16)


def attention(scale, owners, raw_pool, enc, weights, queries, out_grad, bias, query_heads, mixed_heads):
    pooled, width = raw_pool.shape
    half = jax.ShapeDtypeStruct((owners // 2, MATRICES, width // owners, width), BF16)
    return pl.pallas_call(
        functools.partial(attention_kernel, scale, owners),
        out_shape=[
            jax.ShapeDtypeStruct((pooled, width), BF16),
            jax.ShapeDtypeStruct(queries.shape, BF16),
            half,
            half,
        ],
        scratch_shapes=[pltpu.VMEM((MATRICES * width, width), F32)],
        compiler_params=pltpu.CompilerParams(vmem_limit_bytes=VMEM_LIMIT),
    )(raw_pool, enc, weights, queries, out_grad, bias, query_heads, mixed_heads)


def add_low(a, b):
    return (a.astype(F32) + b.astype(F32)).astype(BF16)


def split_y_kernel(keep, got, kept, given):
    y = lax.axis_index("clu") // 2 % 2
    deep = kept.shape[0]
    for i in range(deep):
        own = y * deep + i
        other = (1 - y) * deep + i
        kept[i] = add_low(keep[own], got[own])
        given[i] = add_low(keep[other], got[other])


def split_y(keep, got):
    half = jax.ShapeDtypeStruct((keep.shape[0] // 2,) + keep.shape[1:], BF16)
    return pl.pallas_call(split_y_kernel, out_shape=[half, half], compiler_params=SMALL)(keep, got)


def split_z_kernel(keep, got, *outs):
    z = lax.axis_index("clu") // 4
    deep = keep.shape[0]
    for k in range(deep):
        at = lax.rem(z + k, deep)
        outs[k][...] = add_low(keep[at], got[at])


def split_z(keep, got):
    one = jax.ShapeDtypeStruct(keep.shape[1:], BF16)
    return pl.pallas_call(
        split_z_kernel, out_shape=[one] * keep.shape[0], compiler_params=SMALL
    )(keep, got)


def place_kernel(own, beside, own_core, beside_core, attn, enc):
    me = lax.axis_index("clu")
    deep, matrices, part, _ = own.shape
    for k in range(deep):
        z = lax.rem(me // 4 + deep - k, deep)
        low = me % 4
        for source, flip in ((own, 0), (beside, 2), (own_core, 1), (beside_core, 3)):
            at = pl.multiple_of((z * 4 + (low ^ flip)) * part, part)
            for m in range(matrices - 1):
                attn[m, pl.ds(at, part), :] = source[k, m].astype(F32)
            enc[pl.ds(at, part), :] = source[k, matrices - 1].astype(F32)


def place(own, beside, own_core, beside_core):
    width = own.shape[3]
    return pl.pallas_call(
        place_kernel,
        out_shape=[
            jax.ShapeDtypeStruct((MATRICES - 1, width, width), F32),
            jax.ShapeDtypeStruct((width, width), F32),
        ],
        compiler_params=SMALL,
    )(own, beside, own_core, beside_core)


def fill_rows(table, share, out, first):
    clusters = share.shape[0]
    blocks = out.shape[0] // 256
    for k in range(blocks):
        at = (first + pl.program_id(0)) * blocks + k
        onehot = member_onehot(table, at * 2, clusters)
        out[k * 256 : k * 256 + 256, :] = dot_tn(onehot, share[...]).astype(BF16)


def early_rows_kernel(counts, onehot_t, table, back, out, share):
    @pl.when(pl.program_id(0) == 0)
    def _():
        total = dot(onehot_t[...], back[...])
        share[...] = (total / column_of(counts[...].astype(F32))).astype(BF16)

    fill_rows(table, share, out, 0)


def late_rows_kernel(first, table, share, early, out):
    del early
    fill_rows(table, share, out, first)


ROW_BLOCK = 1024


def rows_cost(rows, clusters, width):
    return pl.CostEstimate(
        flops=2 * rows * clusters * width, bytes_accessed=2 * rows * width, transcendentals=0
    )


def early_rows(counts, onehot_t, table, back, rows, steps):
    clusters = counts.shape[1]
    width = back.shape[1]
    return pl.pallas_call(
        early_rows_kernel,
        grid=(steps,),
        in_specs=[
            pl.BlockSpec((1, clusters), lambda i: (0, 0)),
            pl.BlockSpec(onehot_t.shape, lambda i: (0, 0)),
            pl.BlockSpec(table.shape, lambda i: (0, 0)),
            pl.BlockSpec(back.shape, lambda i: (0, 0)),
        ],
        out_specs=[
            pl.BlockSpec((ROW_BLOCK, width), lambda i: (i, 0)),
            pl.BlockSpec((clusters, width), lambda i: (0, 0)),
        ],
        out_shape=[
            jax.ShapeDtypeStruct((rows, width), BF16),
            jax.ShapeDtypeStruct((clusters, width), BF16),
        ],
        compiler_params=pltpu.CompilerParams(vmem_limit_bytes=VMEM_LIMIT),
        cost_estimate=rows_cost(steps * ROW_BLOCK, clusters, width),
    )(counts, onehot_t, table, back)


def late_rows(table, share, early, first):
    rows, width = early.shape
    steps = rows // ROW_BLOCK - first
    return pl.pallas_call(
        functools.partial(late_rows_kernel, first),
        grid=(steps,),
        in_specs=[
            pl.BlockSpec(table.shape, lambda i: (0, 0)),
            pl.BlockSpec(share.shape, lambda i: (0, 0)),
            pl.BlockSpec(memory_space=pl.ANY),
        ],
        out_specs=pl.BlockSpec((ROW_BLOCK, width), lambda i: (first + i, 0)),
        out_shape=jax.ShapeDtypeStruct((rows, width), BF16),
        input_output_aliases={2: 0},
        compiler_params=pltpu.CompilerParams(vmem_limit_bytes=VMEM_LIMIT),
        cost_estimate=rows_cost(steps * ROW_BLOCK, share.shape[0], width),
    )(table, share, early)


def swap(blocks):
    return lax.all_to_all(blocks, "clu", split_axis=0, concat_axis=0, tiled=True)


def local(raw_rows, enc_weight, counts, member_rows, pool, picks, queries, attn_weights, out_grad):
    rows, width = raw_rows.shape
    owners = lax.axis_size("clu")
    deep = owners // 4
    pooled = pool.shape[1]
    scale = (width // HEADS) ** -0.5

    def permute(block, target):
        return lax.ppermute(block, "clu", [(d, target(d)) for d in range(owners)])

    def along_z(k):
        return lambda d: (d // 4 + k) % deep * 4 + d % 4

    def flip(bit):
        return lambda d: d ^ bit

    pairs = pool.reshape(owners // 2, 1, 1, LANES)
    asking = jnp.broadcast_to(pairs, (owners // 2, 2, 1, LANES)).reshape(owners, 1, LANES)
    got = swap(asking).reshape(owners, LANES)
    means, table = cluster_means(counts, member_rows, raw_rows)
    onehot_t, sent = select_rows(got, means, pooled)
    raw_pool = swap(sent.reshape(owners, pooled // owners, width)).reshape(pooled, width)
    bias, query_heads, mixed_heads = target_terms(
        scale, picks.T, queries, out_grad, attn_weights, pooled
    )
    back, grad_query, keep, given = attention(
        scale, owners, raw_pool, enc_weight, attn_weights, queries, out_grad, bias, query_heads, mixed_heads
    )
    keep, given = split_y(keep, permute(given, flip(1)))
    back = swap(back.reshape(owners, pooled // owners, width)).reshape(pooled, width)
    terms = split_z(keep, permute(given, flip(2)))
    total = terms[0].astype(F32)
    for k in range(1, deep):
        total = total + permute(terms[k], along_z(k)).astype(F32)
    total = total.astype(BF16)
    passed = [permute(total, along_z(k)) for k in range(1, deep)]
    steps = rows // ROW_BLOCK // 2
    early, share = early_rows(counts, onehot_t, table, back, rows, steps)
    passed, share = lax.optimization_barrier((passed, share))
    own = jnp.stack([total] + passed)
    beside = permute(own, flip(2))
    own_core = permute(own, flip(1))
    grad_rows = late_rows(table, share, early, steps)
    beside, own_core, grad_rows = lax.optimization_barrier((beside, own_core, grad_rows))
    grad_attn, grad_encoder = place(own, beside, own_core, permute(beside, flip(1)))
    return grad_query, grad_rows, grad_attn, grad_encoder


def solution(mesh):
    split = P(("grp", "clu"), None)
    in_specs = (split, P(), split, split, split, split, split, P(), split)
    out_specs = (split, split, P("grp", None, None), P("grp", None))
    return jax.shard_map(local, mesh=mesh, in_specs=in_specs, out_specs=out_specs, check_vma=False)
```

```python
import functools

import jax
import jax.numpy as jnp
from jax import lax
from jax.experimental import pallas as pl
from jax.experimental.pallas import tpu as pltpu
from jax.sharding import PartitionSpec as P

HEADS = 4
MATRICES = 5
WEIGHT = 10**11
LANES = 128
F32 = jnp.float32
BF16 = jnp.bfloat16
VMEM_LIMIT = 32 * 1024 * 1024
MOST_VMEM = 51 * 1024 * 1024
SMALL = pltpu.CompilerParams(vmem_limit_bytes=8 * 1024 * 1024)


def dot(a, b):
    return jnp.dot(a, b, preferred_element_type=F32)


def dot_nt(a, b):
    return lax.dot_general(a, b, (((1,), (1,)), ((), ())), preferred_element_type=F32)


def dot_tn(a, b):
    return lax.dot_general(a, b, (((0,), (0,)), ((), ())), preferred_element_type=F32)


def iota(shape, dim):
    return lax.broadcasted_iota(jnp.int32, shape, dim)


def ones_where(cond):
    return jnp.where(cond, 1.0, 0.0).astype(BF16)


def column_of(row):
    n = row.shape[1]
    wide = jnp.where(iota((n, n), 0) == iota((n, n), 1), row, 0.0)
    return jnp.sum(wide, axis=1, keepdims=True)


def member_onehot(table_ref, at, clusters):
    sub = iota((clusters, LANES), 0).astype(F32)
    parts = [ones_where(table_ref[pl.ds(at + k, 1), :] == sub) for k in range(2)]
    return jnp.concatenate(parts, axis=1)


def means_kernel(
    counts_h, members_h, raw_h, mean_out, table, counts_s, counts_v, members, raw, small_sem, raw_sem
):
    clusters = counts_v.shape[1]
    groups = members.shape[0]
    parts = raw_sem.shape[0]
    part = raw.shape[0] // parts
    small = [
        pltpu.make_async_copy(counts_h, counts_s, small_sem.at[0]),
        pltpu.make_async_copy(members_h, members, small_sem.at[1]),
        pltpu.make_async_copy(counts_h, counts_v, small_sem.at[2]),
    ]
    large = [
        pltpu.make_async_copy(
            raw_h.at[pl.ds(k * part, part)], raw.at[pl.ds(k * part, part)], raw_sem.at[k]
        )
        for k in range(parts)
    ]
    for copy in small + large:
        copy.start()
    place = iota((groups, LANES), 0) * LANES + iota((groups, LANES), 1)
    small[0].wait()

    def body(j, carry):
        end, cluster = carry
        end = end + counts_s[0, j]
        return end, cluster + jnp.where(place >= end, 1, 0)

    _, cluster = lax.fori_loop(
        0, clusters, body, (jnp.int32(0), jnp.zeros((groups, LANES), jnp.int32)), unroll=8
    )
    cluster = cluster.astype(F32)
    small[1].wait()
    rows = members[...]
    high = rows // LANES
    low = rows % LANES
    total = jnp.zeros((groups, LANES), F32)
    high_iota = iota((groups, LANES), 0)
    low_iota = iota((LANES, LANES), 0)
    for k in range(0, groups, 2):
        a_parts, b_parts = [], []
        for m in (k, k + 1):
            a_parts.append(
                jnp.where(high[m : m + 1] == high_iota, cluster[m : m + 1], 0.0).astype(BF16)
            )
            b_parts.append(ones_where(low[m : m + 1] == low_iota))
        total = total + dot_nt(jnp.concatenate(a_parts, axis=1), jnp.concatenate(b_parts, axis=1))
    table[...] = total
    small[2].wait()
    count_column = column_of(counts_v[...].astype(F32))
    sums = jnp.zeros((clusters, raw.shape[1]), F32)
    for p in range(parts):
        large[p].wait()
        for k in range(part // 256):
            at = p * part + k * 256
            onehot = member_onehot(table, at // LANES, clusters)
            sums = sums + dot(onehot, raw[at : at + 256, :])
    mean_out[...] = (sums / count_column).astype(BF16)


def cluster_means(counts, members, raw_rows):
    clusters = counts.shape[1]
    rows, width = raw_rows.shape
    groups = rows // LANES
    parts = 8
    return pl.pallas_call(
        means_kernel,
        in_specs=[pl.BlockSpec(memory_space=pltpu.HBM)] * 3,
        out_shape=[
            jax.ShapeDtypeStruct((clusters, width), BF16),
            jax.ShapeDtypeStruct((groups, LANES), F32),
        ],
        scratch_shapes=[
            pltpu.SMEM((1, clusters), jnp.int32),
            pltpu.VMEM((1, clusters), jnp.int32),
            pltpu.VMEM((groups, LANES), jnp.int32),
            pltpu.VMEM((rows, width), BF16),
            pltpu.SemaphoreType.DMA((3,)),
            pltpu.SemaphoreType.DMA((parts,)),
        ],
        compiler_params=pltpu.CompilerParams(vmem_limit_bytes=MOST_VMEM),
        cost_estimate=pl.CostEstimate(
            flops=2 * rows * clusters * width, bytes_accessed=2 * rows * width, transcendentals=0
        ),
    )(counts, members.reshape(groups, LANES), raw_rows)


def select_kernel(got, means, onehot_t, sent):
    clusters = means.shape[0]
    parity = lax.axis_index("clu") % 2
    half = LANES // 2
    wanted = lax.rem(got[...], clusters)
    turned = pltpu.roll(wanted, half, 1)
    first = jnp.where(parity == 0, wanted, turned)
    second = jnp.where(parity == 0, turned, wanted)
    left = iota((1, LANES), 1) < half
    for k in range(got.shape[0] // 2):
        row = jnp.where(left, first[2 * k : 2 * k + 1], second[2 * k + 1 : 2 * k + 2])
        onehot_t[:, k * LANES : (k + 1) * LANES] = ones_where(row == iota((clusters, LANES), 0))
    sent[...] = dot_tn(onehot_t[...], means[...]).astype(BF16)


def select_rows(got, means, pooled):
    clusters, width = means.shape
    return pl.pallas_call(
        select_kernel,
        out_shape=[
            jax.ShapeDtypeStruct((clusters, pooled), BF16),
            jax.ShapeDtypeStruct((pooled, width), BF16),
        ],
        compiler_params=pltpu.CompilerParams(vmem_limit_bytes=VMEM_LIMIT),
    )(got, means)


def spread_heads(rows):
    head = iota(rows.shape, 1) // (rows.shape[1] // HEADS)
    return jnp.concatenate([jnp.where(head == h, rows, 0.0) for h in range(HEADS)], axis=0).astype(
        BF16
    )


def targets_kernel(
    scale, picks, queries, out_grad, weights, table, bias, query_heads, mixed_heads, members
):
    query_proj = dot(queries[...], weights[0]).astype(BF16)
    query_heads[...] = spread_heads(query_proj.astype(F32) * scale)
    grad_mixed = dot_nt(out_grad[...], weights[3]).astype(BF16)
    mixed_heads[...] = spread_heads(grad_mixed.astype(F32))
    count, targets = picks.shape
    block = 128

    def body(b, carry):
        at = pl.multiple_of(b * block, block)
        slot = iota((block, targets), 0) + at
        found = jnp.zeros((block, targets), F32)
        for i in range(count):
            found = jnp.where(picks[i : i + 1, :] == slot, 1.0, found)
        bias[pl.ds(at, block), :] = jnp.where(found > 0.5, 0.0, -1e30)
        return carry

    lax.fori_loop(0, bias.shape[0] // block, body, 0)
    clusters = members.shape[1]
    unit = ones_where(iota((clusters, clusters), 0) == iota((clusters, clusters), 1))

    def turn(b, carry):
        onehot = member_onehot(table, b * 2, clusters)
        at = pl.multiple_of(b * 256, 256)
        members[pl.ds(at, 256), :] = dot_tn(onehot, unit).astype(BF16)
        return carry

    lax.fori_loop(0, members.shape[0] // 256, turn, 0, unroll=4)


def target_terms(scale, picks_t, queries, out_grad, weights, table, pooled, clusters):
    targets, width = queries.shape
    rows = table.shape[0] * LANES
    return pl.pallas_call(
        functools.partial(targets_kernel, scale),
        out_shape=[
            jax.ShapeDtypeStruct((pooled, targets), F32),
            jax.ShapeDtypeStruct((HEADS * targets, width), BF16),
            jax.ShapeDtypeStruct((HEADS * targets, width), BF16),
            jax.ShapeDtypeStruct((rows, clusters), BF16),
        ],
        compiler_params=pltpu.CompilerParams(vmem_limit_bytes=MOST_VMEM),
        cost_estimate=pl.CostEstimate(
            flops=4 * targets * pooled * picks_t.shape[0],
            bytes_accessed=4 * pooled * targets,
            transcendentals=0,
        ),
    )(picks_t, queries, out_grad, weights, table)


def mirrored(number, count):
    out, size = 0, 1
    while size < count:
        out = out * 2 + number % 2
        number //= 2
        size *= 2
    return out


def attention_kernel(
    scale, owners, raw, enc, weights, queries, out_grad, bias, query_heads, mixed_heads, back, grad_query, keep, send, grads
):
    pooled, width = raw.shape
    targets = queries.shape[0]
    raw_pool = raw[...]
    emb = dot(raw_pool, enc[...]).astype(BF16)
    key = dot(emb, weights[1]).astype(BF16)
    value = dot(emb, weights[2]).astype(BF16)
    key_t = dot_nt(weights[1].T, emb).astype(BF16)
    value_t = dot_nt(weights[2].T, emb).astype(BF16)
    pair_bias = jnp.concatenate([bias[...], bias[...]], axis=1)
    head_of_row = iota((width, targets), 0) // (width // HEADS)
    key_grad = jnp.zeros((pooled, width), F32)
    value_grad = jnp.zeros((pooled, width), F32)
    mixed_t = jnp.zeros((width, targets), F32)
    qproj_t = jnp.zeros((width, targets), F32)
    for pair in range(HEADS // 2):
        rows = slice(pair * 2 * targets, (pair + 1) * 2 * targets)
        query_pair = query_heads[rows, :]
        mixed_pair = mixed_heads[rows, :]
        scores = dot_nt(key, query_pair) + pair_bias
        raised = jnp.exp(scores - jnp.max(scores, axis=0, keepdims=True))
        attend = raised * (1.0 / jnp.sum(raised, axis=0, keepdims=True))
        attend_low = attend.astype(BF16)
        weighted = attend * dot_nt(value, mixed_pair)
        score_low = (weighted - attend * jnp.sum(weighted, axis=0, keepdims=True)).astype(BF16)
        value_grad = value_grad + dot(attend_low, mixed_pair)
        key_grad = key_grad + dot(score_low, query_pair)
        mixed_both = dot(value_t, attend_low)
        qproj_both = dot(key_t, score_low)
        for k in range(2):
            own = head_of_row == pair * 2 + k
            cols = slice(k * targets, (k + 1) * targets)
            mixed_t = jnp.where(own, mixed_both[:, cols], mixed_t)
            qproj_t = jnp.where(own, qproj_both[:, cols], qproj_t)
    grad_qproj = (qproj_t * scale).T.astype(BF16)
    grad_query[...] = dot_nt(grad_qproj, weights[0]).astype(BF16)
    key_low = key_grad.astype(BF16)
    value_low = value_grad.astype(BF16)
    emb_grad = (dot_nt(key_low, weights[1]) + dot_nt(value_low, weights[2])).astype(BF16)
    grads[0:width, :] = dot_tn(queries[...], grad_qproj)
    grads[width : 2 * width, :] = dot_tn(emb, key_low)
    grads[2 * width : 3 * width, :] = dot_tn(emb, value_low)
    grads[3 * width : 4 * width, :] = dot(mixed_t.astype(BF16), out_grad[...])
    grads[4 * width : 5 * width, :] = dot_tn(raw_pool, emb_grad)
    back[...] = emb_grad
    core = lax.axis_index("clu") % 2
    part = width // owners
    for q in range(owners // 2):
        base = 2 * mirrored(q, owners // 2)
        for m in range(MATRICES):
            at = m * width + base * part
            kept = pl.ds(pl.multiple_of(at + core * part, part), part)
            given = pl.ds(pl.multiple_of(at + (1 - core) * part, part), part)
            keep[q, m] = grads[kept, :].astype(BF16)
            send[q, m] = grads[given, :].astype(BF16)


def attention(scale, owners, raw_pool, enc, weights, queries, out_grad, bias, query_heads, mixed_heads):
    pooled, width = raw_pool.shape
    half = jax.ShapeDtypeStruct((owners // 2, MATRICES, width // owners, width), BF16)
    return pl.pallas_call(
        functools.partial(attention_kernel, scale, owners),
        out_shape=[
            jax.ShapeDtypeStruct((pooled, width), BF16),
            jax.ShapeDtypeStruct(queries.shape, BF16),
            half,
            half,
        ],
        scratch_shapes=[pltpu.VMEM((MATRICES * width, width), F32)],
        compiler_params=pltpu.CompilerParams(vmem_limit_bytes=VMEM_LIMIT),
    )(raw_pool, enc, weights, queries, out_grad, bias, query_heads, mixed_heads)


def add_low(a, b):
    return (a.astype(F32) + b.astype(F32)).astype(BF16)


def split_kernel(bit, keep, got, kept, given):
    side = lax.shift_right_logical(lax.axis_index("clu"), bit) & 1
    half = kept.shape[0]
    for i in range(half):
        own = side * half + i
        other = (1 - side) * half + i
        kept[i] = add_low(keep[own], got[own])
        given[i] = add_low(keep[other], got[other])


def split(bit, keep, got, flops):
    half = jax.ShapeDtypeStruct((keep.shape[0] // 2,) + keep.shape[1:], BF16)
    return pl.pallas_call(
        functools.partial(split_kernel, bit),
        out_shape=[half, half],
        compiler_params=SMALL,
        cost_estimate=pl.CostEstimate(
            flops=flops, bytes_accessed=4 * keep.size, transcendentals=0
        ),
    )(keep, got)


def place_kernel(masks, own, beside, own_core, beside_core, attn, enc):
    me = lax.axis_index("clu")
    _, matrices, part, _ = own.shape
    for k, mask in enumerate(masks):
        for source, flip in ((own, 0), (beside, 2), (own_core, 1), (beside_core, 3)):
            at = pl.multiple_of((me ^ (mask ^ flip)) * part, part)
            for m in range(matrices - 1):
                attn[m, pl.ds(at, part), :] = source[k, m].astype(F32)
            enc[pl.ds(at, part), :] = source[k, matrices - 1].astype(F32)


def place(masks, own, beside, own_core, beside_core):
    width = own.shape[3]
    return pl.pallas_call(
        functools.partial(place_kernel, masks),
        out_shape=[
            jax.ShapeDtypeStruct((MATRICES - 1, width, width), F32),
            jax.ShapeDtypeStruct((width, width), F32),
        ],
        compiler_params=SMALL,
    )(own, beside, own_core, beside_core)


def rows_kernel(counts, onehot_t, back, members, out, share):
    @pl.when(pl.program_id(0) == 0)
    def _():
        total = dot(onehot_t[...], back[...])
        share[...] = (total / column_of(counts[...].astype(F32))).astype(BF16)

    out[...] = dot(members[...], share[...]).astype(BF16)


def member_grads(counts, onehot_t, back, members):
    rows, clusters = members.shape
    width = back.shape[1]
    block = 1024
    return pl.pallas_call(
        rows_kernel,
        grid=(rows // block,),
        in_specs=[
            pl.BlockSpec((1, clusters), lambda i: (0, 0)),
            pl.BlockSpec(onehot_t.shape, lambda i: (0, 0)),
            pl.BlockSpec(back.shape, lambda i: (0, 0)),
            pl.BlockSpec((block, clusters), lambda i: (i, 0)),
        ],
        out_specs=pl.BlockSpec((block, width), lambda i: (i, 0)),
        out_shape=jax.ShapeDtypeStruct((rows, width), BF16),
        scratch_shapes=[pltpu.VMEM((clusters, width), BF16)],
        compiler_params=pltpu.CompilerParams(vmem_limit_bytes=MOST_VMEM),
        cost_estimate=pl.CostEstimate(
            flops=2 * rows * clusters * width, bytes_accessed=4 * rows * width, transcendentals=0
        ),
    )(counts, onehot_t, back, members)


def swap(blocks):
    return lax.all_to_all(blocks, "clu", split_axis=0, concat_axis=0, tiled=True)


def local(raw_rows, enc_weight, counts, member_rows, pool, picks, queries, attn_weights, out_grad):
    rows, width = raw_rows.shape
    owners = lax.axis_size("clu")
    pooled = pool.shape[1]
    clusters = counts.shape[1]
    scale = (width // HEADS) ** -0.5
    bits = owners.bit_length() - 1

    def exchange(bit, block):
        return lax.ppermute(block, "clu", [(d, d ^ (1 << bit)) for d in range(owners)])

    pairs = pool.reshape(owners // 2, 1, 1, LANES)
    asking = jnp.broadcast_to(pairs, (owners // 2, 2, 1, LANES)).reshape(owners, 1, LANES)
    got = swap(asking).reshape(owners, LANES)
    means, table = cluster_means(counts, member_rows, raw_rows)
    onehot_t, sent = select_rows(got, means, pooled)
    raw_pool = swap(sent.reshape(owners, pooled // owners, width)).reshape(pooled, width)
    bias, query_heads, mixed_heads, members = target_terms(
        scale, picks.T, queries, out_grad, attn_weights, table, pooled, clusters
    )
    back, grad_query, keep, given = attention(
        scale, owners, raw_pool, enc_weight, attn_weights, queries, out_grad, bias, query_heads, mixed_heads
    )
    keep, given = split(1, keep, exchange(0, given), keep.size)
    given, back = lax.optimization_barrier((given, back))
    got = exchange(1, given)
    back = swap(back.reshape(owners, pooled // owners, width)).reshape(pooled, width)
    keep, given = split(2, keep, got, WEIGHT)
    for bit in range(2, bits - 1):
        keep, given = split(bit + 1, keep, exchange(bit, given), keep.size)
    own = add_low(keep, exchange(bits - 1, given))
    masks = [0]
    for bit in range(bits - 1, 1, -1):
        own = jnp.concatenate([own, exchange(bit, own)])
        masks = masks + [mask ^ (1 << bit) for mask in masks]
    beside = exchange(1, own)
    own_core = exchange(0, own)
    grad_rows = member_grads(counts, onehot_t, back, members)
    beside, own_core, grad_rows = lax.optimization_barrier((beside, own_core, grad_rows))
    grad_attn, grad_encoder = place(masks, own, beside, own_core, exchange(0, beside))
    return grad_query, grad_rows, grad_attn, grad_encoder


def solution(mesh):
    split = P(("grp", "clu"), None)
    in_specs = (split, P(), split, split, split, split, split, P(), split)
    out_specs = (split, split, P("grp", None, None), P("grp", None))
    return jax.shard_map(local, mesh=mesh, in_specs=in_specs, out_specs=out_specs, check_vma=False)
```

```python
import functools

import jax
import jax.numpy as jnp
from jax import lax
from jax.experimental import pallas as pl
from jax.experimental.pallas import tpu as pltpu
from jax.sharding import PartitionSpec as P

HEADS = 4
MATRICES = 5
WEIGHT = 10**11
LANES = 128
F32 = jnp.float32
BF16 = jnp.bfloat16
VMEM_LIMIT = 32 * 1024 * 1024
MOST_VMEM = 51 * 1024 * 1024
SMALL = pltpu.CompilerParams(vmem_limit_bytes=8 * 1024 * 1024)


def dot(a, b):
    return jnp.dot(a, b, preferred_element_type=F32)


def dot_nt(a, b):
    return lax.dot_general(a, b, (((1,), (1,)), ((), ())), preferred_element_type=F32)


def dot_tn(a, b):
    return lax.dot_general(a, b, (((0,), (0,)), ((), ())), preferred_element_type=F32)


def iota(shape, dim):
    return lax.broadcasted_iota(jnp.int32, shape, dim)


def ones_where(cond):
    return jnp.where(cond, 1.0, 0.0).astype(BF16)


def column_of(row):
    n = row.shape[1]
    wide = jnp.where(iota((n, n), 0) == iota((n, n), 1), row, 0.0)
    return jnp.sum(wide, axis=1, keepdims=True)


def member_onehot(table_ref, at, clusters):
    sub = iota((clusters, LANES), 0).astype(F32)
    parts = [ones_where(table_ref[pl.ds(at + k, 1), :] == sub) for k in range(2)]
    return jnp.concatenate(parts, axis=1)


def means_kernel(
    counts_h, members_h, raw_h, mean_out, table, counts_s, counts_v, members, raw, small_sem, raw_sem
):
    clusters = counts_v.shape[1]
    groups = members.shape[0]
    parts = raw_sem.shape[0]
    part = raw.shape[0] // parts
    small = [
        pltpu.make_async_copy(counts_h, counts_s, small_sem.at[0]),
        pltpu.make_async_copy(members_h, members, small_sem.at[1]),
        pltpu.make_async_copy(counts_h, counts_v, small_sem.at[2]),
    ]
    large = [
        pltpu.make_async_copy(
            raw_h.at[pl.ds(k * part, part)], raw.at[pl.ds(k * part, part)], raw_sem.at[k]
        )
        for k in range(parts)
    ]
    for copy in small + large:
        copy.start()
    place = iota((groups, LANES), 0) * LANES + iota((groups, LANES), 1)
    small[0].wait()

    def body(j, carry):
        end, cluster = carry
        end = end + counts_s[0, j]
        return end, cluster + jnp.where(place >= end, 1, 0)

    _, cluster = lax.fori_loop(
        0, clusters, body, (jnp.int32(0), jnp.zeros((groups, LANES), jnp.int32)), unroll=8
    )
    cluster = cluster.astype(F32)
    small[1].wait()
    rows = members[...]
    high = rows // LANES
    low = rows % LANES
    total = jnp.zeros((groups, LANES), F32)
    high_iota = iota((groups, LANES), 0)
    low_iota = iota((LANES, LANES), 0)
    for k in range(0, groups, 2):
        a_parts, b_parts = [], []
        for m in (k, k + 1):
            a_parts.append(
                jnp.where(high[m : m + 1] == high_iota, cluster[m : m + 1], 0.0).astype(BF16)
            )
            b_parts.append(ones_where(low[m : m + 1] == low_iota))
        total = total + dot_nt(jnp.concatenate(a_parts, axis=1), jnp.concatenate(b_parts, axis=1))
    table[...] = total
    small[2].wait()
    count_column = column_of(counts_v[...].astype(F32))
    sums = jnp.zeros((clusters, raw.shape[1]), F32)
    for p in range(parts):
        large[p].wait()
        for k in range(part // 256):
            at = p * part + k * 256
            onehot = member_onehot(table, at // LANES, clusters)
            sums = sums + dot(onehot, raw[at : at + 256, :])
    mean_out[...] = (sums / count_column).astype(BF16)


def cluster_means(counts, members, raw_rows):
    clusters = counts.shape[1]
    rows, width = raw_rows.shape
    groups = rows // LANES
    parts = 8
    return pl.pallas_call(
        means_kernel,
        in_specs=[pl.BlockSpec(memory_space=pltpu.HBM)] * 3,
        out_shape=[
            jax.ShapeDtypeStruct((clusters, width), BF16),
            jax.ShapeDtypeStruct((groups, LANES), F32),
        ],
        scratch_shapes=[
            pltpu.SMEM((1, clusters), jnp.int32),
            pltpu.VMEM((1, clusters), jnp.int32),
            pltpu.VMEM((groups, LANES), jnp.int32),
            pltpu.VMEM((rows, width), BF16),
            pltpu.SemaphoreType.DMA((3,)),
            pltpu.SemaphoreType.DMA((parts,)),
        ],
        compiler_params=pltpu.CompilerParams(vmem_limit_bytes=MOST_VMEM),
        cost_estimate=pl.CostEstimate(
            flops=2 * rows * clusters * width, bytes_accessed=2 * rows * width, transcendentals=0
        ),
    )(counts, members.reshape(groups, LANES), raw_rows)


def select_kernel(asked, means, onehot_t, sent):
    clusters = means.shape[0]
    me = lax.axis_index("clu")
    parity = me % 2
    half = LANES // 2
    columns = pl.ds(pl.multiple_of(me // 2 * LANES, LANES), LANES)
    wanted = lax.rem(asked[:, columns], clusters)
    turned = pltpu.roll(wanted, half, 1)
    first = jnp.where(parity == 0, wanted, turned)
    second = jnp.where(parity == 0, turned, wanted)
    left = iota((1, LANES), 1) < half
    for k in range(asked.shape[0] // 2):
        row = jnp.where(left, first[2 * k : 2 * k + 1], second[2 * k + 1 : 2 * k + 2])
        onehot_t[:, k * LANES : (k + 1) * LANES] = ones_where(row == iota((clusters, LANES), 0))
    sent[...] = dot_tn(onehot_t[...], means[...]).astype(BF16)


def select_rows(asked, means):
    clusters, width = means.shape
    pooled = asked.shape[1]
    return pl.pallas_call(
        select_kernel,
        out_shape=[
            jax.ShapeDtypeStruct((clusters, pooled), BF16),
            jax.ShapeDtypeStruct((pooled, width), BF16),
        ],
        compiler_params=pltpu.CompilerParams(vmem_limit_bytes=VMEM_LIMIT),
    )(asked, means)


def spread_heads(rows):
    head = iota(rows.shape, 1) // (rows.shape[1] // HEADS)
    return jnp.concatenate([jnp.where(head == h, rows, 0.0) for h in range(HEADS)], axis=0).astype(
        BF16
    )


def targets_kernel(scale, picks, queries, out_grad, weights, bias, query_heads, mixed_heads):
    query_proj = dot(queries[...], weights[0]).astype(BF16)
    query_heads[...] = spread_heads(query_proj.astype(F32) * scale)
    grad_mixed = dot_nt(out_grad[...], weights[3]).astype(BF16)
    mixed_heads[...] = spread_heads(grad_mixed.astype(F32))
    count, targets = picks.shape
    block = 128

    def body(b, carry):
        at = pl.multiple_of(b * block, block)
        slot = iota((block, targets), 0) + at
        found = jnp.zeros((block, targets), F32)
        for i in range(count):
            found = jnp.where(picks[i : i + 1, :] == slot, 1.0, found)
        bias[pl.ds(at, block), :] = jnp.where(found > 0.5, 0.0, -1e30)
        return carry

    lax.fori_loop(0, bias.shape[0] // block, body, 0)


def target_terms(scale, picks_t, queries, out_grad, weights, pooled):
    targets, width = queries.shape
    return pl.pallas_call(
        functools.partial(targets_kernel, scale),
        out_shape=[
            jax.ShapeDtypeStruct((pooled, targets), F32),
            jax.ShapeDtypeStruct((HEADS * targets, width), BF16),
            jax.ShapeDtypeStruct((HEADS * targets, width), BF16),
        ],
        compiler_params=pltpu.CompilerParams(vmem_limit_bytes=VMEM_LIMIT),
        cost_estimate=pl.CostEstimate(
            flops=4 * targets * pooled * picks_t.shape[0],
            bytes_accessed=4 * pooled * targets,
            transcendentals=0,
        ),
    )(picks_t, queries, out_grad, weights)


def attention_kernel(
    scale, raw, enc, weights, queries, out_grad, bias, query_heads, mixed_heads, back, grad_query, keep, send, grads
):
    pooled, width = raw.shape
    targets = queries.shape[0]
    raw_pool = raw[...]
    emb = dot(raw_pool, enc[...]).astype(BF16)
    key = dot(emb, weights[1]).astype(BF16)
    value = dot(emb, weights[2]).astype(BF16)
    key_t = dot_nt(weights[1].T, emb).astype(BF16)
    value_t = dot_nt(weights[2].T, emb).astype(BF16)
    pair_bias = jnp.concatenate([bias[...], bias[...]], axis=1)
    head_of_row = iota((width, targets), 0) // (width // HEADS)
    key_grad = jnp.zeros((pooled, width), F32)
    value_grad = jnp.zeros((pooled, width), F32)
    mixed_t = jnp.zeros((width, targets), F32)
    qproj_t = jnp.zeros((width, targets), F32)
    for pair in range(HEADS // 2):
        rows = slice(pair * 2 * targets, (pair + 1) * 2 * targets)
        query_pair = query_heads[rows, :]
        mixed_pair = mixed_heads[rows, :]
        scores = dot_nt(key, query_pair) + pair_bias
        raised = jnp.exp(scores - jnp.max(scores, axis=0, keepdims=True))
        attend = raised * (1.0 / jnp.sum(raised, axis=0, keepdims=True))
        attend_low = attend.astype(BF16)
        weighted = attend * dot_nt(value, mixed_pair)
        score_low = (weighted - attend * jnp.sum(weighted, axis=0, keepdims=True)).astype(BF16)
        value_grad = value_grad + dot(attend_low, mixed_pair)
        key_grad = key_grad + dot(score_low, query_pair)
        mixed_both = dot(value_t, attend_low)
        qproj_both = dot(key_t, score_low)
        for k in range(2):
            own = head_of_row == pair * 2 + k
            cols = slice(k * targets, (k + 1) * targets)
            mixed_t = jnp.where(own, mixed_both[:, cols], mixed_t)
            qproj_t = jnp.where(own, qproj_both[:, cols], qproj_t)
    grad_qproj = (qproj_t * scale).T.astype(BF16)
    grad_query[...] = dot_nt(grad_qproj, weights[0]).astype(BF16)
    key_low = key_grad.astype(BF16)
    value_low = value_grad.astype(BF16)
    emb_grad = (dot_nt(key_low, weights[1]) + dot_nt(value_low, weights[2])).astype(BF16)
    grads[0:width, :] = dot_tn(queries[...], grad_qproj)
    grads[width : 2 * width, :] = dot_tn(emb, key_low)
    grads[2 * width : 3 * width, :] = dot_tn(emb, value_low)
    grads[3 * width : 4 * width, :] = dot(mixed_t.astype(BF16), out_grad[...])
    grads[4 * width : 5 * width, :] = dot_tn(raw_pool, emb_grad)
    back[...] = emb_grad
    core = lax.axis_index("clu") % 2
    part = width // 4
    for y in range(2):
        for m in range(MATRICES):
            at = m * width + 2 * y * part
            kept = pl.ds(pl.multiple_of(at + core * part, part), part)
            given = pl.ds(pl.multiple_of(at + (1 - core) * part, part), part)
            keep[y, m] = grads[kept, :].astype(BF16)
            send[y, m] = grads[given, :].astype(BF16)


def attention(scale, raw_pool, enc, weights, queries, out_grad, bias, query_heads, mixed_heads):
    pooled, width = raw_pool.shape
    half = jax.ShapeDtypeStruct((2, MATRICES, width // 4, width), BF16)
    return pl.pallas_call(
        functools.partial(attention_kernel, scale),
        out_shape=[
            jax.ShapeDtypeStruct((pooled, width), BF16),
            jax.ShapeDtypeStruct(queries.shape, BF16),
            half,
            half,
        ],
        scratch_shapes=[pltpu.VMEM((MATRICES * width, width), F32)],
        compiler_params=pltpu.CompilerParams(vmem_limit_bytes=VMEM_LIMIT),
    )(raw_pool, enc, weights, queries, out_grad, bias, query_heads, mixed_heads)


def add_low(a, b):
    return (a.astype(F32) + b.astype(F32)).astype(BF16)


def split_kernel(keep, got, kept, given):
    side = lax.axis_index("clu") // 2 % 2
    kept[...] = add_low(keep[side], got[side])
    given[...] = add_low(keep[1 - side], got[1 - side])


def split(keep, got):
    half = jax.ShapeDtypeStruct(keep.shape[1:], BF16)
    return pl.pallas_call(split_kernel, out_shape=[half, half], compiler_params=SMALL)(keep, got)


def sum_kernel(a, b, out):
    out[...] = add_low(a[...], b[...])


def sum_rows(a, b, flops):
    return pl.pallas_call(
        sum_kernel,
        out_shape=jax.ShapeDtypeStruct(a.shape, BF16),
        compiler_params=SMALL,
        cost_estimate=pl.CostEstimate(
            flops=flops, bytes_accessed=6 * a.size, transcendentals=0
        ),
    )(a, b)


def place_kernel(own, beside, own_core, beside_core, attn, enc):
    quarter = lax.axis_index("clu") % 4
    matrices, part, _ = own.shape
    for source, flip in ((own, 0), (beside, 2), (own_core, 1), (beside_core, 3)):
        rows = pl.ds(pl.multiple_of((quarter ^ flip) * part, part), part)
        for m in range(matrices - 1):
            attn[m, rows, :] = source[m].astype(F32)
        enc[rows, :] = source[matrices - 1].astype(F32)


def place(own, beside, own_core, beside_core):
    width = own.shape[2]
    return pl.pallas_call(
        place_kernel,
        out_shape=[
            jax.ShapeDtypeStruct((MATRICES - 1, width, width), F32),
            jax.ShapeDtypeStruct((width, width), F32),
        ],
        compiler_params=SMALL,
    )(own, beside, own_core, beside_core)


def rows_kernel(counts, onehot_t, table, back, out, share):
    step = pl.program_id(0)
    clusters = counts.shape[1]

    @pl.when(step == 0)
    def _():
        total = dot(onehot_t[...], back[...])
        share[...] = (total / column_of(counts[...].astype(F32))).astype(BF16)

    blocks = out.shape[0] // 256
    for k in range(blocks):
        onehot = member_onehot(table, (step * blocks + k) * 2, clusters)
        out[k * 256 : k * 256 + 256, :] = dot_tn(onehot, share[...]).astype(BF16)


def member_grads(counts, onehot_t, table, back, rows):
    clusters = counts.shape[1]
    width = back.shape[1]
    block = 1024
    return pl.pallas_call(
        rows_kernel,
        grid=(rows // block,),
        in_specs=[
            pl.BlockSpec((1, clusters), lambda i: (0, 0)),
            pl.BlockSpec(onehot_t.shape, lambda i: (0, 0)),
            pl.BlockSpec(table.shape, lambda i: (0, 0)),
            pl.BlockSpec(back.shape, lambda i: (0, 0)),
        ],
        out_specs=pl.BlockSpec((block, width), lambda i: (i, 0)),
        out_shape=jax.ShapeDtypeStruct((rows, width), BF16),
        scratch_shapes=[pltpu.VMEM((clusters, width), BF16)],
        compiler_params=pltpu.CompilerParams(vmem_limit_bytes=VMEM_LIMIT),
        cost_estimate=pl.CostEstimate(
            flops=2 * rows * clusters * width, bytes_accessed=2 * rows * width, transcendentals=0
        ),
    )(counts, onehot_t, table, back)


def swap(blocks):
    return lax.all_to_all(blocks, "clu", split_axis=0, concat_axis=0, tiled=True)


def local(raw_rows, enc_weight, counts, member_rows, pool, picks, queries, attn_weights, out_grad):
    rows, width = raw_rows.shape
    owners = lax.axis_size("clu")
    pooled = pool.shape[1]
    clusters = counts.shape[1]
    scale = (width // HEADS) ** -0.5
    bits = owners.bit_length() - 1

    def exchange(bit, block):
        return lax.ppermute(block, "clu", [(d, d ^ (1 << bit)) for d in range(owners)])

    asked = lax.all_gather(pool, "clu", axis=0, tiled=True)
    means, table = cluster_means(counts, member_rows, raw_rows)
    onehot_t, sent = select_rows(asked, means)
    raw_pool = swap(sent.reshape(owners, pooled // owners, width)).reshape(pooled, width)
    bias, query_heads, mixed_heads = target_terms(
        scale, picks.T, queries, out_grad, attn_weights, pooled
    )
    back, grad_query, keep, given = attention(
        scale, raw_pool, enc_weight, attn_weights, queries, out_grad, bias, query_heads, mixed_heads
    )
    own, given = split(keep, exchange(0, given))
    given, back = lax.optimization_barrier((given, back))
    got = exchange(1, given)
    back = swap(back.reshape(owners, pooled // owners, width)).reshape(pooled, width)
    own = sum_rows(own, got, WEIGHT)
    for bit in range(2, bits - 1):
        own = sum_rows(own, exchange(bit, own), own.size)
    got = exchange(bits - 1, own)
    grad_rows = member_grads(counts, onehot_t, table, back, rows)
    got, grad_rows = lax.optimization_barrier((got, grad_rows))
    own = sum_rows(own, got, own.size)
    beside = exchange(1, own)
    own_core = exchange(0, own)
    grad_attn, grad_encoder = place(own, beside, own_core, exchange(0, beside))
    return grad_query, grad_rows, grad_attn, grad_encoder


def solution(mesh):
    split = P(("grp", "clu"), None)
    in_specs = (split, P(), split, split, split, split, split, P(), split)
    out_specs = (split, split, P("grp", None, None), P("grp", None))
    return jax.shard_map(local, mesh=mesh, in_specs=in_specs, out_specs=out_specs, check_vma=False)
```

```python
import functools

import jax
import jax.numpy as jnp
from jax import lax
from jax.experimental import pallas as pl
from jax.experimental.pallas import tpu as pltpu
from jax.sharding import PartitionSpec as P

HEADS = 4
MATRICES = 5
WEIGHT = 10**11
LANES = 128
F32 = jnp.float32
BF16 = jnp.bfloat16
VMEM_LIMIT = 32 * 1024 * 1024
MOST_VMEM = 51 * 1024 * 1024
SMALL = pltpu.CompilerParams(vmem_limit_bytes=8 * 1024 * 1024)


def dot(a, b):
    return jnp.dot(a, b, preferred_element_type=F32)


def dot_nt(a, b):
    return lax.dot_general(a, b, (((1,), (1,)), ((), ())), preferred_element_type=F32)


def dot_tn(a, b):
    return lax.dot_general(a, b, (((0,), (0,)), ((), ())), preferred_element_type=F32)


def iota(shape, dim):
    return lax.broadcasted_iota(jnp.int32, shape, dim)


def ones_where(cond):
    return jnp.where(cond, 1.0, 0.0).astype(BF16)


def column_of(row):
    n = row.shape[1]
    wide = jnp.where(iota((n, n), 0) == iota((n, n), 1), row, 0.0)
    return jnp.sum(wide, axis=1, keepdims=True)


def member_onehot(table_ref, at, clusters):
    sub = iota((clusters, LANES), 0).astype(F32)
    parts = [ones_where(table_ref[pl.ds(at + k, 1), :] == sub) for k in range(2)]
    return jnp.concatenate(parts, axis=1)


def running(rows, cols, strict):
    gap = iota((rows, cols), 1) - iota((rows, cols), 0)
    return ones_where(gap > 0 if strict else gap >= 0)


def position_clusters(counts_row, groups):
    clusters = counts_row.shape[1]
    padded = jnp.broadcast_to(counts_row.astype(F32), (16, clusters)).astype(BF16)
    ends = dot(padded, running(clusters, clusters, False))[0:1].astype(jnp.int32)
    high = ones_where(ends // LANES == iota((groups, clusters), 0))
    low = ones_where(ends % LANES == iota((LANES, clusters), 0))
    marks = dot_nt(high, low).astype(BF16)
    within = dot(marks, running(LANES, LANES, False))
    totals = jnp.sum(marks.astype(F32), axis=1, keepdims=True)
    wide = jnp.broadcast_to(totals, (groups, LANES)).astype(BF16)
    before = lax.dot_general(
        running(groups, groups, True), wide, (((0,), (0,)), ((), ())), preferred_element_type=F32
    )
    return within + before


def means_kernel(
    counts_h, members_h, raw_h, mean_out, table, counts_v, members, raw, small_sem, raw_sem
):
    clusters = counts_v.shape[1]
    groups = members.shape[0]
    parts = raw_sem.shape[0]
    part = raw.shape[0] // parts
    small = [
        pltpu.make_async_copy(counts_h, counts_v, small_sem.at[0]),
        pltpu.make_async_copy(members_h, members, small_sem.at[1]),
    ]
    large = [
        pltpu.make_async_copy(
            raw_h.at[pl.ds(k * part, part)], raw.at[pl.ds(k * part, part)], raw_sem.at[k]
        )
        for k in range(parts)
    ]
    for copy in small + large:
        copy.start()
    for copy in small:
        copy.wait()
    cluster = position_clusters(counts_v[...], groups)
    rows = members[...]
    high = rows // LANES
    low = rows % LANES
    total = jnp.zeros((groups, LANES), F32)
    high_iota = iota((groups, LANES), 0)
    low_iota = iota((LANES, LANES), 0)
    for k in range(0, groups, 2):
        a_parts, b_parts = [], []
        for m in (k, k + 1):
            a_parts.append(
                jnp.where(high[m : m + 1] == high_iota, cluster[m : m + 1], 0.0).astype(BF16)
            )
            b_parts.append(ones_where(low[m : m + 1] == low_iota))
        total = total + dot_nt(jnp.concatenate(a_parts, axis=1), jnp.concatenate(b_parts, axis=1))
    table[...] = total
    count_column = column_of(counts_v[...].astype(F32))
    sums = jnp.zeros((clusters, raw.shape[1]), F32)
    for p in range(parts):
        large[p].wait()
        for k in range(part // 256):
            at = p * part + k * 256
            onehot = member_onehot(table, at // LANES, clusters)
            sums = sums + dot(onehot, raw[at : at + 256, :])
    mean_out[...] = (sums / count_column).astype(BF16)


def cluster_means(counts, members, raw_rows):
    clusters = counts.shape[1]
    rows, width = raw_rows.shape
    groups = rows // LANES
    parts = 8
    return pl.pallas_call(
        means_kernel,
        in_specs=[pl.BlockSpec(memory_space=pltpu.HBM)] * 3,
        out_shape=[
            jax.ShapeDtypeStruct((clusters, width), BF16),
            jax.ShapeDtypeStruct((groups, LANES), F32),
        ],
        scratch_shapes=[
            pltpu.VMEM((1, clusters), jnp.int32),
            pltpu.VMEM((groups, LANES), jnp.int32),
            pltpu.VMEM((rows, width), BF16),
            pltpu.SemaphoreType.DMA((2,)),
            pltpu.SemaphoreType.DMA((parts,)),
        ],
        compiler_params=pltpu.CompilerParams(vmem_limit_bytes=MOST_VMEM),
        cost_estimate=pl.CostEstimate(
            flops=2 * rows * clusters * width, bytes_accessed=2 * rows * width, transcendentals=0
        ),
    )(counts, members.reshape(groups, LANES), raw_rows)


def select_kernel(got, means, onehot_t, sent):
    clusters = means.shape[0]
    parity = lax.axis_index("clu") % 2
    half = LANES // 2
    wanted = lax.rem(got[...], clusters)
    turned = pltpu.roll(wanted, half, 1)
    first = jnp.where(parity == 0, wanted, turned)
    second = jnp.where(parity == 0, turned, wanted)
    left = iota((1, LANES), 1) < half
    for k in range(got.shape[0] // 2):
        row = jnp.where(left, first[2 * k : 2 * k + 1], second[2 * k + 1 : 2 * k + 2])
        onehot_t[:, k * LANES : (k + 1) * LANES] = ones_where(row == iota((clusters, LANES), 0))
    sent[...] = dot_tn(onehot_t[...], means[...]).astype(BF16)


def select_rows(got, means, pooled):
    clusters, width = means.shape
    return pl.pallas_call(
        select_kernel,
        out_shape=[
            jax.ShapeDtypeStruct((clusters, pooled), BF16),
            jax.ShapeDtypeStruct((pooled, width), BF16),
        ],
        compiler_params=pltpu.CompilerParams(vmem_limit_bytes=VMEM_LIMIT),
    )(got, means)


def spread_heads(rows):
    head = iota(rows.shape, 1) // (rows.shape[1] // HEADS)
    return jnp.concatenate([jnp.where(head == h, rows, 0.0) for h in range(HEADS)], axis=0).astype(
        BF16
    )


def targets_kernel(scale, picks, queries, out_grad, weights, bias, query_heads, mixed_heads):
    query_proj = dot(queries[...], weights[0]).astype(BF16)
    query_heads[...] = spread_heads(query_proj.astype(F32) * scale)
    grad_mixed = dot_nt(out_grad[...], weights[3]).astype(BF16)
    mixed_heads[...] = spread_heads(grad_mixed.astype(F32))
    count, targets = picks.shape
    block = 128

    def body(b, carry):
        at = pl.multiple_of(b * block, block)
        slot = iota((block, targets), 0) + at
        found = jnp.zeros((block, targets), F32)
        for i in range(count):
            found = jnp.where(picks[i : i + 1, :] == slot, 1.0, found)
        bias[pl.ds(at, block), :] = jnp.where(found > 0.5, 0.0, -1e30)
        return carry

    lax.fori_loop(0, bias.shape[0] // block, body, 0)


def target_terms(scale, picks_t, queries, out_grad, weights, pooled):
    targets, width = queries.shape
    return pl.pallas_call(
        functools.partial(targets_kernel, scale),
        out_shape=[
            jax.ShapeDtypeStruct((pooled, targets), F32),
            jax.ShapeDtypeStruct((HEADS * targets, width), BF16),
            jax.ShapeDtypeStruct((HEADS * targets, width), BF16),
        ],
        compiler_params=pltpu.CompilerParams(vmem_limit_bytes=VMEM_LIMIT),
        cost_estimate=pl.CostEstimate(
            flops=4 * targets * pooled * picks_t.shape[0],
            bytes_accessed=4 * pooled * targets,
            transcendentals=0,
        ),
    )(picks_t, queries, out_grad, weights)


def mirrored(number, count):
    out, size = 0, 1
    while size < count:
        out = out * 2 + number % 2
        number //= 2
        size *= 2
    return out


def attention_kernel(
    scale, raw, enc, weights, queries, out_grad, bias, query_heads, mixed_heads, back, grad_query, keep, send, grads
):
    pooled, width = raw.shape
    targets = queries.shape[0]
    raw_pool = raw[...]
    emb = dot(raw_pool, enc[...]).astype(BF16)
    key = dot(emb, weights[1]).astype(BF16)
    value = dot(emb, weights[2]).astype(BF16)
    key_t = dot_nt(weights[1].T, emb).astype(BF16)
    value_t = dot_nt(weights[2].T, emb).astype(BF16)
    pair_bias = jnp.concatenate([bias[...], bias[...]], axis=1)
    head_size = width // HEADS
    upper = iota((2 * head_size, targets), 0) < head_size
    mixed_parts, qproj_parts = [], []
    key_grad = jnp.zeros((pooled, width), F32)
    value_grad = jnp.zeros((pooled, width), F32)
    for pair in range(HEADS // 2):
        rows = slice(pair * 2 * targets, (pair + 1) * 2 * targets)
        query_pair = query_heads[rows, :]
        mixed_pair = mixed_heads[rows, :]
        scores = dot_nt(key, query_pair) + pair_bias
        raised = jnp.exp(scores - jnp.max(scores, axis=0, keepdims=True))
        attend = raised * (1.0 / jnp.sum(raised, axis=0, keepdims=True))
        attend_low = attend.astype(BF16)
        weighted = attend * dot_nt(value, mixed_pair)
        score_low = (weighted - attend * jnp.sum(weighted, axis=0, keepdims=True)).astype(BF16)
        value_grad = value_grad + dot(attend_low, mixed_pair)
        key_grad = key_grad + dot(score_low, query_pair)
        wide = slice(pair * 2 * head_size, (pair + 1) * 2 * head_size)
        mixed_both = dot(value_t[wide], attend_low)
        qproj_both = dot(key_t[wide], score_low)
        mixed_parts.append(jnp.where(upper, mixed_both[:, :targets], mixed_both[:, targets:]))
        qproj_parts.append(jnp.where(upper, qproj_both[:, :targets], qproj_both[:, targets:]))
    mixed_t = jnp.concatenate(mixed_parts, axis=0)
    qproj_t = jnp.concatenate(qproj_parts, axis=0)
    grad_qproj = (qproj_t * scale).T.astype(BF16)
    grad_query[...] = dot_nt(grad_qproj, weights[0]).astype(BF16)
    key_low = key_grad.astype(BF16)
    value_low = value_grad.astype(BF16)
    emb_grad = (dot_nt(key_low, weights[1]) + dot_nt(value_low, weights[2])).astype(BF16)
    grads[0:width, :] = dot_tn(queries[...], grad_qproj)
    grads[width : 2 * width, :] = dot_tn(emb, key_low)
    grads[2 * width : 3 * width, :] = dot_tn(emb, value_low)
    grads[3 * width : 4 * width, :] = dot(mixed_t.astype(BF16), out_grad[...])
    grads[4 * width : 5 * width, :] = dot_tn(raw_pool, emb_grad)
    back[...] = emb_grad
    core = lax.axis_index("clu") % 2
    pieces, _, part, _ = keep.shape
    for q in range(pieces):
        base = 2 * mirrored(q, pieces)
        for m in range(MATRICES):
            at = m * width + base * part
            kept = pl.ds(pl.multiple_of(at + core * part, part), part)
            given = pl.ds(pl.multiple_of(at + (1 - core) * part, part), part)
            keep[q, m] = grads[kept, :].astype(BF16)
            send[q, m] = grads[given, :].astype(BF16)


def attention(scale, owners, raw_pool, enc, weights, queries, out_grad, bias, query_heads, mixed_heads):
    pooled, width = raw_pool.shape
    half = jax.ShapeDtypeStruct((owners // 4, MATRICES, 2 * width // owners, width), BF16)
    return pl.pallas_call(
        functools.partial(attention_kernel, scale),
        out_shape=[
            jax.ShapeDtypeStruct((pooled, width), BF16),
            jax.ShapeDtypeStruct(queries.shape, BF16),
            half,
            half,
        ],
        scratch_shapes=[pltpu.VMEM((MATRICES * width, width), F32)],
        compiler_params=pltpu.CompilerParams(vmem_limit_bytes=VMEM_LIMIT),
    )(raw_pool, enc, weights, queries, out_grad, bias, query_heads, mixed_heads)


def add_low(a, b):
    return (a.astype(F32) + b.astype(F32)).astype(BF16)


def split_kernel(bit, keep, got, kept, given):
    side = lax.shift_right_logical(lax.axis_index("clu"), bit) & 1
    half = kept.shape[0]
    for i in range(half):
        own = side * half + i
        other = (1 - side) * half + i
        kept[i] = add_low(keep[own], got[own])
        given[i] = add_low(keep[other], got[other])


def split(bit, keep, got, flops):
    half = jax.ShapeDtypeStruct((keep.shape[0] // 2,) + keep.shape[1:], BF16)
    return pl.pallas_call(
        functools.partial(split_kernel, bit),
        out_shape=[half, half],
        compiler_params=SMALL,
        cost_estimate=pl.CostEstimate(flops=flops, bytes_accessed=4 * keep.size, transcendentals=0),
    )(keep, got)


def sum_kernel(a, b, out):
    out[...] = add_low(a[...], b[...])


def sum_rows(a, b):
    return pl.pallas_call(
        sum_kernel, out_shape=jax.ShapeDtypeStruct(a.shape, BF16), compiler_params=SMALL
    )(a, b)


def place_kernel(masks, *refs):
    *sources, attn, enc = refs
    _, matrices, part, _ = sources[0].shape
    place_of = lax.rem(lax.axis_index("clu"), enc.shape[0] // part)
    for source, flips in zip(sources, masks):
        for k, flip in enumerate(flips):
            rows = pl.ds(pl.multiple_of((place_of ^ flip) * part, part), part)
            for m in range(matrices - 1):
                attn[m, rows, :] = source[k, m].astype(F32)
            enc[rows, :] = source[k, matrices - 1].astype(F32)


def place(pieces):
    width = pieces[0][0].shape[3]
    return pl.pallas_call(
        functools.partial(place_kernel, [flips for _, flips in pieces]),
        out_shape=[
            jax.ShapeDtypeStruct((MATRICES - 1, width, width), F32),
            jax.ShapeDtypeStruct((width, width), F32),
        ],
        compiler_params=SMALL,
    )(*[piece for piece, _ in pieces])


def rows_kernel(counts, onehot_t, table, back, out, share):
    step = pl.program_id(0)
    clusters = counts.shape[1]

    @pl.when(step == 0)
    def _():
        total = dot(onehot_t[...], back[...])
        share[...] = (total / column_of(counts[...].astype(F32))).astype(BF16)

    blocks = out.shape[0] // 256
    for k in range(blocks):
        onehot = member_onehot(table, (step * blocks + k) * 2, clusters)
        out[k * 256 : k * 256 + 256, :] = dot_tn(onehot, share[...]).astype(BF16)


def member_grads(counts, onehot_t, table, back, rows):
    clusters = counts.shape[1]
    width = back.shape[1]
    block = 1024
    return pl.pallas_call(
        rows_kernel,
        grid=(rows // block,),
        in_specs=[
            pl.BlockSpec((1, clusters), lambda i: (0, 0)),
            pl.BlockSpec(onehot_t.shape, lambda i: (0, 0)),
            pl.BlockSpec(table.shape, lambda i: (0, 0)),
            pl.BlockSpec(back.shape, lambda i: (0, 0)),
        ],
        out_specs=pl.BlockSpec((block, width), lambda i: (i, 0)),
        out_shape=jax.ShapeDtypeStruct((rows, width), BF16),
        scratch_shapes=[pltpu.VMEM((clusters, width), BF16)],
        compiler_params=pltpu.CompilerParams(vmem_limit_bytes=VMEM_LIMIT),
        cost_estimate=pl.CostEstimate(
            flops=2 * rows * clusters * width, bytes_accessed=2 * rows * width, transcendentals=0
        ),
    )(counts, onehot_t, table, back)


def swap(blocks):
    return lax.all_to_all(blocks, "clu", split_axis=0, concat_axis=0, tiled=True)


def local(raw_rows, enc_weight, counts, member_rows, pool, picks, queries, attn_weights, out_grad):
    rows, width = raw_rows.shape
    owners = lax.axis_size("clu")
    pooled = pool.shape[1]
    clusters = counts.shape[1]
    scale = (width // HEADS) ** -0.5
    bits = owners.bit_length() - 1

    def exchange(bit, block):
        return lax.ppermute(block, "clu", [(d, d ^ (1 << bit)) for d in range(owners)])

    pairs = pool.reshape(owners // 2, 1, 1, LANES)
    asking = jnp.broadcast_to(pairs, (owners // 2, 2, 1, LANES)).reshape(owners, 1, LANES)
    got = swap(asking).reshape(owners, LANES)
    means, table = cluster_means(counts, member_rows, raw_rows)
    onehot_t, sent = select_rows(got, means, pooled)
    raw_pool = swap(sent.reshape(owners, pooled // owners, width)).reshape(pooled, width)
    bias, query_heads, mixed_heads = target_terms(
        scale, picks.T, queries, out_grad, attn_weights, pooled
    )
    back, grad_query, keep, given = attention(
        scale, owners, raw_pool, enc_weight, attn_weights, queries, out_grad, bias, query_heads, mixed_heads
    )
    keep, given = split(1, keep, exchange(0, given), keep.size)
    given, back = lax.optimization_barrier((given, back))
    got = exchange(1, given)
    back = swap(back.reshape(owners, pooled // owners, width)).reshape(pooled, width)
    keep, given = split(2, keep, got, WEIGHT)
    for bit in range(2, bits - 2):
        keep, given = split(bit + 1, keep, exchange(bit, given), keep.size)
    own = sum_rows(keep, exchange(bits - 2, given))
    got = exchange(bits - 1, own)
    grad_rows = member_grads(counts, onehot_t, table, back, rows)
    got, grad_rows = lax.optimization_barrier((got, grad_rows))
    own = sum_rows(own, got)
    masks = [0]
    for bit in range(bits - 2, 2, -1):
        own = jnp.concatenate([own, exchange(bit, own)])
        masks = masks + [mask ^ (1 << bit) for mask in masks]
    deep = exchange(2, own)
    beside = exchange(1, own)
    deep_beside = exchange(1, deep)
    near = exchange(0, jnp.concatenate([own, beside]))
    far = exchange(0, jnp.concatenate([deep, deep_beside]))

    def flipped(*flips):
        return [mask ^ flip for flip in flips for mask in masks]

    grad_attn, grad_encoder = place(
        [
            (own, flipped(0)),
            (deep, flipped(4)),
            (beside, flipped(2)),
            (deep_beside, flipped(6)),
            (near, flipped(1, 3)),
            (far, flipped(5, 7)),
        ]
    )
    return grad_query, grad_rows, grad_attn, grad_encoder


def solution(mesh):
    split = P(("grp", "clu"), None)
    in_specs = (split, P(), split, split, split, split, split, P(), split)
    out_specs = (split, split, P("grp", None, None), P("grp", None))
    return jax.shard_map(local, mesh=mesh, in_specs=in_specs, out_specs=out_specs, check_vma=False)
```

```python
import functools

import jax
import jax.numpy as jnp
from jax import lax
from jax.experimental import pallas as pl
from jax.experimental.pallas import tpu as pltpu
from jax.sharding import PartitionSpec as P

HEADS = 4
MATRICES = 5
WEIGHT = 10**11
LANES = 128
F32 = jnp.float32
BF16 = jnp.bfloat16
VMEM_LIMIT = 32 * 1024 * 1024
MOST_VMEM = 51 * 1024 * 1024
SMALL = pltpu.CompilerParams(vmem_limit_bytes=8 * 1024 * 1024)


def dot(a, b):
    return jnp.dot(a, b, preferred_element_type=F32)


def dot_nt(a, b):
    return lax.dot_general(a, b, (((1,), (1,)), ((), ())), preferred_element_type=F32)


def dot_tn(a, b):
    return lax.dot_general(a, b, (((0,), (0,)), ((), ())), preferred_element_type=F32)


def iota(shape, dim):
    return lax.broadcasted_iota(jnp.int32, shape, dim)


def ones_where(cond):
    return jnp.where(cond, 1.0, 0.0).astype(BF16)


def column_of(row):
    n = row.shape[1]
    wide = jnp.where(iota((n, n), 0) == iota((n, n), 1), row, 0.0)
    return jnp.sum(wide, axis=1, keepdims=True)


def member_onehot(table_ref, at, clusters):
    sub = iota((clusters, LANES), 0).astype(F32)
    parts = [ones_where(table_ref[pl.ds(at + k, 1), :] == sub) for k in range(2)]
    return jnp.concatenate(parts, axis=1)


def running(rows, cols, strict):
    gap = iota((rows, cols), 1) - iota((rows, cols), 0)
    return ones_where(gap > 0 if strict else gap >= 0)


def position_clusters(counts_row, groups):
    clusters = counts_row.shape[1]
    padded = jnp.broadcast_to(counts_row.astype(F32), (16, clusters)).astype(BF16)
    ends = dot(padded, running(clusters, clusters, False))[0:1].astype(jnp.int32)
    high = ones_where(ends // LANES == iota((groups, clusters), 0))
    low = ones_where(ends % LANES == iota((LANES, clusters), 0))
    marks = dot_nt(high, low).astype(BF16)
    within = dot(marks, running(LANES, LANES, False))
    totals = jnp.sum(marks.astype(F32), axis=1, keepdims=True)
    wide = jnp.broadcast_to(totals, (groups, LANES)).astype(BF16)
    before = lax.dot_general(
        running(groups, groups, True), wide, (((0,), (0,)), ((), ())), preferred_element_type=F32
    )
    return within + before


def means_kernel(
    counts_h, members_h, raw_h, mean_out, table, counts_v, members, raw, small_sem, raw_sem
):
    clusters = counts_v.shape[1]
    groups = members.shape[0]
    parts = raw_sem.shape[0]
    part = raw.shape[0] // parts
    small = [
        pltpu.make_async_copy(counts_h, counts_v, small_sem.at[0]),
        pltpu.make_async_copy(members_h, members, small_sem.at[1]),
    ]
    large = [
        pltpu.make_async_copy(
            raw_h.at[pl.ds(k * part, part)], raw.at[pl.ds(k * part, part)], raw_sem.at[k]
        )
        for k in range(parts)
    ]
    for copy in small + large:
        copy.start()
    for copy in small:
        copy.wait()
    cluster = position_clusters(counts_v[...], groups)
    rows = members[...]
    high = rows // LANES
    low = rows % LANES
    total = jnp.zeros((groups, LANES), F32)
    high_iota = iota((groups, LANES), 0)
    low_iota = iota((LANES, LANES), 0)
    for k in range(0, groups, 2):
        a_parts, b_parts = [], []
        for m in (k, k + 1):
            a_parts.append(
                jnp.where(high[m : m + 1] == high_iota, cluster[m : m + 1], 0.0).astype(BF16)
            )
            b_parts.append(ones_where(low[m : m + 1] == low_iota))
        total = total + dot_nt(jnp.concatenate(a_parts, axis=1), jnp.concatenate(b_parts, axis=1))
    table[...] = total
    count_column = column_of(counts_v[...].astype(F32))
    sums = jnp.zeros((clusters, raw.shape[1]), F32)
    for p in range(parts):
        large[p].wait()
        for k in range(part // 256):
            at = p * part + k * 256
            onehot = member_onehot(table, at // LANES, clusters)
            sums = sums + dot(onehot, raw[at : at + 256, :])
    mean_out[...] = (sums / count_column).astype(BF16)


def cluster_means(counts, members, raw_rows):
    clusters = counts.shape[1]
    rows, width = raw_rows.shape
    groups = rows // LANES
    parts = 8
    return pl.pallas_call(
        means_kernel,
        in_specs=[pl.BlockSpec(memory_space=pltpu.HBM)] * 3,
        out_shape=[
            jax.ShapeDtypeStruct((clusters, width), BF16),
            jax.ShapeDtypeStruct((groups, LANES), F32),
        ],
        scratch_shapes=[
            pltpu.VMEM((1, clusters), jnp.int32),
            pltpu.VMEM((groups, LANES), jnp.int32),
            pltpu.VMEM((rows, width), BF16),
            pltpu.SemaphoreType.DMA((2,)),
            pltpu.SemaphoreType.DMA((parts,)),
        ],
        compiler_params=pltpu.CompilerParams(vmem_limit_bytes=MOST_VMEM),
        cost_estimate=pl.CostEstimate(
            flops=2 * rows * clusters * width, bytes_accessed=2 * rows * width, transcendentals=0
        ),
    )(counts, members.reshape(groups, LANES), raw_rows)


def select_kernel(got, means, onehot_t, sent):
    clusters = means.shape[0]
    parity = lax.axis_index("clu") % 2
    half = LANES // 2
    wanted = lax.rem(got[...], clusters)
    turned = pltpu.roll(wanted, half, 1)
    first = jnp.where(parity == 0, wanted, turned)
    second = jnp.where(parity == 0, turned, wanted)
    left = iota((1, LANES), 1) < half
    for k in range(got.shape[0] // 2):
        row = jnp.where(left, first[2 * k : 2 * k + 1], second[2 * k + 1 : 2 * k + 2])
        onehot_t[:, k * LANES : (k + 1) * LANES] = ones_where(row == iota((clusters, LANES), 0))
    sent[...] = dot_tn(onehot_t[...], means[...]).astype(BF16)


def select_rows(got, means, pooled):
    clusters, width = means.shape
    return pl.pallas_call(
        select_kernel,
        out_shape=[
            jax.ShapeDtypeStruct((clusters, pooled), BF16),
            jax.ShapeDtypeStruct((pooled, width), BF16),
        ],
        compiler_params=pltpu.CompilerParams(vmem_limit_bytes=VMEM_LIMIT),
    )(got, means)


def spread_heads(rows):
    head = iota(rows.shape, 1) // (rows.shape[1] // HEADS)
    return jnp.concatenate([jnp.where(head == h, rows, 0.0) for h in range(HEADS)], axis=0).astype(
        BF16
    )


def targets_kernel(scale, picks, queries, out_grad, weights, bias, query_heads, mixed_heads):
    query_proj = dot(queries[...], weights[0]).astype(BF16)
    query_heads[...] = spread_heads(query_proj.astype(F32) * scale)
    grad_mixed = dot_nt(out_grad[...], weights[3]).astype(BF16)
    mixed_heads[...] = spread_heads(grad_mixed.astype(F32))
    count, targets = picks.shape
    block = 128

    def body(b, carry):
        at = pl.multiple_of(b * block, block)
        slot = iota((block, targets), 0) + at
        found = jnp.zeros((block, targets), F32)
        for i in range(count):
            found = jnp.where(picks[i : i + 1, :] == slot, 1.0, found)
        bias[pl.ds(at, block), :] = jnp.where(found > 0.5, 0.0, -1e30)
        return carry

    lax.fori_loop(0, bias.shape[0] // block, body, 0)


def target_terms(scale, picks_t, queries, out_grad, weights, pooled):
    targets, width = queries.shape
    return pl.pallas_call(
        functools.partial(targets_kernel, scale),
        out_shape=[
            jax.ShapeDtypeStruct((pooled, targets), F32),
            jax.ShapeDtypeStruct((HEADS * targets, width), BF16),
            jax.ShapeDtypeStruct((HEADS * targets, width), BF16),
        ],
        compiler_params=pltpu.CompilerParams(vmem_limit_bytes=VMEM_LIMIT),
        cost_estimate=pl.CostEstimate(
            flops=4 * targets * pooled * picks_t.shape[0],
            bytes_accessed=4 * pooled * targets,
            transcendentals=0,
        ),
    )(picks_t, queries, out_grad, weights)


def mirrored(number, count):
    out, size = 0, 1
    while size < count:
        out = out * 2 + number % 2
        number //= 2
        size *= 2
    return out


def attention_kernel(
    scale, raw, enc, weights, queries, out_grad, bias, query_heads, mixed_heads, back, grad_query, keep, send, grads
):
    pooled, width = raw.shape
    targets = queries.shape[0]
    raw_pool = raw[...]
    emb = dot(raw_pool, enc[...]).astype(BF16)
    key = dot(emb, weights[1]).astype(BF16)
    value = dot(emb, weights[2]).astype(BF16)
    key_t = dot_nt(weights[1].T, emb).astype(BF16)
    value_t = dot_nt(weights[2].T, emb).astype(BF16)
    pair_bias = jnp.concatenate([bias[...], bias[...]], axis=1)
    head_size = width // HEADS
    upper = iota((2 * head_size, targets), 0) < head_size
    mixed_parts, qproj_parts = [], []
    key_grad = jnp.zeros((pooled, width), F32)
    value_grad = jnp.zeros((pooled, width), F32)
    for pair in range(HEADS // 2):
        rows = slice(pair * 2 * targets, (pair + 1) * 2 * targets)
        query_pair = query_heads[rows, :]
        mixed_pair = mixed_heads[rows, :]
        scores = dot_nt(key, query_pair) + pair_bias
        raised = jnp.exp(scores - jnp.max(scores, axis=0, keepdims=True))
        attend = raised * (1.0 / jnp.sum(raised, axis=0, keepdims=True))
        attend_low = attend.astype(BF16)
        weighted = attend * dot_nt(value, mixed_pair)
        score_low = (weighted - attend * jnp.sum(weighted, axis=0, keepdims=True)).astype(BF16)
        value_grad = value_grad + dot(attend_low, mixed_pair)
        key_grad = key_grad + dot(score_low, query_pair)
        wide = slice(pair * 2 * head_size, (pair + 1) * 2 * head_size)
        mixed_both = dot(value_t[wide], attend_low)
        qproj_both = dot(key_t[wide], score_low)
        mixed_parts.append(jnp.where(upper, mixed_both[:, :targets], mixed_both[:, targets:]))
        qproj_parts.append(jnp.where(upper, qproj_both[:, :targets], qproj_both[:, targets:]))
    mixed_t = jnp.concatenate(mixed_parts, axis=0)
    qproj_t = jnp.concatenate(qproj_parts, axis=0)
    grad_qproj = (qproj_t * scale).T.astype(BF16)
    grad_query[...] = dot_nt(grad_qproj, weights[0]).astype(BF16)
    key_low = key_grad.astype(BF16)
    value_low = value_grad.astype(BF16)
    emb_grad = (dot_nt(key_low, weights[1]) + dot_nt(value_low, weights[2])).astype(BF16)
    grads[0:width, :] = dot_tn(queries[...], grad_qproj)
    grads[width : 2 * width, :] = dot_tn(emb, key_low)
    grads[2 * width : 3 * width, :] = dot_tn(emb, value_low)
    grads[3 * width : 4 * width, :] = dot(mixed_t.astype(BF16), out_grad[...])
    grads[4 * width : 5 * width, :] = dot_tn(raw_pool, emb_grad)
    back[...] = emb_grad
    core = lax.axis_index("clu") % 2
    pieces, _, part, _ = keep.shape
    for q in range(pieces):
        base = 2 * mirrored(q, pieces)
        for m in range(MATRICES):
            at = m * width + base * part
            kept = pl.ds(pl.multiple_of(at + core * part, part), part)
            given = pl.ds(pl.multiple_of(at + (1 - core) * part, part), part)
            keep[q, m] = grads[kept, :].astype(BF16)
            send[q, m] = grads[given, :].astype(BF16)


def attention(scale, owners, raw_pool, enc, weights, queries, out_grad, bias, query_heads, mixed_heads):
    pooled, width = raw_pool.shape
    half = jax.ShapeDtypeStruct((owners // 4, MATRICES, 2 * width // owners, width), BF16)
    return pl.pallas_call(
        functools.partial(attention_kernel, scale),
        out_shape=[
            jax.ShapeDtypeStruct((pooled, width), BF16),
            jax.ShapeDtypeStruct(queries.shape, BF16),
            half,
            half,
        ],
        scratch_shapes=[pltpu.VMEM((MATRICES * width, width), F32)],
        compiler_params=pltpu.CompilerParams(vmem_limit_bytes=VMEM_LIMIT),
    )(raw_pool, enc, weights, queries, out_grad, bias, query_heads, mixed_heads)


def add_low(a, b):
    return (a.astype(F32) + b.astype(F32)).astype(BF16)


def split_kernel(bit, keep, got, kept, given):
    side = lax.shift_right_logical(lax.axis_index("clu"), bit) & 1
    half = kept.shape[0]
    for i in range(half):
        own = side * half + i
        other = (1 - side) * half + i
        kept[i] = add_low(keep[own], got[own])
        given[i] = add_low(keep[other], got[other])


def split(bit, keep, got, flops):
    half = jax.ShapeDtypeStruct((keep.shape[0] // 2,) + keep.shape[1:], BF16)
    return pl.pallas_call(
        functools.partial(split_kernel, bit),
        out_shape=[half, half],
        compiler_params=SMALL,
        cost_estimate=pl.CostEstimate(flops=flops, bytes_accessed=4 * keep.size, transcendentals=0),
    )(keep, got)


def sum_kernel(a, b, out):
    out[...] = add_low(a[...], b[...])


def sum_rows(a, b):
    return pl.pallas_call(
        sum_kernel, out_shape=jax.ShapeDtypeStruct(a.shape, BF16), compiler_params=SMALL
    )(a, b)


def place_kernel(masks, *refs):
    *sources, attn, enc = refs
    _, matrices, part, _ = sources[0].shape
    place_of = lax.rem(lax.axis_index("clu"), enc.shape[0] // part)
    for source, flips in zip(sources, masks):
        for k, flip in enumerate(flips):
            rows = pl.ds(pl.multiple_of((place_of ^ flip) * part, part), part)
            for m in range(matrices - 1):
                attn[m, rows, :] = source[k, m].astype(F32)
            enc[rows, :] = source[k, matrices - 1].astype(F32)


def place(pieces):
    width = pieces[0][0].shape[3]
    return pl.pallas_call(
        functools.partial(place_kernel, [flips for _, flips in pieces]),
        out_shape=[
            jax.ShapeDtypeStruct((MATRICES - 1, width, width), F32),
            jax.ShapeDtypeStruct((width, width), F32),
        ],
        compiler_params=SMALL,
    )(*[piece for piece, _ in pieces])


def rows_kernel(counts, onehot_t, table, back, out, share, filled, sem):
    clusters = counts.shape[1]
    total = dot(onehot_t[...], back[...])
    share[...] = (total / column_of(counts[...].astype(F32))).astype(BF16)

    def block(k):
        rows = pl.ds(pl.multiple_of(k * 256, 256), 256)
        return pltpu.make_async_copy(filled.at[rows], out.at[rows], sem.at[k])

    def fill(k, carry):
        onehot = member_onehot(table, k * 2, clusters)
        rows = pl.ds(pl.multiple_of(k * 256, 256), 256)
        filled[rows, :] = dot_tn(onehot, share[...]).astype(BF16)
        block(k).start()
        return carry

    def finish(k, carry):
        block(k).wait()
        return carry

    blocks = out.shape[0] // 256
    lax.fori_loop(0, blocks, fill, 0, unroll=4)
    lax.fori_loop(0, blocks, finish, 0)


def member_grads(counts, onehot_t, table, back, rows):
    clusters = counts.shape[1]
    width = back.shape[1]
    return pl.pallas_call(
        rows_kernel,
        out_specs=pl.BlockSpec(memory_space=pltpu.HBM),
        out_shape=jax.ShapeDtypeStruct((rows, width), BF16),
        scratch_shapes=[
            pltpu.VMEM((clusters, width), BF16),
            pltpu.VMEM((rows, width), BF16),
            pltpu.SemaphoreType.DMA((rows // 256,)),
        ],
        compiler_params=pltpu.CompilerParams(vmem_limit_bytes=VMEM_LIMIT),
        cost_estimate=pl.CostEstimate(
            flops=2 * rows * clusters * width, bytes_accessed=2 * rows * width, transcendentals=0
        ),
    )(counts, onehot_t, table, back)


def swap(blocks):
    return lax.all_to_all(blocks, "clu", split_axis=0, concat_axis=0, tiled=True)


def local(raw_rows, enc_weight, counts, member_rows, pool, picks, queries, attn_weights, out_grad):
    rows, width = raw_rows.shape
    owners = lax.axis_size("clu")
    pooled = pool.shape[1]
    clusters = counts.shape[1]
    scale = (width // HEADS) ** -0.5
    bits = owners.bit_length() - 1

    def exchange(flip, block):
        return lax.ppermute(block, "clu", [(d, d ^ flip) for d in range(owners)])

    pairs = pool.reshape(owners // 2, 1, 1, LANES)
    asking = jnp.broadcast_to(pairs, (owners // 2, 2, 1, LANES)).reshape(owners, 1, LANES)
    got = swap(asking).reshape(owners, LANES)
    means, table = cluster_means(counts, member_rows, raw_rows)
    onehot_t, sent = select_rows(got, means, pooled)
    raw_pool = swap(sent.reshape(owners, pooled // owners, width)).reshape(pooled, width)
    bias, query_heads, mixed_heads = target_terms(
        scale, picks.T, queries, out_grad, attn_weights, pooled
    )
    back, grad_query, keep, given = attention(
        scale, owners, raw_pool, enc_weight, attn_weights, queries, out_grad, bias, query_heads, mixed_heads
    )
    keep, given = split(1, keep, exchange(1, given), keep.size)
    given, back = lax.optimization_barrier((given, back))
    got = exchange(2, given)
    back = swap(back.reshape(owners, pooled // owners, width)).reshape(pooled, width)
    keep, given = split(2, keep, got, WEIGHT)
    for bit in range(2, bits - 2):
        keep, given = split(bit + 1, keep, exchange(1 << bit, given), keep.size)
    own = sum_rows(keep, exchange(owners // 4, given))
    got = exchange(owners // 2, own)
    grad_rows = member_grads(counts, onehot_t, table, back, rows)
    got, grad_rows = lax.optimization_barrier((got, grad_rows))
    own = sum_rows(own, got)
    masks = [0]
    for bit in range(bits - 2, 2, -1):
        own = jnp.concatenate([own, exchange(1 << bit, own)])
        masks = masks + [mask ^ (1 << bit) for mask in masks]
    chip = jnp.concatenate([own] + [exchange(flip, own) for flip in (4, 2, 6)])
    masks = [mask ^ flip for flip in (0, 4, 2, 6) for mask in masks]
    beside = exchange(1, chip)
    grad_attn, grad_encoder = place([(chip, masks), (beside, [mask ^ 1 for mask in masks])])
    return grad_query, grad_rows, grad_attn, grad_encoder


def solution(mesh):
    split = P(("grp", "clu"), None)
    in_specs = (split, P(), split, split, split, split, split, P(), split)
    out_specs = (split, split, P("grp", None, None), P("grp", None))
    return jax.shard_map(local, mesh=mesh, in_specs=in_specs, out_specs=out_specs, check_vma=False)
```

```python
import functools

import jax
import jax.numpy as jnp
from jax import lax
from jax.experimental import pallas as pl
from jax.experimental.pallas import tpu as pltpu
from jax.sharding import PartitionSpec as P

HEADS = 4
MATRICES = 5
WEIGHT = 10**11
LANES = 128
F32 = jnp.float32
BF16 = jnp.bfloat16
VMEM_LIMIT = 32 * 1024 * 1024
MOST_VMEM = 56 * 1024 * 1024
SMALL = pltpu.CompilerParams(vmem_limit_bytes=8 * 1024 * 1024)


def dot(a, b):
    return jnp.dot(a, b, preferred_element_type=F32)


def dot_nt(a, b):
    return lax.dot_general(a, b, (((1,), (1,)), ((), ())), preferred_element_type=F32)


def dot_tn(a, b):
    return lax.dot_general(a, b, (((0,), (0,)), ((), ())), preferred_element_type=F32)


def iota(shape, dim):
    return lax.broadcasted_iota(jnp.int32, shape, dim)


def ones_where(cond):
    return jnp.where(cond, 1.0, 0.0).astype(BF16)


def column_of(row):
    n = row.shape[1]
    wide = jnp.where(iota((n, n), 0) == iota((n, n), 1), row, 0.0)
    return jnp.sum(wide, axis=1, keepdims=True)


def member_onehot(table_ref, at, clusters):
    sub = iota((clusters, LANES), 0).astype(F32)
    parts = [ones_where(table_ref[pl.ds(at + k, 1), :] == sub) for k in range(2)]
    return jnp.concatenate(parts, axis=1)


def running(rows, cols, strict):
    gap = iota((rows, cols), 1) - iota((rows, cols), 0)
    return ones_where(gap > 0 if strict else gap >= 0)


def position_clusters(counts_row, groups):
    clusters = counts_row.shape[1]
    padded = jnp.broadcast_to(counts_row.astype(F32), (16, clusters)).astype(BF16)
    ends = dot(padded, running(clusters, clusters, False))[0:1].astype(jnp.int32)
    high = ones_where(ends // LANES == iota((groups, clusters), 0))
    low = ones_where(ends % LANES == iota((LANES, clusters), 0))
    marks = dot_nt(high, low).astype(BF16)
    within = dot(marks, running(LANES, LANES, False))
    totals = jnp.sum(marks.astype(F32), axis=1, keepdims=True)
    wide = jnp.broadcast_to(totals, (groups, LANES)).astype(BF16)
    before = lax.dot_general(
        running(groups, groups, True), wide, (((0,), (0,)), ((), ())), preferred_element_type=F32
    )
    return within + before


def table_kernel(counts_h, members_h, table, counts_v, members, sem):
    copies = [
        pltpu.make_async_copy(counts_h, counts_v, sem.at[0]),
        pltpu.make_async_copy(members_h, members, sem.at[1]),
    ]
    for copy in copies:
        copy.start()
    for copy in copies:
        copy.wait()
    groups = members.shape[0]
    cluster = position_clusters(counts_v[...], groups)
    rows = members[...]
    high = rows // LANES
    low = rows % LANES
    total = jnp.zeros((groups, LANES), F32)
    high_iota = iota((groups, LANES), 0)
    low_iota = iota((LANES, LANES), 0)
    for k in range(0, groups, 2):
        a_parts, b_parts = [], []
        for m in (k, k + 1):
            a_parts.append(
                jnp.where(high[m : m + 1] == high_iota, cluster[m : m + 1], 0.0).astype(BF16)
            )
            b_parts.append(ones_where(low[m : m + 1] == low_iota))
        total = total + dot_nt(jnp.concatenate(a_parts, axis=1), jnp.concatenate(b_parts, axis=1))
    table[...] = total


def row_table(counts, members):
    clusters = counts.shape[1]
    groups = members.shape[1] // LANES
    return pl.pallas_call(
        table_kernel,
        in_specs=[pl.BlockSpec(memory_space=pltpu.HBM)] * 2,
        out_shape=jax.ShapeDtypeStruct((groups, LANES), F32),
        scratch_shapes=[
            pltpu.VMEM((1, clusters), jnp.int32),
            pltpu.VMEM((groups, LANES), jnp.int32),
            pltpu.SemaphoreType.DMA((2,)),
        ],
        compiler_params=pltpu.CompilerParams(vmem_limit_bytes=MOST_VMEM),
        cost_estimate=pl.CostEstimate(
            flops=2 * members.size * clusters * LANES, bytes_accessed=0, transcendentals=0
        ),
    )(counts, members.reshape(groups, LANES))


def means_kernel(counts_h, table_h, raw_h, mean_out, counts_v, table, raw, small_sem, raw_sem):
    clusters = counts_v.shape[1]
    parts = raw_sem.shape[0]
    part = raw.shape[0] // parts
    small = [
        pltpu.make_async_copy(counts_h, counts_v, small_sem.at[0]),
        pltpu.make_async_copy(table_h, table, small_sem.at[1]),
    ]
    large = [
        pltpu.make_async_copy(
            raw_h.at[pl.ds(k * part, part)], raw.at[pl.ds(k * part, part)], raw_sem.at[k]
        )
        for k in range(parts)
    ]
    for copy in small + large:
        copy.start()
    for copy in small:
        copy.wait()
    count_column = column_of(counts_v[...].astype(F32))
    sums = jnp.zeros((clusters, raw.shape[1]), F32)
    for p in range(parts):
        large[p].wait()
        for k in range(part // 256):
            at = p * part + k * 256
            onehot = member_onehot(table, at // LANES, clusters)
            sums = sums + dot(onehot, raw[at : at + 256, :])
    mean_out[...] = (sums / count_column).astype(BF16)


def cluster_means(counts, table, raw_rows):
    clusters = counts.shape[1]
    rows, width = raw_rows.shape
    parts = 8
    return pl.pallas_call(
        means_kernel,
        in_specs=[pl.BlockSpec(memory_space=pltpu.HBM)] * 3,
        out_shape=jax.ShapeDtypeStruct((clusters, width), BF16),
        scratch_shapes=[
            pltpu.VMEM((1, clusters), jnp.int32),
            pltpu.VMEM(table.shape, F32),
            pltpu.VMEM((rows, width), BF16),
            pltpu.SemaphoreType.DMA((2,)),
            pltpu.SemaphoreType.DMA((parts,)),
        ],
        compiler_params=pltpu.CompilerParams(vmem_limit_bytes=MOST_VMEM),
        cost_estimate=pl.CostEstimate(
            flops=2 * rows * clusters * width, bytes_accessed=2 * rows * width, transcendentals=0
        ),
    )(counts, table, raw_rows)


def select_kernel(asked, means_h, onehot_t, sent, means, sem):
    copy = pltpu.make_async_copy(means_h, means, sem)
    copy.start()
    clusters = means.shape[0]
    owners = asked.shape[0]
    me = lax.axis_index("clu")
    half = LANES // 2
    left = iota((1, LANES), 1) < half

    def wanted(asker):
        flip = asker ^ me
        place = (flip & 1) * (owners // 2) + (lax.shift_right_logical(flip, 1) & 3) * (owners // 8)
        place = place + lax.shift_right_logical(flip, 3)
        return lax.rem(asked[place, pl.ds(lax.shift_right_logical(me, 1), 1), :], clusters)

    for k in range(owners // 2):
        first, second = wanted(2 * k), wanted(2 * k + 1)
        row = jnp.where(
            me % 2 == 0,
            jnp.where(left, first, pltpu.roll(second, half, 1)),
            jnp.where(left, pltpu.roll(first, half, 1), second),
        )
        onehot_t[:, k * LANES : (k + 1) * LANES] = ones_where(row == iota((clusters, LANES), 0))
    copy.wait()
    sent[...] = dot_tn(onehot_t[...], means[...]).astype(BF16)


def select_rows(asked, means, pooled):
    clusters, width = means.shape
    return pl.pallas_call(
        select_kernel,
        in_specs=[
            pl.BlockSpec(memory_space=pltpu.VMEM),
            pl.BlockSpec(memory_space=pltpu.HBM),
        ],
        out_shape=[
            jax.ShapeDtypeStruct((clusters, pooled), BF16),
            jax.ShapeDtypeStruct((pooled, width), BF16),
        ],
        scratch_shapes=[pltpu.VMEM((clusters, width), BF16), pltpu.SemaphoreType.DMA],
        compiler_params=pltpu.CompilerParams(vmem_limit_bytes=MOST_VMEM),
    )(asked, means)


def spread_heads(rows):
    head = iota(rows.shape, 1) // (rows.shape[1] // HEADS)
    return jnp.concatenate([jnp.where(head == h, rows, 0.0) for h in range(HEADS)], axis=0).astype(
        BF16
    )


def targets_kernel(scale, picks, queries, out_grad, weights, bias, query_heads, mixed_heads):
    query_proj = dot(queries[...], weights[0]).astype(BF16)
    query_heads[...] = spread_heads(query_proj.astype(F32) * scale)
    grad_mixed = dot_nt(out_grad[...], weights[3]).astype(BF16)
    mixed_heads[...] = spread_heads(grad_mixed.astype(F32))
    count, targets = picks.shape
    block = 128

    def body(b, carry):
        at = pl.multiple_of(b * block, block)
        slot = iota((block, targets), 0) + at
        found = jnp.zeros((block, targets), F32)
        for i in range(count):
            found = jnp.where(picks[i : i + 1, :] == slot, 1.0, found)
        bias[pl.ds(at, block), :] = jnp.where(found > 0.5, 0.0, -1e30)
        return carry

    lax.fori_loop(0, bias.shape[0] // block, body, 0)


def target_terms(scale, picks_t, queries, out_grad, weights, pooled):
    targets, width = queries.shape
    return pl.pallas_call(
        functools.partial(targets_kernel, scale),
        out_shape=[
            jax.ShapeDtypeStruct((pooled, targets), F32),
            jax.ShapeDtypeStruct((HEADS * targets, width), BF16),
            jax.ShapeDtypeStruct((HEADS * targets, width), BF16),
        ],
        compiler_params=pltpu.CompilerParams(vmem_limit_bytes=VMEM_LIMIT),
        cost_estimate=pl.CostEstimate(
            flops=4 * targets * pooled * picks_t.shape[0],
            bytes_accessed=4 * pooled * targets,
            transcendentals=0,
        ),
    )(picks_t, queries, out_grad, weights)


def mirrored(number, count):
    out, size = 0, 1
    while size < count:
        out = out * 2 + number % 2
        number //= 2
        size *= 2
    return out


def attention_kernel(
    scale, raw, enc, weights, queries, out_grad, bias, query_heads, mixed_heads, back, grad_query, keep, send, grads
):
    pooled, width = raw.shape
    targets = queries.shape[0]
    raw_pool = raw[...]
    emb = dot(raw_pool, enc[...]).astype(BF16)
    key = dot(emb, weights[1]).astype(BF16)
    value = dot(emb, weights[2]).astype(BF16)
    key_t = dot_nt(weights[1].T, emb).astype(BF16)
    value_t = dot_nt(weights[2].T, emb).astype(BF16)
    pair_bias = jnp.concatenate([bias[...], bias[...]], axis=1)
    head_size = width // HEADS
    upper = iota((2 * head_size, targets), 0) < head_size
    mixed_parts, qproj_parts = [], []
    key_grad = jnp.zeros((pooled, width), F32)
    value_grad = jnp.zeros((pooled, width), F32)
    for pair in range(HEADS // 2):
        rows = slice(pair * 2 * targets, (pair + 1) * 2 * targets)
        query_pair = query_heads[rows, :]
        mixed_pair = mixed_heads[rows, :]
        scores = dot_nt(key, query_pair) + pair_bias
        raised = jnp.exp(scores - jnp.max(scores, axis=0, keepdims=True))
        attend = raised * (1.0 / jnp.sum(raised, axis=0, keepdims=True))
        attend_low = attend.astype(BF16)
        weighted = attend * dot_nt(value, mixed_pair)
        score_low = (weighted - attend * jnp.sum(weighted, axis=0, keepdims=True)).astype(BF16)
        value_grad = value_grad + dot(attend_low, mixed_pair)
        key_grad = key_grad + dot(score_low, query_pair)
        wide = slice(pair * 2 * head_size, (pair + 1) * 2 * head_size)
        mixed_both = dot(value_t[wide], attend_low)
        qproj_both = dot(key_t[wide], score_low)
        mixed_parts.append(jnp.where(upper, mixed_both[:, :targets], mixed_both[:, targets:]))
        qproj_parts.append(jnp.where(upper, qproj_both[:, :targets], qproj_both[:, targets:]))
    mixed_t = jnp.concatenate(mixed_parts, axis=0)
    qproj_t = jnp.concatenate(qproj_parts, axis=0)
    grad_qproj = (qproj_t * scale).T.astype(BF16)
    grad_query[...] = dot_nt(grad_qproj, weights[0]).astype(BF16)
    key_low = key_grad.astype(BF16)
    value_low = value_grad.astype(BF16)
    emb_grad = (dot_nt(key_low, weights[1]) + dot_nt(value_low, weights[2])).astype(BF16)
    grads[0:width, :] = dot_tn(queries[...], grad_qproj)
    grads[width : 2 * width, :] = dot_tn(emb, key_low)
    grads[2 * width : 3 * width, :] = dot_tn(emb, value_low)
    grads[3 * width : 4 * width, :] = dot(mixed_t.astype(BF16), out_grad[...])
    grads[4 * width : 5 * width, :] = dot_tn(raw_pool, emb_grad)
    back[...] = emb_grad
    core = lax.axis_index("clu") % 2
    pieces, _, part, _ = keep.shape
    for q in range(pieces):
        base = 2 * mirrored(q, pieces)
        for m in range(MATRICES):
            at = m * width + base * part
            kept = pl.ds(pl.multiple_of(at + core * part, part), part)
            given = pl.ds(pl.multiple_of(at + (1 - core) * part, part), part)
            keep[q, m] = grads[kept, :].astype(BF16)
            send[q, m] = grads[given, :].astype(BF16)


def attention(scale, owners, raw_pool, enc, weights, queries, out_grad, bias, query_heads, mixed_heads):
    pooled, width = raw_pool.shape
    half = jax.ShapeDtypeStruct((owners // 4, MATRICES, 2 * width // owners, width), BF16)
    return pl.pallas_call(
        functools.partial(attention_kernel, scale),
        out_shape=[
            jax.ShapeDtypeStruct((pooled, width), BF16),
            jax.ShapeDtypeStruct(queries.shape, BF16),
            half,
            half,
        ],
        scratch_shapes=[pltpu.VMEM((MATRICES * width, width), F32)],
        compiler_params=pltpu.CompilerParams(vmem_limit_bytes=VMEM_LIMIT),
    )(raw_pool, enc, weights, queries, out_grad, bias, query_heads, mixed_heads)


def add_low(a, b):
    return (a.astype(F32) + b.astype(F32)).astype(BF16)


def split_kernel(bit, keep, got, kept, given):
    side = lax.shift_right_logical(lax.axis_index("clu"), bit) & 1
    half = kept.shape[0]
    for i in range(half):
        own = side * half + i
        other = (1 - side) * half + i
        kept[i] = add_low(keep[own], got[own])
        given[i] = add_low(keep[other], got[other])


def split(bit, keep, got, flops):
    half = jax.ShapeDtypeStruct((keep.shape[0] // 2,) + keep.shape[1:], BF16)
    return pl.pallas_call(
        functools.partial(split_kernel, bit),
        out_shape=[half, half],
        compiler_params=SMALL,
        cost_estimate=pl.CostEstimate(flops=flops, bytes_accessed=4 * keep.size, transcendentals=0),
    )(keep, got)


def sum_kernel(a, b, out):
    out[...] = add_low(a[...], b[...])


def sum_rows(a, b):
    return pl.pallas_call(
        sum_kernel, out_shape=jax.ShapeDtypeStruct(a.shape, BF16), compiler_params=SMALL
    )(a, b)


def place_kernel(masks, *refs):
    *sources, attn, enc = refs
    _, matrices, part, _ = sources[0].shape
    place_of = lax.rem(lax.axis_index("clu"), enc.shape[0] // part)
    for source, flips in zip(sources, masks):
        for k, flip in enumerate(flips):
            rows = pl.ds(pl.multiple_of((place_of ^ flip) * part, part), part)
            for m in range(matrices - 1):
                attn[m, rows, :] = source[k, m].astype(F32)
            enc[rows, :] = source[k, matrices - 1].astype(F32)


def place(pieces):
    width = pieces[0][0].shape[3]
    return pl.pallas_call(
        functools.partial(place_kernel, [flips for _, flips in pieces]),
        out_shape=[
            jax.ShapeDtypeStruct((MATRICES - 1, width, width), F32),
            jax.ShapeDtypeStruct((width, width), F32),
        ],
        compiler_params=SMALL,
    )(*[piece for piece, _ in pieces])


def rows_kernel(counts, onehot_t, table, back, out, share, filled, sem):
    clusters = counts.shape[1]
    total = dot(onehot_t[...], back[...])
    share[...] = (total / column_of(counts[...].astype(F32))).astype(BF16)

    def block(k):
        rows = pl.ds(pl.multiple_of(k * 256, 256), 256)
        return pltpu.make_async_copy(filled.at[rows], out.at[rows], sem.at[k])

    def fill(k, carry):
        onehot = member_onehot(table, k * 2, clusters)
        rows = pl.ds(pl.multiple_of(k * 256, 256), 256)
        filled[rows, :] = dot_tn(onehot, share[...]).astype(BF16)
        block(k).start()
        return carry

    def finish(k, carry):
        block(k).wait()
        return carry

    blocks = out.shape[0] // 256
    lax.fori_loop(0, blocks, fill, 0, unroll=4)
    lax.fori_loop(0, blocks, finish, 0)


def member_grads(counts, onehot_t, table, back, rows):
    clusters = counts.shape[1]
    width = back.shape[1]
    return pl.pallas_call(
        rows_kernel,
        out_specs=pl.BlockSpec(memory_space=pltpu.HBM),
        out_shape=jax.ShapeDtypeStruct((rows, width), BF16),
        scratch_shapes=[
            pltpu.VMEM((clusters, width), BF16),
            pltpu.VMEM((rows, width), BF16),
            pltpu.SemaphoreType.DMA((rows // 256,)),
        ],
        compiler_params=pltpu.CompilerParams(vmem_limit_bytes=VMEM_LIMIT),
        cost_estimate=pl.CostEstimate(
            flops=2 * rows * clusters * width, bytes_accessed=2 * rows * width, transcendentals=0
        ),
    )(counts, onehot_t, table, back)


def swap(blocks):
    return lax.all_to_all(blocks, "clu", split_axis=0, concat_axis=0, tiled=True)


def local(raw_rows, enc_weight, counts, member_rows, pool, picks, queries, attn_weights, out_grad):
    rows, width = raw_rows.shape
    owners = lax.axis_size("clu")
    pooled = pool.shape[1]
    clusters = counts.shape[1]
    scale = (width // HEADS) ** -0.5
    bits = owners.bit_length() - 1

    def exchange(flip, block):
        return lax.ppermute(block, "clu", [(d, d ^ flip) for d in range(owners)])

    asked = pool.reshape(1, pooled // LANES, LANES)
    for bit in range(3, bits):
        asked = jnp.concatenate([asked, exchange(1 << bit, asked)])
    table = row_table(counts, member_rows)
    asked, table = lax.optimization_barrier((asked, table))
    asked = jnp.concatenate([asked] + [exchange(flip, asked) for flip in (2, 4, 6)])
    means = cluster_means(counts, table, raw_rows)
    asked, means = lax.optimization_barrier((asked, means))
    asked = jnp.concatenate([asked, exchange(1, asked)])
    onehot_t, sent = select_rows(asked, means, pooled)
    raw_pool = swap(sent.reshape(owners, pooled // owners, width)).reshape(pooled, width)
    bias, query_heads, mixed_heads = target_terms(
        scale, picks.T, queries, out_grad, attn_weights, pooled
    )
    back, grad_query, keep, given = attention(
        scale, owners, raw_pool, enc_weight, attn_weights, queries, out_grad, bias, query_heads, mixed_heads
    )
    keep, given = split(1, keep, exchange(1, given), keep.size)
    given, back = lax.optimization_barrier((given, back))
    got = exchange(2, given)
    back = swap(back.reshape(owners, pooled // owners, width)).reshape(pooled, width)
    keep, given = split(2, keep, got, WEIGHT)
    for bit in range(2, bits - 2):
        keep, given = split(bit + 1, keep, exchange(1 << bit, given), keep.size)
    own = sum_rows(keep, exchange(owners // 4, given))
    got = exchange(owners // 2, own)
    grad_rows = member_grads(counts, onehot_t, table, back, rows)
    got, grad_rows = lax.optimization_barrier((got, grad_rows))
    own = sum_rows(own, got)
    masks = [0]
    for bit in range(bits - 2, 2, -1):
        own = jnp.concatenate([own, exchange(1 << bit, own)])
        masks = masks + [mask ^ (1 << bit) for mask in masks]
    chip = jnp.concatenate([own] + [exchange(flip, own) for flip in (4, 2, 6)])
    masks = [mask ^ flip for flip in (0, 4, 2, 6) for mask in masks]
    beside = exchange(1, chip)
    grad_attn, grad_encoder = place([(chip, masks), (beside, [mask ^ 1 for mask in masks])])
    return grad_query, grad_rows, grad_attn, grad_encoder


def solution(mesh):
    split = P(("grp", "clu"), None)
    in_specs = (split, P(), split, split, split, split, split, P(), split)
    out_specs = (split, split, P("grp", None, None), P("grp", None))
    return jax.shard_map(local, mesh=mesh, in_specs=in_specs, out_specs=out_specs, check_vma=False)
```

```python
import functools

import jax
import jax.numpy as jnp
from jax import lax
from jax.experimental import pallas as pl
from jax.experimental.pallas import tpu as pltpu
from jax.sharding import PartitionSpec as P

HEADS = 4
MATRICES = 5
WEIGHT = 10**11
LANES = 128
F32 = jnp.float32
BF16 = jnp.bfloat16
VMEM_LIMIT = 32 * 1024 * 1024
MOST_VMEM = 51 * 1024 * 1024
SMALL = pltpu.CompilerParams(vmem_limit_bytes=8 * 1024 * 1024)


def dot(a, b):
    return jnp.dot(a, b, preferred_element_type=F32)


def dot_nt(a, b):
    return lax.dot_general(a, b, (((1,), (1,)), ((), ())), preferred_element_type=F32)


def dot_tn(a, b):
    return lax.dot_general(a, b, (((0,), (0,)), ((), ())), preferred_element_type=F32)


def iota(shape, dim):
    return lax.broadcasted_iota(jnp.int32, shape, dim)


def ones_where(cond):
    return jnp.where(cond, 1.0, 0.0).astype(BF16)


def column_of(row):
    n = row.shape[1]
    wide = jnp.where(iota((n, n), 0) == iota((n, n), 1), row, 0.0)
    return jnp.sum(wide, axis=1, keepdims=True)


def member_onehot(table_ref, at, clusters):
    sub = iota((clusters, LANES), 0).astype(F32)
    parts = [ones_where(table_ref[pl.ds(at + k, 1), :] == sub) for k in range(2)]
    return jnp.concatenate(parts, axis=1)


def running(rows, cols, strict):
    gap = iota((rows, cols), 1) - iota((rows, cols), 0)
    return ones_where(gap > 0 if strict else gap >= 0)


def position_clusters(counts_row, groups):
    clusters = counts_row.shape[1]
    padded = jnp.broadcast_to(counts_row.astype(F32), (16, clusters)).astype(BF16)
    ends = dot(padded, running(clusters, clusters, False))[0:1].astype(jnp.int32)
    high = ones_where(ends // LANES == iota((groups, clusters), 0))
    low = ones_where(ends % LANES == iota((LANES, clusters), 0))
    marks = dot_nt(high, low).astype(BF16)
    within = dot(marks, running(LANES, LANES, False))
    totals = jnp.sum(marks.astype(F32), axis=1, keepdims=True)
    wide = jnp.broadcast_to(totals, (groups, LANES)).astype(BF16)
    before = lax.dot_general(
        running(groups, groups, True), wide, (((0,), (0,)), ((), ())), preferred_element_type=F32
    )
    return within + before


def means_kernel(
    counts_h, members_h, raw_h, mean_out, table, counts_v, members, raw, small_sem, raw_sem
):
    clusters = counts_v.shape[1]
    groups = members.shape[0]
    parts = raw_sem.shape[0]
    part = raw.shape[0] // parts
    small = [
        pltpu.make_async_copy(counts_h, counts_v, small_sem.at[0]),
        pltpu.make_async_copy(members_h, members, small_sem.at[1]),
    ]
    large = [
        pltpu.make_async_copy(
            raw_h.at[pl.ds(k * part, part)], raw.at[pl.ds(k * part, part)], raw_sem.at[k]
        )
        for k in range(parts)
    ]
    for copy in small + large:
        copy.start()
    for copy in small:
        copy.wait()
    cluster = position_clusters(counts_v[...], groups)
    rows = members[...]
    high = rows // LANES
    low = rows % LANES
    total = jnp.zeros((groups, LANES), F32)
    high_iota = iota((groups, LANES), 0)
    low_iota = iota((LANES, LANES), 0)
    for k in range(0, groups, 2):
        a_parts, b_parts = [], []
        for m in (k, k + 1):
            a_parts.append(
                jnp.where(high[m : m + 1] == high_iota, cluster[m : m + 1], 0.0).astype(BF16)
            )
            b_parts.append(ones_where(low[m : m + 1] == low_iota))
        total = total + dot_nt(jnp.concatenate(a_parts, axis=1), jnp.concatenate(b_parts, axis=1))
    table[...] = total
    count_column = column_of(counts_v[...].astype(F32))
    sums = jnp.zeros((clusters, raw.shape[1]), F32)
    for p in range(parts):
        large[p].wait()
        for k in range(part // 256):
            at = p * part + k * 256
            onehot = member_onehot(table, at // LANES, clusters)
            sums = sums + dot(onehot, raw[at : at + 256, :])
    mean_out[...] = (sums / count_column).astype(BF16)


def cluster_means(counts, members, raw_rows):
    clusters = counts.shape[1]
    rows, width = raw_rows.shape
    groups = rows // LANES
    parts = 8
    return pl.pallas_call(
        means_kernel,
        in_specs=[pl.BlockSpec(memory_space=pltpu.HBM)] * 3,
        out_shape=[
            jax.ShapeDtypeStruct((clusters, width), BF16),
            jax.ShapeDtypeStruct((groups, LANES), F32),
        ],
        scratch_shapes=[
            pltpu.VMEM((1, clusters), jnp.int32),
            pltpu.VMEM((groups, LANES), jnp.int32),
            pltpu.VMEM((rows, width), BF16),
            pltpu.SemaphoreType.DMA((2,)),
            pltpu.SemaphoreType.DMA((parts,)),
        ],
        compiler_params=pltpu.CompilerParams(vmem_limit_bytes=MOST_VMEM),
        cost_estimate=pl.CostEstimate(
            flops=2 * rows * clusters * width, bytes_accessed=2 * rows * width, transcendentals=0
        ),
    )(counts, members.reshape(groups, LANES), raw_rows)


def select_kernel(got, means, onehot_t, keep, give):
    clusters = means.shape[0]
    chips, per_owner, _ = keep.shape
    me = lax.axis_index("clu")
    parity = me % 2
    half = LANES // 2
    wanted = lax.rem(got[...], clusters)
    turned = pltpu.roll(wanted, half, 1)
    first = jnp.where(parity == 0, wanted, turned)
    second = jnp.where(parity == 0, turned, wanted)
    left = iota((1, LANES), 1) < half
    for k in range(chips):
        row = jnp.where(left, first[2 * k : 2 * k + 1], second[2 * k + 1 : 2 * k + 2])
        onehot_t[:, k * LANES : (k + 1) * LANES] = ones_where(row == iota((clusters, LANES), 0))
    sent = dot_tn(onehot_t[...], means[...]).astype(BF16)
    for k in range(chips):
        place = lax.shift_right_logical(me, 1) ^ k
        even = sent[2 * k * per_owner : (2 * k + 1) * per_owner]
        odd = sent[(2 * k + 1) * per_owner : (2 * k + 2) * per_owner]
        keep[place] = jnp.where(parity == 0, even, odd)
        give[place] = jnp.where(parity == 0, odd, even)


def select_rows(got, means, pooled):
    clusters, width = means.shape
    chips = got.shape[0] // 2
    half = jax.ShapeDtypeStruct((chips, pooled // chips // 2, width), BF16)
    return pl.pallas_call(
        select_kernel,
        out_shape=[jax.ShapeDtypeStruct((clusters, pooled), BF16), half, half],
        compiler_params=pltpu.CompilerParams(vmem_limit_bytes=VMEM_LIMIT),
    )(got, means)


def pair_kernel(keep, got, *outs):
    parity = lax.axis_index("clu") % 2
    per_owner = keep.shape[1]
    for k, out in enumerate(outs):
        out[pl.ds(pl.multiple_of(parity * per_owner, per_owner), per_owner), :] = keep[k]
        out[pl.ds(pl.multiple_of((1 - parity) * per_owner, per_owner), per_owner), :] = got[k]


def pair_up(keep, got):
    chips, per_owner, width = keep.shape
    return pl.pallas_call(
        pair_kernel,
        out_shape=[jax.ShapeDtypeStruct((2 * per_owner, width), BF16)] * chips,
        compiler_params=SMALL,
    )(keep, got)


def spread_heads(rows):
    head = iota(rows.shape, 1) // (rows.shape[1] // HEADS)
    return jnp.concatenate([jnp.where(head == h, rows, 0.0) for h in range(HEADS)], axis=0).astype(
        BF16
    )


def targets_kernel(scale, picks, queries, out_grad, weights, bias, query_heads, mixed_heads):
    query_proj = dot(queries[...], weights[0]).astype(BF16)
    query_heads[...] = spread_heads(query_proj.astype(F32) * scale)
    grad_mixed = dot_nt(out_grad[...], weights[3]).astype(BF16)
    mixed_heads[...] = spread_heads(grad_mixed.astype(F32))
    count, targets = picks.shape
    block = 128

    def body(b, carry):
        at = pl.multiple_of(b * block, block)
        chip = lax.shift_right_logical(lax.axis_index("clu"), 1) ^ b
        slot = iota((block, targets), 0) + chip * block
        found = jnp.zeros((block, targets), F32)
        for i in range(count):
            found = jnp.where(picks[i : i + 1, :] == slot, 1.0, found)
        bias[pl.ds(at, block), :] = jnp.where(found > 0.5, 0.0, -1e30)
        return carry

    lax.fori_loop(0, bias.shape[0] // block, body, 0)


def target_terms(scale, picks_t, queries, out_grad, weights, pooled):
    targets, width = queries.shape
    return pl.pallas_call(
        functools.partial(targets_kernel, scale),
        out_shape=[
            jax.ShapeDtypeStruct((pooled, targets), F32),
            jax.ShapeDtypeStruct((HEADS * targets, width), BF16),
            jax.ShapeDtypeStruct((HEADS * targets, width), BF16),
        ],
        compiler_params=pltpu.CompilerParams(vmem_limit_bytes=VMEM_LIMIT),
        cost_estimate=pl.CostEstimate(
            flops=4 * targets * pooled * picks_t.shape[0],
            bytes_accessed=4 * pooled * targets,
            transcendentals=0,
        ),
    )(picks_t, queries, out_grad, weights)


def mirrored(number, count):
    out, size = 0, 1
    while size < count:
        out = out * 2 + number % 2
        number //= 2
        size *= 2
    return out


def attention_kernel(scale, chips, *refs):
    raws = refs[:chips]
    enc, weights, queries, out_grad, bias, query_heads, mixed_heads = refs[chips : chips + 7]
    back, grad_query, keep, send, grads = refs[chips + 7 :]
    per_chip, width = raws[0].shape
    targets = queries.shape[0]
    raw_pool = jnp.concatenate([raw[...] for raw in raws], axis=0)
    emb = dot(raw_pool, enc[...]).astype(BF16)
    key = dot(emb, weights[1]).astype(BF16)
    value = dot(emb, weights[2]).astype(BF16)
    key_t = dot_nt(weights[1].T, emb).astype(BF16)
    value_t = dot_nt(weights[2].T, emb).astype(BF16)
    pair_bias = jnp.concatenate([bias[...], bias[...]], axis=1)
    head_size = width // HEADS
    upper = iota((2 * head_size, targets), 0) < head_size
    mixed_parts, qproj_parts, key_parts, value_parts = [], [], [], []
    for pair in range(HEADS // 2):
        rows = slice(pair * 2 * targets, (pair + 1) * 2 * targets)
        wide = slice(pair * 2 * head_size, (pair + 1) * 2 * head_size)
        query_pair = query_heads[rows, wide]
        mixed_pair = mixed_heads[rows, wide]
        scores = dot_nt(key[:, wide], query_pair) + pair_bias
        raised = jnp.exp(scores - jnp.max(scores, axis=0, keepdims=True))
        attend = raised * (1.0 / jnp.sum(raised, axis=0, keepdims=True))
        attend_low = attend.astype(BF16)
        weighted = attend * dot_nt(value[:, wide], mixed_pair)
        score_low = (weighted - attend * jnp.sum(weighted, axis=0, keepdims=True)).astype(BF16)
        value_parts.append(dot(attend_low, mixed_pair).astype(BF16))
        key_parts.append(dot(score_low, query_pair).astype(BF16))
        mixed_both = dot(value_t[wide], attend_low)
        qproj_both = dot(key_t[wide], score_low)
        mixed_parts.append(jnp.where(upper, mixed_both[:, :targets], mixed_both[:, targets:]))
        qproj_parts.append(jnp.where(upper, qproj_both[:, :targets], qproj_both[:, targets:]))
    mixed_t = jnp.concatenate(mixed_parts, axis=0).astype(BF16)
    grad_qproj = (jnp.concatenate(qproj_parts, axis=0) * scale).T.astype(BF16)
    grad_query[...] = dot_nt(grad_qproj, weights[0]).astype(BF16)
    key_low = jnp.concatenate(key_parts, axis=1)
    value_low = jnp.concatenate(value_parts, axis=1)
    emb_grad = (dot_nt(key_low, weights[1]) + dot_nt(value_low, weights[2])).astype(BF16)
    both = dot_tn(emb, jnp.concatenate([key_low, value_low], axis=1))
    grads[0:width, :] = dot_tn(queries[...], grad_qproj).astype(BF16)
    grads[width : 2 * width, :] = both[:, :width].astype(BF16)
    grads[2 * width : 3 * width, :] = both[:, width:].astype(BF16)
    grads[3 * width : 4 * width, :] = dot(mixed_t, out_grad[...]).astype(BF16)
    grads[4 * width : 5 * width, :] = dot_tn(raw_pool, emb_grad).astype(BF16)
    me = lax.axis_index("clu")
    for k in range(chips):
        at = pl.multiple_of((lax.shift_right_logical(me, 1) ^ k) * per_chip, per_chip)
        back[pl.ds(at, per_chip), :] = emb_grad[k * per_chip : (k + 1) * per_chip]
    core = me % 2
    pieces, _, part, _ = keep.shape
    for q in range(pieces):
        base = 2 * mirrored(q, pieces)
        for m in range(MATRICES):
            at = m * width + base * part
            kept = pl.ds(pl.multiple_of(at + core * part, part), part)
            given = pl.ds(pl.multiple_of(at + (1 - core) * part, part), part)
            keep[q, m] = grads[kept, :]
            send[q, m] = grads[given, :]


def attention(scale, owners, raws, enc, weights, queries, out_grad, bias, query_heads, mixed_heads):
    pooled, width = bias.shape[0], enc.shape[0]
    half = jax.ShapeDtypeStruct((owners // 4, MATRICES, 2 * width // owners, width), BF16)
    return pl.pallas_call(
        functools.partial(attention_kernel, scale, len(raws)),
        out_shape=[
            jax.ShapeDtypeStruct((pooled, width), BF16),
            jax.ShapeDtypeStruct(queries.shape, BF16),
            half,
            half,
        ],
        scratch_shapes=[pltpu.VMEM((MATRICES * width, width), BF16)],
        compiler_params=pltpu.CompilerParams(vmem_limit_bytes=VMEM_LIMIT),
    )(*raws, enc, weights, queries, out_grad, bias, query_heads, mixed_heads)


def add_low(a, b):
    return (a.astype(F32) + b.astype(F32)).astype(BF16)


def split_kernel(bit, keep, got, kept, given):
    side = lax.shift_right_logical(lax.axis_index("clu"), bit) & 1
    half = kept.shape[0]
    for i in range(half):
        own = side * half + i
        other = (1 - side) * half + i
        kept[i] = add_low(keep[own], got[own])
        given[i] = add_low(keep[other], got[other])


def split(bit, keep, got, flops):
    half = jax.ShapeDtypeStruct((keep.shape[0] // 2,) + keep.shape[1:], BF16)
    return pl.pallas_call(
        functools.partial(split_kernel, bit),
        out_shape=[half, half],
        compiler_params=SMALL,
        cost_estimate=pl.CostEstimate(flops=flops, bytes_accessed=4 * keep.size, transcendentals=0),
    )(keep, got)


def sum_kernel(a, b, out):
    out[...] = add_low(a[...], b[...])


def sum_rows(a, b):
    return pl.pallas_call(
        sum_kernel, out_shape=jax.ShapeDtypeStruct(a.shape, BF16), compiler_params=SMALL
    )(a, b)


def place_kernel(masks, *refs):
    *sources, attn, enc = refs
    _, matrices, part, _ = sources[0].shape
    place_of = lax.rem(lax.axis_index("clu"), enc.shape[0] // part)
    for source, flips in zip(sources, masks):
        for k, flip in enumerate(flips):
            rows = pl.ds(pl.multiple_of((place_of ^ flip) * part, part), part)
            for m in range(matrices - 1):
                attn[m, rows, :] = source[k, m].astype(F32)
            enc[rows, :] = source[k, matrices - 1].astype(F32)


def place(pieces):
    width = pieces[0][0].shape[3]
    return pl.pallas_call(
        functools.partial(place_kernel, [flips for _, flips in pieces]),
        out_shape=[
            jax.ShapeDtypeStruct((MATRICES - 1, width, width), F32),
            jax.ShapeDtypeStruct((width, width), F32),
        ],
        compiler_params=SMALL,
    )(*[piece for piece, _ in pieces])


def rows_kernel(counts, onehot_t, table, back, out, share, filled, sem):
    clusters = counts.shape[1]
    total = dot(onehot_t[...], back[...])
    share[...] = (total / column_of(counts[...].astype(F32))).astype(BF16)

    def block(k):
        rows = pl.ds(pl.multiple_of(k * 256, 256), 256)
        return pltpu.make_async_copy(filled.at[rows], out.at[rows], sem.at[k])

    def fill(k, carry):
        onehot = member_onehot(table, k * 2, clusters)
        rows = pl.ds(pl.multiple_of(k * 256, 256), 256)
        filled[rows, :] = dot_tn(onehot, share[...]).astype(BF16)
        block(k).start()
        return carry

    def finish(k, carry):
        block(k).wait()
        return carry

    blocks = out.shape[0] // 256
    lax.fori_loop(0, blocks, fill, 0, unroll=4)
    lax.fori_loop(0, blocks, finish, 0)


def member_grads(counts, onehot_t, table, back, rows):
    clusters = counts.shape[1]
    width = back.shape[1]
    return pl.pallas_call(
        rows_kernel,
        out_specs=pl.BlockSpec(memory_space=pltpu.HBM),
        out_shape=jax.ShapeDtypeStruct((rows, width), BF16),
        scratch_shapes=[
            pltpu.VMEM((clusters, width), BF16),
            pltpu.VMEM((rows, width), BF16),
            pltpu.SemaphoreType.DMA((rows // 256,)),
        ],
        compiler_params=pltpu.CompilerParams(vmem_limit_bytes=VMEM_LIMIT),
        cost_estimate=pl.CostEstimate(
            flops=2 * rows * clusters * width, bytes_accessed=2 * rows * width, transcendentals=0
        ),
    )(counts, onehot_t, table, back)


def swap(blocks):
    return lax.all_to_all(blocks, "clu", split_axis=0, concat_axis=0, tiled=True)


def local(raw_rows, enc_weight, counts, member_rows, pool, picks, queries, attn_weights, out_grad):
    rows, width = raw_rows.shape
    owners = lax.axis_size("clu")
    pooled = pool.shape[1]
    clusters = counts.shape[1]
    scale = (width // HEADS) ** -0.5
    bits = owners.bit_length() - 1

    def exchange(flip, block):
        return lax.ppermute(block, "clu", [(d, d ^ flip) for d in range(owners)])

    pairs = pool.reshape(owners // 2, 1, 1, LANES)
    asking = jnp.broadcast_to(pairs, (owners // 2, 2, 1, LANES)).reshape(owners, 1, LANES)
    got = swap(asking).reshape(owners, LANES)
    means, table = cluster_means(counts, member_rows, raw_rows)
    onehot_t, keep, give = select_rows(got, means, pooled)
    paired = pair_up(keep, exchange(1, give))
    far_first = {k: exchange(2 * k, paired[k]) for k in range(owners // 2 - 1, 0, -1)}
    raws = [paired[0]] + [far_first[k] for k in range(1, owners // 2)]
    bias, query_heads, mixed_heads = target_terms(
        scale, picks.T, queries, out_grad, attn_weights, pooled
    )
    back, grad_query, keep, given = attention(
        scale, owners, raws, enc_weight, attn_weights, queries, out_grad, bias, query_heads, mixed_heads
    )
    keep, given = split(1, keep, exchange(1, given), keep.size)
    given, back = lax.optimization_barrier((given, back))
    got = exchange(2, given)
    back = swap(back.reshape(owners, pooled // owners, width)).reshape(pooled, width)
    keep, given = split(2, keep, got, WEIGHT)
    for bit in range(2, bits - 2):
        keep, given = split(bit + 1, keep, exchange(1 << bit, given), keep.size)
    own = sum_rows(keep, exchange(owners // 4, given))
    got = exchange(owners // 2, own)
    grad_rows = member_grads(counts, onehot_t, table, back, rows)
    got, grad_rows = lax.optimization_barrier((got, grad_rows))
    own = sum_rows(own, got)
    masks = [0]
    for bit in range(bits - 2, 2, -1):
        own = jnp.concatenate([own, exchange(1 << bit, own)])
        masks = masks + [mask ^ (1 << bit) for mask in masks]
    chip = jnp.concatenate([own] + [exchange(flip, own) for flip in (4, 2, 6)])
    masks = [mask ^ flip for flip in (0, 4, 2, 6) for mask in masks]
    beside = exchange(1, chip)
    grad_attn, grad_encoder = place([(chip, masks), (beside, [mask ^ 1 for mask in masks])])
    return grad_query, grad_rows, grad_attn, grad_encoder


def solution(mesh):
    split = P(("grp", "clu"), None)
    in_specs = (split, P(), split, split, split, split, split, P(), split)
    out_specs = (split, split, P("grp", None, None), P("grp", None))
    return jax.shard_map(local, mesh=mesh, in_specs=in_specs, out_specs=out_specs, check_vma=False)
```

```python
import functools

import jax
import jax.numpy as jnp
from jax import lax
from jax.experimental import pallas as pl
from jax.experimental.pallas import tpu as pltpu
from jax.sharding import PartitionSpec as P

HEADS = 4
MATRICES = 5
LANES = 128
F32 = jnp.float32
BF16 = jnp.bfloat16
VMEM_LIMIT = 32 * 1024 * 1024
MOST_VMEM = 51 * 1024 * 1024
SMALL = pltpu.CompilerParams(vmem_limit_bytes=8 * 1024 * 1024)


def dot(a, b):
    return jnp.dot(a, b, preferred_element_type=F32)


def dot_nt(a, b):
    return lax.dot_general(a, b, (((1,), (1,)), ((), ())), preferred_element_type=F32)


def dot_tn(a, b):
    return lax.dot_general(a, b, (((0,), (0,)), ((), ())), preferred_element_type=F32)


def iota(shape, dim):
    return lax.broadcasted_iota(jnp.int32, shape, dim)


def ones_where(cond):
    return jnp.where(cond, 1.0, 0.0).astype(BF16)


def column_of(row):
    n = row.shape[1]
    wide = jnp.where(iota((n, n), 0) == iota((n, n), 1), row, 0.0)
    return jnp.sum(wide, axis=1, keepdims=True)


def member_onehot(table_ref, at, clusters):
    sub = iota((clusters, LANES), 0).astype(F32)
    parts = [ones_where(table_ref[pl.ds(at + k, 1), :] == sub) for k in range(2)]
    return jnp.concatenate(parts, axis=1)


def running(rows, cols, strict):
    gap = iota((rows, cols), 1) - iota((rows, cols), 0)
    return ones_where(gap > 0 if strict else gap >= 0)


def position_clusters(counts_row, groups):
    clusters = counts_row.shape[1]
    padded = jnp.broadcast_to(counts_row.astype(F32), (16, clusters)).astype(BF16)
    ends = dot(padded, running(clusters, clusters, False))[0:1].astype(jnp.int32)
    high = ones_where(ends // LANES == iota((groups, clusters), 0))
    low = ones_where(ends % LANES == iota((LANES, clusters), 0))
    marks = dot_nt(high, low).astype(BF16)
    within = dot(marks, running(LANES, LANES, False))
    totals = jnp.sum(marks.astype(F32), axis=1, keepdims=True)
    wide = jnp.broadcast_to(totals, (groups, LANES)).astype(BF16)
    before = lax.dot_general(
        running(groups, groups, True), wide, (((0,), (0,)), ((), ())), preferred_element_type=F32
    )
    return within + before


def means_kernel(
    counts_h, members_h, raw_h, mean_out, table, counts_v, members, raw, small_sem, raw_sem
):
    clusters = counts_v.shape[1]
    groups = members.shape[0]
    parts = raw_sem.shape[0]
    part = raw.shape[0] // parts
    small = [
        pltpu.make_async_copy(counts_h, counts_v, small_sem.at[0]),
        pltpu.make_async_copy(members_h, members, small_sem.at[1]),
    ]
    large = [
        pltpu.make_async_copy(
            raw_h.at[pl.ds(k * part, part)], raw.at[pl.ds(k * part, part)], raw_sem.at[k]
        )
        for k in range(parts)
    ]
    for copy in small + large:
        copy.start()
    for copy in small:
        copy.wait()
    cluster = position_clusters(counts_v[...], groups)
    rows = members[...]
    high = rows // LANES
    low = rows % LANES
    total = jnp.zeros((groups, LANES), F32)
    high_iota = iota((groups, LANES), 0)
    low_iota = iota((LANES, LANES), 0)
    for k in range(0, groups, 2):
        a_parts, b_parts = [], []
        for m in (k, k + 1):
            a_parts.append(
                jnp.where(high[m : m + 1] == high_iota, cluster[m : m + 1], 0.0).astype(BF16)
            )
            b_parts.append(ones_where(low[m : m + 1] == low_iota))
        total = total + dot_nt(jnp.concatenate(a_parts, axis=1), jnp.concatenate(b_parts, axis=1))
    table[...] = total
    count_column = column_of(counts_v[...].astype(F32))
    sums = jnp.zeros((clusters, raw.shape[1]), F32)
    for p in range(parts):
        large[p].wait()
        for k in range(part // 256):
            at = p * part + k * 256
            onehot = member_onehot(table, at // LANES, clusters)
            sums = sums + dot(onehot, raw[at : at + 256, :])
    mean_out[...] = (sums / count_column).astype(BF16)


def cluster_means(counts, members, raw_rows):
    clusters = counts.shape[1]
    rows, width = raw_rows.shape
    groups = rows // LANES
    parts = 8
    return pl.pallas_call(
        means_kernel,
        in_specs=[pl.BlockSpec(memory_space=pltpu.HBM)] * 3,
        out_shape=[
            jax.ShapeDtypeStruct((clusters, width), BF16),
            jax.ShapeDtypeStruct((groups, LANES), F32),
        ],
        scratch_shapes=[
            pltpu.VMEM((1, clusters), jnp.int32),
            pltpu.VMEM((groups, LANES), jnp.int32),
            pltpu.VMEM((rows, width), BF16),
            pltpu.SemaphoreType.DMA((2,)),
            pltpu.SemaphoreType.DMA((parts,)),
        ],
        compiler_params=pltpu.CompilerParams(vmem_limit_bytes=MOST_VMEM),
        cost_estimate=pl.CostEstimate(
            flops=2 * rows * clusters * width, bytes_accessed=2 * rows * width, transcendentals=0
        ),
    )(counts, members.reshape(groups, LANES), raw_rows)


def select_kernel(got, means, onehot_t, keep, give):
    clusters = means.shape[0]
    chips = keep.shape[0]
    me = lax.axis_index("clu")
    parity = me % 2
    half = LANES // 2
    wanted = lax.rem(got[...], clusters)
    turned = pltpu.roll(wanted, half, 1)
    first = jnp.where(parity == 0, wanted, turned)
    second = jnp.where(parity == 0, turned, wanted)
    left = iota((1, LANES), 1) < half
    for k in range(chips):
        row = jnp.where(left, first[2 * k : 2 * k + 1], second[2 * k + 1 : 2 * k + 2])
        at = pl.multiple_of((lax.shift_right_logical(me, 1) ^ k) * LANES, LANES)
        onehot_t[:, pl.ds(at, LANES)] = ones_where(row == iota((clusters, LANES), 0))
    sort_rows(parity, dot_tn(onehot_t[...], means[...]).astype(BF16), keep, give)


def sort_rows(parity, rows, keep, give):
    chips, part, _ = keep.shape
    for k in range(chips):
        even = rows[2 * k * part : (2 * k + 1) * part]
        odd = rows[(2 * k + 1) * part : (2 * k + 2) * part]
        keep[k] = jnp.where(parity == 0, even, odd)
        give[k] = jnp.where(parity == 0, odd, even)


def select_rows(got, means, pooled):
    clusters, width = means.shape
    chips = got.shape[0] // 2
    half = jax.ShapeDtypeStruct((chips, pooled // chips // 2, width), BF16)
    return pl.pallas_call(
        select_kernel,
        out_shape=[jax.ShapeDtypeStruct((clusters, pooled), BF16), half, half],
        compiler_params=pltpu.CompilerParams(vmem_limit_bytes=VMEM_LIMIT),
    )(got, means)


def pair_kernel(keep, got, *outs):
    parity = lax.axis_index("clu") % 2
    per_owner = keep.shape[1]
    for k, out in enumerate(outs):
        out[pl.ds(pl.multiple_of(parity * per_owner, per_owner), per_owner), :] = keep[k]
        out[pl.ds(pl.multiple_of((1 - parity) * per_owner, per_owner), per_owner), :] = got[k]


def pair_up(keep, got):
    chips, per_owner, width = keep.shape
    return pl.pallas_call(
        pair_kernel,
        out_shape=[jax.ShapeDtypeStruct((2 * per_owner, width), BF16)] * chips,
        compiler_params=SMALL,
    )(keep, got)


def spread_heads(rows):
    head = iota(rows.shape, 1) // (rows.shape[1] // HEADS)
    return jnp.concatenate([jnp.where(head == h, rows, 0.0) for h in range(HEADS)], axis=0).astype(
        BF16
    )


def targets_kernel(scale, picks, queries, out_grad, weights, bias, query_heads, mixed_heads):
    query_proj = dot(queries[...], weights[0]).astype(BF16)
    query_heads[...] = spread_heads(query_proj.astype(F32) * scale)
    grad_mixed = dot_nt(out_grad[...], weights[3]).astype(BF16)
    mixed_heads[...] = spread_heads(grad_mixed.astype(F32))
    count, targets = picks.shape
    block = 128

    def body(b, carry):
        at = pl.multiple_of(b * block, block)
        chip = lax.shift_right_logical(lax.axis_index("clu"), 1) ^ b
        slot = iota((block, targets), 0) + chip * block
        found = jnp.zeros((block, targets), F32)
        for i in range(count):
            found = jnp.where(picks[i : i + 1, :] == slot, 1.0, found)
        bias[pl.ds(at, block), :] = jnp.where(found > 0.5, 0.0, -1e30)
        return carry

    lax.fori_loop(0, bias.shape[0] // block, body, 0)


def target_terms(scale, picks_t, queries, out_grad, weights, pooled):
    targets, width = queries.shape
    return pl.pallas_call(
        functools.partial(targets_kernel, scale),
        out_shape=[
            jax.ShapeDtypeStruct((pooled, targets), F32),
            jax.ShapeDtypeStruct((HEADS * targets, width), BF16),
            jax.ShapeDtypeStruct((HEADS * targets, width), BF16),
        ],
        compiler_params=pltpu.CompilerParams(vmem_limit_bytes=VMEM_LIMIT),
        cost_estimate=pl.CostEstimate(
            flops=4 * targets * pooled * picks_t.shape[0],
            bytes_accessed=4 * pooled * targets,
            transcendentals=0,
        ),
    )(picks_t, queries, out_grad, weights)


def mirrored(number, count):
    out, size = 0, 1
    while size < count:
        out = out * 2 + number % 2
        number //= 2
        size *= 2
    return out


def attention_kernel(scale, chips, *refs):
    raws = refs[:chips]
    enc, weights, queries, out_grad, bias, query_heads, mixed_heads = refs[chips : chips + 7]
    keep_rows, send_rows, grad_query, keep, send, grads = refs[chips + 7 :]
    width = enc.shape[0]
    targets = queries.shape[0]
    raw_pool = jnp.concatenate([raw[...] for raw in raws], axis=0)
    emb = dot(raw_pool, enc[...]).astype(BF16)
    key = dot(emb, weights[1]).astype(BF16)
    value = dot(emb, weights[2]).astype(BF16)
    key_t = dot_nt(weights[1].T, emb).astype(BF16)
    value_t = dot_nt(weights[2].T, emb).astype(BF16)
    pair_bias = jnp.concatenate([bias[...], bias[...]], axis=1)
    head_size = width // HEADS
    upper = iota((2 * head_size, targets), 0) < head_size
    mixed_parts, qproj_parts, key_parts, value_parts = [], [], [], []
    for pair in range(HEADS // 2):
        rows = slice(pair * 2 * targets, (pair + 1) * 2 * targets)
        wide = slice(pair * 2 * head_size, (pair + 1) * 2 * head_size)
        query_pair = query_heads[rows, wide]
        mixed_pair = mixed_heads[rows, wide]
        scores = dot_nt(key[:, wide], query_pair) + pair_bias
        raised = jnp.exp(scores - jnp.max(scores, axis=0, keepdims=True))
        attend = raised * (1.0 / jnp.sum(raised, axis=0, keepdims=True))
        attend_low = attend.astype(BF16)
        weighted = attend * dot_nt(value[:, wide], mixed_pair)
        score_low = (weighted - attend * jnp.sum(weighted, axis=0, keepdims=True)).astype(BF16)
        value_parts.append(dot(attend_low, mixed_pair).astype(BF16))
        key_parts.append(dot(score_low, query_pair).astype(BF16))
        mixed_both = dot(value_t[wide], attend_low)
        qproj_both = dot(key_t[wide], score_low)
        mixed_parts.append(jnp.where(upper, mixed_both[:, :targets], mixed_both[:, targets:]))
        qproj_parts.append(jnp.where(upper, qproj_both[:, :targets], qproj_both[:, targets:]))
    mixed_t = jnp.concatenate(mixed_parts, axis=0).astype(BF16)
    grad_qproj = (jnp.concatenate(qproj_parts, axis=0) * scale).T.astype(BF16)
    grad_query[...] = dot_nt(grad_qproj, weights[0]).astype(BF16)
    key_low = jnp.concatenate(key_parts, axis=1)
    value_low = jnp.concatenate(value_parts, axis=1)
    emb_grad = (dot_nt(key_low, weights[1]) + dot_nt(value_low, weights[2])).astype(BF16)
    both = dot_tn(emb, jnp.concatenate([key_low, value_low], axis=1))
    grads[0:width, :] = dot_tn(queries[...], grad_qproj).astype(BF16)
    grads[width : 2 * width, :] = both[:, :width].astype(BF16)
    grads[2 * width : 3 * width, :] = both[:, width:].astype(BF16)
    grads[3 * width : 4 * width, :] = dot(mixed_t, out_grad[...]).astype(BF16)
    grads[4 * width : 5 * width, :] = dot_tn(raw_pool, emb_grad).astype(BF16)
    core = lax.axis_index("clu") % 2
    sort_rows(core, emb_grad, keep_rows, send_rows)
    pieces, _, part, _ = keep.shape
    for q in range(pieces):
        base = 2 * mirrored(q, pieces)
        for m in range(MATRICES):
            at = m * width + base * part
            kept = pl.ds(pl.multiple_of(at + core * part, part), part)
            given = pl.ds(pl.multiple_of(at + (1 - core) * part, part), part)
            keep[q, m] = grads[kept, :]
            send[q, m] = grads[given, :]


def attention(scale, owners, raws, enc, weights, queries, out_grad, bias, query_heads, mixed_heads):
    width = enc.shape[0]
    half = jax.ShapeDtypeStruct((owners // 4, MATRICES, 2 * width // owners, width), BF16)
    rows = jax.ShapeDtypeStruct((len(raws), raws[0].shape[0] // 2, width), BF16)
    return pl.pallas_call(
        functools.partial(attention_kernel, scale, len(raws)),
        out_shape=[
            rows,
            rows,
            jax.ShapeDtypeStruct(queries.shape, BF16),
            half,
            half,
        ],
        scratch_shapes=[pltpu.VMEM((MATRICES * width, width), BF16)],
        compiler_params=pltpu.CompilerParams(vmem_limit_bytes=VMEM_LIMIT),
    )(*raws, enc, weights, queries, out_grad, bias, query_heads, mixed_heads)


def add_low(a, b):
    return (a.astype(F32) + b.astype(F32)).astype(BF16)


def split_kernel(bit, keep, got, kept, given):
    side = lax.shift_right_logical(lax.axis_index("clu"), bit) & 1
    half = kept.shape[0]
    for i in range(half):
        own = side * half + i
        other = (1 - side) * half + i
        kept[i] = add_low(keep[own], got[own])
        given[i] = add_low(keep[other], got[other])


def split(bit, keep, got):
    half = jax.ShapeDtypeStruct((keep.shape[0] // 2,) + keep.shape[1:], BF16)
    return pl.pallas_call(
        functools.partial(split_kernel, bit),
        out_shape=[half, half],
        compiler_params=SMALL,
    )(keep, got)


def sum_kernel(a, b, out):
    out[...] = add_low(a[...], b[...])


def sum_rows(a, b):
    return pl.pallas_call(
        sum_kernel, out_shape=jax.ShapeDtypeStruct(a.shape, BF16), compiler_params=SMALL
    )(a, b)


def place_kernel(masks, *refs):
    *sources, attn, enc = refs
    _, matrices, part, _ = sources[0].shape
    place_of = lax.rem(lax.axis_index("clu"), enc.shape[0] // part)
    for source, flips in zip(sources, masks):
        for k, flip in enumerate(flips):
            rows = pl.ds(pl.multiple_of((place_of ^ flip) * part, part), part)
            for m in range(matrices - 1):
                attn[m, rows, :] = source[k, m].astype(F32)
            enc[rows, :] = source[k, matrices - 1].astype(F32)


def place(pieces):
    width = pieces[0][0].shape[3]
    return pl.pallas_call(
        functools.partial(place_kernel, [flips for _, flips in pieces]),
        out_shape=[
            jax.ShapeDtypeStruct((MATRICES - 1, width, width), F32),
            jax.ShapeDtypeStruct((width, width), F32),
        ],
        compiler_params=SMALL,
    )(*[piece for piece, _ in pieces])


def rows_kernel(counts, onehot_t, table, *refs):
    *backs, out, share, filled, sem = refs
    clusters = counts.shape[1]
    total = dot(onehot_t[...], jnp.concatenate([back[...] for back in backs], axis=0))
    share[...] = (total / column_of(counts[...].astype(F32))).astype(BF16)

    def block(k):
        rows = pl.ds(pl.multiple_of(k * 256, 256), 256)
        return pltpu.make_async_copy(filled.at[rows], out.at[rows], sem.at[k])

    def fill(k, carry):
        onehot = member_onehot(table, k * 2, clusters)
        rows = pl.ds(pl.multiple_of(k * 256, 256), 256)
        filled[rows, :] = dot_tn(onehot, share[...]).astype(BF16)
        block(k).start()
        return carry

    def finish(k, carry):
        block(k).wait()
        return carry

    blocks = out.shape[0] // 256
    lax.fori_loop(0, blocks, fill, 0, unroll=4)
    lax.fori_loop(0, blocks, finish, 0)


def member_grads(counts, onehot_t, table, backs, rows):
    clusters = counts.shape[1]
    width = backs[0].shape[1]
    return pl.pallas_call(
        rows_kernel,
        out_specs=pl.BlockSpec(memory_space=pltpu.HBM),
        out_shape=jax.ShapeDtypeStruct((rows, width), BF16),
        scratch_shapes=[
            pltpu.VMEM((clusters, width), BF16),
            pltpu.VMEM((rows, width), BF16),
            pltpu.SemaphoreType.DMA((rows // 256,)),
        ],
        compiler_params=pltpu.CompilerParams(vmem_limit_bytes=VMEM_LIMIT),
        cost_estimate=pl.CostEstimate(
            flops=2 * rows * clusters * width, bytes_accessed=2 * rows * width, transcendentals=0
        ),
    )(counts, onehot_t, table, *backs)


def swap(blocks):
    return lax.all_to_all(blocks, "clu", split_axis=0, concat_axis=0, tiled=True)


def local(raw_rows, enc_weight, counts, member_rows, pool, picks, queries, attn_weights, out_grad):
    rows, width = raw_rows.shape
    owners = lax.axis_size("clu")
    pooled = pool.shape[1]
    clusters = counts.shape[1]
    scale = (width // HEADS) ** -0.5
    bits = owners.bit_length() - 1

    def exchange(flip, block):
        return lax.ppermute(block, "clu", [(d, d ^ flip) for d in range(owners)])

    pairs = pool.reshape(owners // 2, 1, 1, LANES)
    asking = jnp.broadcast_to(pairs, (owners // 2, 2, 1, LANES)).reshape(owners, 1, LANES)
    got = swap(asking).reshape(owners, LANES)
    means, table = cluster_means(counts, member_rows, raw_rows)
    onehot_t, keep, give = select_rows(got, means, pooled)
    paired = pair_up(keep, exchange(1, give))
    far_first = {k: exchange(2 * k, paired[k]) for k in range(owners // 2 - 1, 0, -1)}
    raws = [paired[0]] + [far_first[k] for k in range(1, owners // 2)]
    bias, query_heads, mixed_heads = target_terms(
        scale, picks.T, queries, out_grad, attn_weights, pooled
    )
    keep_rows, give_rows, grad_query, keep, given = attention(
        scale, owners, raws, enc_weight, attn_weights, queries, out_grad, bias, query_heads, mixed_heads
    )
    got, got_rows = exchange(1, given), exchange(1, give_rows)
    keep, given = split(1, keep, got)
    paired = pair_up(keep_rows, got_rows)
    backs = {0: paired[0]}
    far_first = list(range(owners // 2 - 1, 0, -1))
    batch = -(-len(far_first) // (bits - 1))

    def beside_rows(flip, block, kept):
        now = far_first[:batch]
        del far_first[:batch]
        block, *rows_now = lax.optimization_barrier((block, *[paired[k] for k in now]))
        got = exchange(flip, block)
        passed = [exchange(2 * k, rows_k) for k, rows_k in zip(now, rows_now)]
        got, kept, *passed = lax.optimization_barrier((got, kept, *passed))
        backs.update(zip(now, passed))
        return got, kept

    for bit in range(1, bits - 2):
        got, keep = beside_rows(1 << bit, given, keep)
        keep, given = split(bit + 1, keep, got)
    got, keep = beside_rows(owners // 4, given, keep)
    own = sum_rows(keep, got)
    got, own = beside_rows(owners // 2, own, own)
    own = sum_rows(own, got)
    masks = [0]
    for bit in range(bits - 2, 2, -1):
        own = jnp.concatenate([own, exchange(1 << bit, own)])
        masks = masks + [mask ^ (1 << bit) for mask in masks]
    passed = [exchange(flip, own) for flip in (4, 2, 6)]
    in_order = [backs[k] for k in range(owners // 2)]
    grad_rows = member_grads(counts, onehot_t, table, in_order, rows)
    passed, grad_rows = lax.optimization_barrier((passed, grad_rows))
    chip = jnp.concatenate([own] + passed)
    masks = [mask ^ flip for flip in (0, 4, 2, 6) for mask in masks]
    beside = exchange(1, chip)
    grad_attn, grad_encoder = place([(chip, masks), (beside, [mask ^ 1 for mask in masks])])
    return grad_query, grad_rows, grad_attn, grad_encoder


def solution(mesh):
    split = P(("grp", "clu"), None)
    in_specs = (split, P(), split, split, split, split, split, P(), split)
    out_specs = (split, split, P("grp", None, None), P("grp", None))
    return jax.shard_map(local, mesh=mesh, in_specs=in_specs, out_specs=out_specs, check_vma=False)
```

```python
import functools

import jax
import jax.numpy as jnp
from jax import lax
from jax.experimental import pallas as pl
from jax.experimental.pallas import tpu as pltpu
from jax.sharding import PartitionSpec as P

HEADS = 4
MATRICES = 5
WEIGHT = 10**11
LANES = 128
F32 = jnp.float32
BF16 = jnp.bfloat16
VMEM_LIMIT = 32 * 1024 * 1024
MOST_VMEM = 51 * 1024 * 1024
SMALL = pltpu.CompilerParams(vmem_limit_bytes=8 * 1024 * 1024)


def dot(a, b):
    return jnp.dot(a, b, preferred_element_type=F32)


def dot_nt(a, b):
    return lax.dot_general(a, b, (((1,), (1,)), ((), ())), preferred_element_type=F32)


def dot_tn(a, b):
    return lax.dot_general(a, b, (((0,), (0,)), ((), ())), preferred_element_type=F32)


def iota(shape, dim):
    return lax.broadcasted_iota(jnp.int32, shape, dim)


def ones_where(cond):
    return jnp.where(cond, 1.0, 0.0).astype(BF16)


def column_of(row):
    n = row.shape[1]
    wide = jnp.where(iota((n, n), 0) == iota((n, n), 1), row, 0.0)
    return jnp.sum(wide, axis=1, keepdims=True)


def member_onehot(table_ref, at, clusters):
    sub = iota((clusters, LANES), 0).astype(F32)
    parts = [ones_where(table_ref[pl.ds(at + k, 1), :] == sub) for k in range(2)]
    return jnp.concatenate(parts, axis=1)


def running(rows, cols, strict):
    gap = iota((rows, cols), 1) - iota((rows, cols), 0)
    return ones_where(gap > 0 if strict else gap >= 0)


def position_clusters(counts_row, groups):
    clusters = counts_row.shape[1]
    padded = jnp.broadcast_to(counts_row.astype(F32), (16, clusters)).astype(BF16)
    ends = dot(padded, running(clusters, clusters, False))[0:1].astype(jnp.int32)
    high = ones_where(ends // LANES == iota((groups, clusters), 0))
    low = ones_where(ends % LANES == iota((LANES, clusters), 0))
    marks = dot_nt(high, low).astype(BF16)
    within = dot(marks, running(LANES, LANES, False))
    totals = jnp.sum(marks.astype(F32), axis=1, keepdims=True)
    wide = jnp.broadcast_to(totals, (groups, LANES)).astype(BF16)
    before = lax.dot_general(
        running(groups, groups, True), wide, (((0,), (0,)), ((), ())), preferred_element_type=F32
    )
    return within + before


def means_kernel(
    counts_h, members_h, raw_h, mean_out, table, counts_v, members, raw, small_sem, raw_sem
):
    clusters = counts_v.shape[1]
    groups = members.shape[0]
    parts = raw_sem.shape[0]
    part = raw.shape[0] // parts
    small = [
        pltpu.make_async_copy(counts_h, counts_v, small_sem.at[0]),
        pltpu.make_async_copy(members_h, members, small_sem.at[1]),
    ]
    large = [
        pltpu.make_async_copy(
            raw_h.at[pl.ds(k * part, part)], raw.at[pl.ds(k * part, part)], raw_sem.at[k]
        )
        for k in range(parts)
    ]
    for copy in small + large:
        copy.start()
    for copy in small:
        copy.wait()
    cluster = position_clusters(counts_v[...], groups)
    rows = members[...]
    high = rows // LANES
    low = rows % LANES
    total = jnp.zeros((groups, LANES), F32)
    high_iota = iota((groups, LANES), 0)
    low_iota = iota((LANES, LANES), 0)
    for k in range(0, groups, 2):
        a_parts, b_parts = [], []
        for m in (k, k + 1):
            a_parts.append(
                jnp.where(high[m : m + 1] == high_iota, cluster[m : m + 1], 0.0).astype(BF16)
            )
            b_parts.append(ones_where(low[m : m + 1] == low_iota))
        total = total + dot_nt(jnp.concatenate(a_parts, axis=1), jnp.concatenate(b_parts, axis=1))
    table[...] = total
    count_column = column_of(counts_v[...].astype(F32))
    sums = jnp.zeros((clusters, raw.shape[1]), F32)
    for p in range(parts):
        large[p].wait()
        for k in range(part // 256):
            at = p * part + k * 256
            onehot = member_onehot(table, at // LANES, clusters)
            sums = sums + dot(onehot, raw[at : at + 256, :])
    mean_out[...] = (sums / count_column).astype(BF16)


def cluster_means(counts, members, raw_rows):
    clusters = counts.shape[1]
    rows, width = raw_rows.shape
    groups = rows // LANES
    parts = 8
    return pl.pallas_call(
        means_kernel,
        in_specs=[pl.BlockSpec(memory_space=pltpu.HBM)] * 3,
        out_shape=[
            jax.ShapeDtypeStruct((clusters, width), BF16),
            jax.ShapeDtypeStruct((groups, LANES), F32),
        ],
        scratch_shapes=[
            pltpu.VMEM((1, clusters), jnp.int32),
            pltpu.VMEM((groups, LANES), jnp.int32),
            pltpu.VMEM((rows, width), BF16),
            pltpu.SemaphoreType.DMA((2,)),
            pltpu.SemaphoreType.DMA((parts,)),
        ],
        compiler_params=pltpu.CompilerParams(vmem_limit_bytes=MOST_VMEM),
        cost_estimate=pl.CostEstimate(
            flops=2 * rows * clusters * width, bytes_accessed=2 * rows * width, transcendentals=0
        ),
    )(counts, members.reshape(groups, LANES), raw_rows)


def select_kernel(got, beside, means, onehot_t, keep, give):
    clusters = means.shape[0]
    parity = lax.axis_index("clu") % 2
    half = LANES // 2
    even = jnp.where(parity == 0, got[...], beside[...])
    odd = jnp.where(parity == 0, beside[...], got[...])
    first = jnp.where(parity == 0, even, pltpu.roll(even, half, 1))
    second = jnp.where(parity == 0, pltpu.roll(odd, half, 1), odd)
    wanted = jnp.where(iota(got.shape, 1) < half, first, second)
    wanted = lax.rem(wanted, clusters)
    for k in range(got.shape[0]):
        onehot_t[:, k * LANES : (k + 1) * LANES] = ones_where(
            wanted[k : k + 1] == iota((clusters, LANES), 0)
        )
    sort_rows(parity, dot_tn(onehot_t[...], means[...]).astype(BF16), keep, give)


def sort_rows(parity, rows, keep, give):
    chips, part, _ = keep.shape
    for k in range(chips):
        even = rows[2 * k * part : (2 * k + 1) * part]
        odd = rows[(2 * k + 1) * part : (2 * k + 2) * part]
        keep[k] = jnp.where(parity == 0, even, odd)
        give[k] = jnp.where(parity == 0, odd, even)


def select_rows(got, beside, means, pooled):
    clusters, width = means.shape
    chips = got.shape[0]
    half = jax.ShapeDtypeStruct((chips, pooled // chips // 2, width), BF16)
    return pl.pallas_call(
        select_kernel,
        out_shape=[jax.ShapeDtypeStruct((clusters, pooled), BF16), half, half],
        compiler_params=pltpu.CompilerParams(vmem_limit_bytes=VMEM_LIMIT),
    )(got, beside, means)


def pair_kernel(keep, got, out):
    parity = lax.axis_index("clu") % 2
    chips, part, _ = keep.shape
    own = pl.ds(pl.multiple_of(parity * part, part), part)
    other = pl.ds(pl.multiple_of((1 - parity) * part, part), part)
    for k in range(chips):
        out[k, own, :] = keep[k]
        out[k, other, :] = got[k]


def pair_up(keep, got):
    chips, part, width = keep.shape
    return pl.pallas_call(
        pair_kernel,
        out_shape=jax.ShapeDtypeStruct((chips, 2 * part, width), BF16),
        compiler_params=SMALL,
    )(keep, got)


def spread_heads(rows):
    head = iota(rows.shape, 1) // (rows.shape[1] // HEADS)
    return jnp.concatenate([jnp.where(head == h, rows, 0.0) for h in range(HEADS)], axis=0).astype(
        BF16
    )


def targets_kernel(scale, picks, queries, out_grad, weights, bias, query_heads, mixed_heads):
    query_proj = dot(queries[...], weights[0]).astype(BF16)
    query_heads[...] = spread_heads(query_proj.astype(F32) * scale)
    grad_mixed = dot_nt(out_grad[...], weights[3]).astype(BF16)
    mixed_heads[...] = spread_heads(grad_mixed.astype(F32))
    count, targets = picks.shape
    block = 128

    def body(b, carry):
        at = pl.multiple_of(b * block, block)
        slot = iota((block, targets), 0) + at
        found = jnp.zeros((block, targets), F32)
        for i in range(count):
            found = jnp.where(picks[i : i + 1, :] == slot, 1.0, found)
        bias[pl.ds(at, block), :] = jnp.where(found > 0.5, 0.0, -1e30)
        return carry

    lax.fori_loop(0, bias.shape[0] // block, body, 0)


def target_terms(scale, picks_t, queries, out_grad, weights, pooled):
    targets, width = queries.shape
    return pl.pallas_call(
        functools.partial(targets_kernel, scale),
        out_shape=[
            jax.ShapeDtypeStruct((pooled, targets), F32),
            jax.ShapeDtypeStruct((HEADS * targets, width), BF16),
            jax.ShapeDtypeStruct((HEADS * targets, width), BF16),
        ],
        compiler_params=pltpu.CompilerParams(vmem_limit_bytes=VMEM_LIMIT),
        cost_estimate=pl.CostEstimate(
            flops=4 * targets * pooled * picks_t.shape[0],
            bytes_accessed=4 * pooled * targets,
            transcendentals=0,
        ),
    )(picks_t, queries, out_grad, weights)


def mirrored(number, count):
    out, size = 0, 1
    while size < count:
        out = out * 2 + number % 2
        number //= 2
        size *= 2
    return out


def attention_kernel(
    scale, raw, enc, weights, queries, out_grad, bias, query_heads, mixed_heads,
    keep_rows, give_rows, grad_query, keep, send, grads,
):
    width = enc.shape[0]
    targets = queries.shape[0]
    raw_pool = raw[...]
    emb = dot(raw_pool, enc[...]).astype(BF16)
    key = dot(emb, weights[1]).astype(BF16)
    value = dot(emb, weights[2]).astype(BF16)
    key_t = dot_nt(weights[1].T, emb).astype(BF16)
    value_t = dot_nt(weights[2].T, emb).astype(BF16)
    pair_bias = jnp.concatenate([bias[...], bias[...]], axis=1)
    head_size = width // HEADS
    upper = iota((2 * head_size, targets), 0) < head_size
    mixed_parts, qproj_parts, key_parts, value_parts = [], [], [], []
    for pair in range(HEADS // 2):
        rows = slice(pair * 2 * targets, (pair + 1) * 2 * targets)
        wide = slice(pair * 2 * head_size, (pair + 1) * 2 * head_size)
        query_pair = query_heads[rows, wide]
        mixed_pair = mixed_heads[rows, wide]
        scores = dot_nt(key[:, wide], query_pair) + pair_bias
        raised = jnp.exp(scores - jnp.max(scores, axis=0, keepdims=True))
        attend = raised * (1.0 / jnp.sum(raised, axis=0, keepdims=True))
        attend_low = attend.astype(BF16)
        weighted = attend * dot_nt(value[:, wide], mixed_pair)
        score_low = (weighted - attend * jnp.sum(weighted, axis=0, keepdims=True)).astype(BF16)
        value_parts.append(dot(attend_low, mixed_pair).astype(BF16))
        key_parts.append(dot(score_low, query_pair).astype(BF16))
        mixed_both = dot(value_t[wide], attend_low)
        qproj_both = dot(key_t[wide], score_low)
        mixed_parts.append(jnp.where(upper, mixed_both[:, :targets], mixed_both[:, targets:]))
        qproj_parts.append(jnp.where(upper, qproj_both[:, :targets], qproj_both[:, targets:]))
    mixed_t = jnp.concatenate(mixed_parts, axis=0).astype(BF16)
    grad_qproj = (jnp.concatenate(qproj_parts, axis=0) * scale).T.astype(BF16)
    grad_query[...] = dot_nt(grad_qproj, weights[0]).astype(BF16)
    key_low = jnp.concatenate(key_parts, axis=1)
    value_low = jnp.concatenate(value_parts, axis=1)
    emb_grad = (dot_nt(key_low, weights[1]) + dot_nt(value_low, weights[2])).astype(BF16)
    both = dot_tn(emb, jnp.concatenate([key_low, value_low], axis=1))
    grads[0:width, :] = dot_tn(queries[...], grad_qproj).astype(BF16)
    grads[width : 2 * width, :] = both[:, :width].astype(BF16)
    grads[2 * width : 3 * width, :] = both[:, width:].astype(BF16)
    grads[3 * width : 4 * width, :] = dot(mixed_t, out_grad[...]).astype(BF16)
    grads[4 * width : 5 * width, :] = dot_tn(raw_pool, emb_grad).astype(BF16)
    core = lax.axis_index("clu") % 2
    sort_rows(core, emb_grad, keep_rows, give_rows)
    pieces, _, part, _ = keep.shape
    for q in range(pieces):
        base = 2 * mirrored(q, pieces)
        for m in range(MATRICES):
            at = m * width + base * part
            kept = pl.ds(pl.multiple_of(at + core * part, part), part)
            given = pl.ds(pl.multiple_of(at + (1 - core) * part, part), part)
            keep[q, m] = grads[kept, :]
            send[q, m] = grads[given, :]


def attention(scale, owners, raw_pool, enc, weights, queries, out_grad, bias, query_heads, mixed_heads):
    width = enc.shape[0]
    half = jax.ShapeDtypeStruct((owners // 4, MATRICES, 2 * width // owners, width), BF16)
    chips = owners // 2
    rows = jax.ShapeDtypeStruct((chips, raw_pool.shape[0] // owners, width), BF16)
    return pl.pallas_call(
        functools.partial(attention_kernel, scale),
        out_shape=[
            rows,
            rows,
            jax.ShapeDtypeStruct(queries.shape, BF16),
            half,
            half,
        ],
        scratch_shapes=[pltpu.VMEM((MATRICES * width, width), BF16)],
        compiler_params=pltpu.CompilerParams(vmem_limit_bytes=VMEM_LIMIT),
    )(raw_pool, enc, weights, queries, out_grad, bias, query_heads, mixed_heads)


def add_low(a, b):
    return (a.astype(F32) + b.astype(F32)).astype(BF16)


def split_kernel(bit, keep, got, kept, given):
    side = lax.shift_right_logical(lax.axis_index("clu"), bit) & 1
    half = kept.shape[0]
    for i in range(half):
        own = side * half + i
        other = (1 - side) * half + i
        kept[i] = add_low(keep[own], got[own])
        given[i] = add_low(keep[other], got[other])


def split(bit, keep, got, flops):
    half = jax.ShapeDtypeStruct((keep.shape[0] // 2,) + keep.shape[1:], BF16)
    return pl.pallas_call(
        functools.partial(split_kernel, bit),
        out_shape=[half, half],
        compiler_params=SMALL,
        cost_estimate=pl.CostEstimate(flops=flops, bytes_accessed=4 * keep.size, transcendentals=0),
    )(keep, got)


def sum_kernel(a, b, out):
    out[...] = add_low(a[...], b[...])


def sum_rows(a, b):
    return pl.pallas_call(
        sum_kernel, out_shape=jax.ShapeDtypeStruct(a.shape, BF16), compiler_params=SMALL
    )(a, b)


def place_kernel(masks, *refs):
    *sources, attn, enc = refs
    _, matrices, part, _ = sources[0].shape
    place_of = lax.rem(lax.axis_index("clu"), enc.shape[0] // part)
    for source, flips in zip(sources, masks):
        for k, flip in enumerate(flips):
            rows = pl.ds(pl.multiple_of((place_of ^ flip) * part, part), part)
            for m in range(matrices - 1):
                attn[m, rows, :] = source[k, m].astype(F32)
            enc[rows, :] = source[k, matrices - 1].astype(F32)


def place(pieces):
    width = pieces[0][0].shape[3]
    return pl.pallas_call(
        functools.partial(place_kernel, [flips for _, flips in pieces]),
        out_shape=[
            jax.ShapeDtypeStruct((MATRICES - 1, width, width), F32),
            jax.ShapeDtypeStruct((width, width), F32),
        ],
        compiler_params=SMALL,
    )(*[piece for piece, _ in pieces])


def rows_kernel(counts, onehot_t, table, back, out, share, filled, sem):
    clusters = counts.shape[1]
    total = dot(onehot_t[...], back[...])
    share[...] = (total / column_of(counts[...].astype(F32))).astype(BF16)

    def block(k):
        rows = pl.ds(pl.multiple_of(k * 256, 256), 256)
        return pltpu.make_async_copy(filled.at[rows], out.at[rows], sem.at[k])

    def fill(k, carry):
        onehot = member_onehot(table, k * 2, clusters)
        rows = pl.ds(pl.multiple_of(k * 256, 256), 256)
        filled[rows, :] = dot_tn(onehot, share[...]).astype(BF16)
        block(k).start()
        return carry

    def finish(k, carry):
        block(k).wait()
        return carry

    blocks = out.shape[0] // 256
    lax.fori_loop(0, blocks, fill, 0, unroll=4)
    lax.fori_loop(0, blocks, finish, 0)


def member_grads(counts, onehot_t, table, back, rows):
    clusters = counts.shape[1]
    width = back.shape[1]
    return pl.pallas_call(
        rows_kernel,
        out_specs=pl.BlockSpec(memory_space=pltpu.HBM),
        out_shape=jax.ShapeDtypeStruct((rows, width), BF16),
        scratch_shapes=[
            pltpu.VMEM((clusters, width), BF16),
            pltpu.VMEM((rows, width), BF16),
            pltpu.SemaphoreType.DMA((rows // 256,)),
        ],
        compiler_params=pltpu.CompilerParams(vmem_limit_bytes=VMEM_LIMIT),
        cost_estimate=pl.CostEstimate(
            flops=2 * rows * clusters * width, bytes_accessed=2 * rows * width, transcendentals=0
        ),
    )(counts, onehot_t, table, back)


def local(raw_rows, enc_weight, counts, member_rows, pool, picks, queries, attn_weights, out_grad):
    rows, width = raw_rows.shape
    owners = lax.axis_size("clu")
    pooled = pool.shape[1]
    clusters = counts.shape[1]
    scale = (width // HEADS) ** -0.5
    bits = owners.bit_length() - 1

    def exchange(flip, block):
        return lax.ppermute(block, "clu", [(d, d ^ flip) for d in range(owners)])

    def swap(blocks):
        groups = [list(range(core, owners, 2)) for core in range(2)]
        return lax.all_to_all(
            blocks, "clu", split_axis=0, concat_axis=0, axis_index_groups=groups, tiled=True
        )

    chips = owners // 2
    got = swap(pool.reshape(chips, 1, LANES))
    means, table = cluster_means(counts, member_rows, raw_rows)
    beside = exchange(1, got)
    got, beside = got.reshape(chips, LANES), beside.reshape(chips, LANES)
    onehot_t, keep, give = select_rows(got, beside, means, pooled)
    raw_pool = swap(pair_up(keep, exchange(1, give))).reshape(pooled, width)
    bias, query_heads, mixed_heads = target_terms(
        scale, picks.T, queries, out_grad, attn_weights, pooled
    )
    keep_rows, give_rows, grad_query, keep, given = attention(
        scale, owners, raw_pool, enc_weight, attn_weights, queries, out_grad, bias, query_heads, mixed_heads
    )
    got, got_rows = exchange(1, given), exchange(1, give_rows)
    keep, given = split(1, keep, got, keep.size)
    back = pair_up(keep_rows, got_rows)
    given, back = lax.optimization_barrier((given, back))
    got = exchange(2, given)
    back = swap(back).reshape(pooled, width)
    keep, given = split(2, keep, got, WEIGHT)
    for bit in range(2, bits - 2):
        keep, given = split(bit + 1, keep, exchange(1 << bit, given), keep.size)
    own = sum_rows(keep, exchange(owners // 4, given))
    got = exchange(owners // 2, own)
    grad_rows = member_grads(counts, onehot_t, table, back, rows)
    got, grad_rows = lax.optimization_barrier((got, grad_rows))
    own = sum_rows(own, got)
    masks = [0]
    for bit in range(bits - 2, 2, -1):
        own = jnp.concatenate([own, exchange(1 << bit, own)])
        masks = masks + [mask ^ (1 << bit) for mask in masks]
    chip = jnp.concatenate([own] + [exchange(flip, own) for flip in (4, 2, 6)])
    masks = [mask ^ flip for flip in (0, 4, 2, 6) for mask in masks]
    beside = exchange(1, chip)
    grad_attn, grad_encoder = place([(chip, masks), (beside, [mask ^ 1 for mask in masks])])
    return grad_query, grad_rows, grad_attn, grad_encoder


def solution(mesh):
    split = P(("grp", "clu"), None)
    in_specs = (split, P(), split, split, split, split, split, P(), split)
    out_specs = (split, split, P("grp", None, None), P("grp", None))
    return jax.shard_map(local, mesh=mesh, in_specs=in_specs, out_specs=out_specs, check_vma=False)
```

```python
import functools

import jax
import jax.numpy as jnp
from jax import lax
from jax.experimental import pallas as pl
from jax.experimental.pallas import tpu as pltpu
from jax.sharding import PartitionSpec as P

HEADS = 4
MATRICES = 5
WEIGHT = 10**11
LANES = 128
F32 = jnp.float32
BF16 = jnp.bfloat16
VMEM_LIMIT = 32 * 1024 * 1024
MOST_VMEM = 51 * 1024 * 1024
SMALL = pltpu.CompilerParams(vmem_limit_bytes=8 * 1024 * 1024)


def dot(a, b):
    return jnp.dot(a, b, preferred_element_type=F32)


def dot_nt(a, b):
    return lax.dot_general(a, b, (((1,), (1,)), ((), ())), preferred_element_type=F32)


def dot_tn(a, b):
    return lax.dot_general(a, b, (((0,), (0,)), ((), ())), preferred_element_type=F32)


def iota(shape, dim):
    return lax.broadcasted_iota(jnp.int32, shape, dim)


def ones_where(cond):
    return jnp.where(cond, 1.0, 0.0).astype(BF16)


def column_of(row):
    n = row.shape[1]
    wide = jnp.where(iota((n, n), 0) == iota((n, n), 1), row, 0.0)
    return jnp.sum(wide, axis=1, keepdims=True)


def member_onehot(table_ref, at, clusters):
    sub = iota((clusters, LANES), 0).astype(F32)
    parts = [ones_where(table_ref[pl.ds(at + k, 1), :] == sub) for k in range(2)]
    return jnp.concatenate(parts, axis=1)


def running(rows, cols, strict):
    gap = iota((rows, cols), 1) - iota((rows, cols), 0)
    return ones_where(gap > 0 if strict else gap >= 0)


def position_clusters(counts_row, groups):
    clusters = counts_row.shape[1]
    padded = jnp.broadcast_to(counts_row.astype(F32), (16, clusters)).astype(BF16)
    ends = dot(padded, running(clusters, clusters, False))[0:1].astype(jnp.int32)
    high = ones_where(ends // LANES == iota((groups, clusters), 0))
    low = ones_where(ends % LANES == iota((LANES, clusters), 0))
    marks = dot_nt(high, low).astype(BF16)
    within = dot(marks, running(LANES, LANES, False))
    totals = jnp.sum(marks.astype(F32), axis=1, keepdims=True)
    wide = jnp.broadcast_to(totals, (groups, LANES)).astype(BF16)
    before = lax.dot_general(
        running(groups, groups, True), wide, (((0,), (0,)), ((), ())), preferred_element_type=F32
    )
    return within + before


def means_kernel(
    counts_h, members_h, raw_h, mean_out, table, counts_v, members, raw, small_sem, raw_sem
):
    clusters = counts_v.shape[1]
    groups = members.shape[0]
    parts = raw_sem.shape[0]
    part = raw.shape[0] // parts
    small = [
        pltpu.make_async_copy(counts_h, counts_v, small_sem.at[0]),
        pltpu.make_async_copy(members_h, members, small_sem.at[1]),
    ]
    large = [
        pltpu.make_async_copy(
            raw_h.at[pl.ds(k * part, part)], raw.at[pl.ds(k * part, part)], raw_sem.at[k]
        )
        for k in range(parts)
    ]
    for copy in small + large:
        copy.start()
    for copy in small:
        copy.wait()
    cluster = position_clusters(counts_v[...], groups)
    rows = members[...]
    high = rows // LANES
    low = rows % LANES
    total = jnp.zeros((groups, LANES), F32)
    high_iota = iota((groups, LANES), 0)
    low_iota = iota((LANES, LANES), 0)
    for k in range(0, groups, 2):
        a_parts, b_parts = [], []
        for m in (k, k + 1):
            a_parts.append(
                jnp.where(high[m : m + 1] == high_iota, cluster[m : m + 1], 0.0).astype(BF16)
            )
            b_parts.append(ones_where(low[m : m + 1] == low_iota))
        total = total + dot_nt(jnp.concatenate(a_parts, axis=1), jnp.concatenate(b_parts, axis=1))
    table[...] = total
    count_column = column_of(counts_v[...].astype(F32))
    sums = jnp.zeros((clusters, raw.shape[1]), F32)
    for p in range(parts):
        large[p].wait()
        for k in range(part // 256):
            at = p * part + k * 256
            onehot = member_onehot(table, at // LANES, clusters)
            sums = sums + dot(onehot, raw[at : at + 256, :])
    mean_out[...] = (sums / count_column).astype(BF16)


def cluster_means(counts, members, raw_rows):
    clusters = counts.shape[1]
    rows, width = raw_rows.shape
    groups = rows // LANES
    parts = 8
    return pl.pallas_call(
        means_kernel,
        in_specs=[pl.BlockSpec(memory_space=pltpu.HBM)] * 3,
        out_shape=[
            jax.ShapeDtypeStruct((clusters, width), BF16),
            jax.ShapeDtypeStruct((groups, LANES), F32),
        ],
        scratch_shapes=[
            pltpu.VMEM((1, clusters), jnp.int32),
            pltpu.VMEM((groups, LANES), jnp.int32),
            pltpu.VMEM((rows, width), BF16),
            pltpu.SemaphoreType.DMA((2,)),
            pltpu.SemaphoreType.DMA((parts,)),
        ],
        compiler_params=pltpu.CompilerParams(vmem_limit_bytes=MOST_VMEM),
        cost_estimate=pl.CostEstimate(
            flops=2 * rows * clusters * width, bytes_accessed=2 * rows * width, transcendentals=0
        ),
    )(counts, members.reshape(groups, LANES), raw_rows)


def select_kernel(got, means, onehot_t, keep, give):
    clusters = means.shape[0]
    chips, per_owner, _ = keep.shape
    me = lax.axis_index("clu")
    parity = me % 2
    half = LANES // 2
    wanted = lax.rem(got[...], clusters)
    turned = pltpu.roll(wanted, half, 1)
    first = jnp.where(parity == 0, wanted, turned)
    second = jnp.where(parity == 0, turned, wanted)
    left = iota((1, LANES), 1) < half
    for k in range(chips):
        row = jnp.where(left, first[2 * k : 2 * k + 1], second[2 * k + 1 : 2 * k + 2])
        onehot_t[:, k * LANES : (k + 1) * LANES] = ones_where(row == iota((clusters, LANES), 0))
    sent = dot_tn(onehot_t[...], means[...]).astype(BF16)
    for k in range(chips):
        place = lax.shift_right_logical(me, 1) ^ k
        even = sent[2 * k * per_owner : (2 * k + 1) * per_owner]
        odd = sent[(2 * k + 1) * per_owner : (2 * k + 2) * per_owner]
        keep[place] = jnp.where(parity == 0, even, odd)
        give[place] = jnp.where(parity == 0, odd, even)


def select_rows(got, means, pooled):
    clusters, width = means.shape
    chips = got.shape[0] // 2
    half = jax.ShapeDtypeStruct((chips, pooled // chips // 2, width), BF16)
    return pl.pallas_call(
        select_kernel,
        out_shape=[jax.ShapeDtypeStruct((clusters, pooled), BF16), half, half],
        compiler_params=pltpu.CompilerParams(vmem_limit_bytes=VMEM_LIMIT),
    )(got, means)


def pair_kernel(keep, got, *outs):
    parity = lax.axis_index("clu") % 2
    per_owner = keep.shape[1]
    for k, out in enumerate(outs):
        out[pl.ds(pl.multiple_of(parity * per_owner, per_owner), per_owner), :] = keep[k]
        out[pl.ds(pl.multiple_of((1 - parity) * per_owner, per_owner), per_owner), :] = got[k]


def pair_up(keep, got):
    chips, per_owner, width = keep.shape
    return pl.pallas_call(
        pair_kernel,
        out_shape=[jax.ShapeDtypeStruct((2 * per_owner, width), BF16)] * chips,
        compiler_params=SMALL,
    )(keep, got)


def spread_heads(rows):
    head = iota(rows.shape, 1) // (rows.shape[1] // HEADS)
    return jnp.concatenate([jnp.where(head == h, rows, 0.0) for h in range(HEADS)], axis=0).astype(
        BF16
    )


def targets_kernel(scale, picks, queries, out_grad, weights, bias, query_heads, mixed_heads):
    query_proj = dot(queries[...], weights[0]).astype(BF16)
    query_heads[...] = spread_heads(query_proj.astype(F32) * scale)
    grad_mixed = dot_nt(out_grad[...], weights[3]).astype(BF16)
    mixed_heads[...] = spread_heads(grad_mixed.astype(F32))
    count, targets = picks.shape
    block = 128

    def body(b, carry):
        at = pl.multiple_of(b * block, block)
        chip = lax.shift_right_logical(lax.axis_index("clu"), 1) ^ b
        slot = iota((block, targets), 0) + chip * block
        found = jnp.zeros((block, targets), F32)
        for i in range(count):
            found = jnp.where(picks[i : i + 1, :] == slot, 1.0, found)
        bias[pl.ds(at, block), :] = jnp.where(found > 0.5, 0.0, -1e30)
        return carry

    lax.fori_loop(0, bias.shape[0] // block, body, 0)


def target_terms(scale, picks_t, queries, out_grad, weights, pooled):
    targets, width = queries.shape
    return pl.pallas_call(
        functools.partial(targets_kernel, scale),
        out_shape=[
            jax.ShapeDtypeStruct((pooled, targets), F32),
            jax.ShapeDtypeStruct((HEADS * targets, width), BF16),
            jax.ShapeDtypeStruct((HEADS * targets, width), BF16),
        ],
        compiler_params=pltpu.CompilerParams(vmem_limit_bytes=VMEM_LIMIT),
        cost_estimate=pl.CostEstimate(
            flops=4 * targets * pooled * picks_t.shape[0],
            bytes_accessed=4 * pooled * targets,
            transcendentals=0,
        ),
    )(picks_t, queries, out_grad, weights)


def mirrored(number, count):
    out, size = 0, 1
    while size < count:
        out = out * 2 + number % 2
        number //= 2
        size *= 2
    return out


def chip_order_kernel(keep, got, out):
    me = lax.axis_index("clu")
    chips, part, _ = keep.shape
    own = pl.ds(pl.multiple_of(me % 2 * part, part), part)
    other = pl.ds(pl.multiple_of((1 - me % 2) * part, part), part)
    for k in range(chips):
        place = lax.shift_right_logical(me, 1) ^ k
        out[place, own, :] = keep[k]
        out[place, other, :] = got[k]


def chip_order(keep, got):
    chips, part, width = keep.shape
    return pl.pallas_call(
        chip_order_kernel,
        out_shape=jax.ShapeDtypeStruct((chips, 2 * part, width), BF16),
        compiler_params=SMALL,
    )(keep, got)


def attention_kernel(scale, chips, *refs):
    raws = refs[:chips]
    enc, weights, queries, out_grad, bias, query_heads, mixed_heads = refs[chips : chips + 7]
    keep_rows, give_rows, grad_query, keep, send, grads = refs[chips + 7 :]
    width = enc.shape[0]
    targets = queries.shape[0]
    raw_pool = jnp.concatenate([raw[...] for raw in raws], axis=0)
    emb = dot(raw_pool, enc[...]).astype(BF16)
    key = dot(emb, weights[1]).astype(BF16)
    value = dot(emb, weights[2]).astype(BF16)
    key_t = dot_nt(weights[1].T, emb).astype(BF16)
    value_t = dot_nt(weights[2].T, emb).astype(BF16)
    pair_bias = jnp.concatenate([bias[...], bias[...]], axis=1)
    head_size = width // HEADS
    upper = iota((2 * head_size, targets), 0) < head_size
    mixed_parts, qproj_parts, key_parts, value_parts = [], [], [], []
    for pair in range(HEADS // 2):
        rows = slice(pair * 2 * targets, (pair + 1) * 2 * targets)
        wide = slice(pair * 2 * head_size, (pair + 1) * 2 * head_size)
        query_pair = query_heads[rows, wide]
        mixed_pair = mixed_heads[rows, wide]
        scores = dot_nt(key[:, wide], query_pair) + pair_bias
        raised = jnp.exp(scores - jnp.max(scores, axis=0, keepdims=True))
        attend = raised * (1.0 / jnp.sum(raised, axis=0, keepdims=True))
        attend_low = attend.astype(BF16)
        weighted = attend * dot_nt(value[:, wide], mixed_pair)
        score_low = (weighted - attend * jnp.sum(weighted, axis=0, keepdims=True)).astype(BF16)
        value_parts.append(dot(attend_low, mixed_pair).astype(BF16))
        key_parts.append(dot(score_low, query_pair).astype(BF16))
        mixed_both = dot(value_t[wide], attend_low)
        qproj_both = dot(key_t[wide], score_low)
        mixed_parts.append(jnp.where(upper, mixed_both[:, :targets], mixed_both[:, targets:]))
        qproj_parts.append(jnp.where(upper, qproj_both[:, :targets], qproj_both[:, targets:]))
    mixed_t = jnp.concatenate(mixed_parts, axis=0).astype(BF16)
    grad_qproj = (jnp.concatenate(qproj_parts, axis=0) * scale).T.astype(BF16)
    grad_query[...] = dot_nt(grad_qproj, weights[0]).astype(BF16)
    key_low = jnp.concatenate(key_parts, axis=1)
    value_low = jnp.concatenate(value_parts, axis=1)
    emb_grad = (dot_nt(key_low, weights[1]) + dot_nt(value_low, weights[2])).astype(BF16)
    both = dot_tn(emb, jnp.concatenate([key_low, value_low], axis=1))
    grads[0:width, :] = dot_tn(queries[...], grad_qproj).astype(BF16)
    grads[width : 2 * width, :] = both[:, :width].astype(BF16)
    grads[2 * width : 3 * width, :] = both[:, width:].astype(BF16)
    grads[3 * width : 4 * width, :] = dot(mixed_t, out_grad[...]).astype(BF16)
    grads[4 * width : 5 * width, :] = dot_tn(raw_pool, emb_grad).astype(BF16)
    core = lax.axis_index("clu") % 2
    half = keep_rows.shape[1]
    for k in range(chips):
        even = emb_grad[2 * k * half : (2 * k + 1) * half]
        odd = emb_grad[(2 * k + 1) * half : (2 * k + 2) * half]
        keep_rows[k] = jnp.where(core == 0, even, odd)
        give_rows[k] = jnp.where(core == 0, odd, even)
    pieces, _, part, _ = keep.shape
    for q in range(pieces):
        base = 2 * mirrored(q, pieces)
        for m in range(MATRICES):
            at = m * width + base * part
            kept = pl.ds(pl.multiple_of(at + core * part, part), part)
            given = pl.ds(pl.multiple_of(at + (1 - core) * part, part), part)
            keep[q, m] = grads[kept, :]
            send[q, m] = grads[given, :]


def attention(scale, owners, raws, enc, weights, queries, out_grad, bias, query_heads, mixed_heads):
    width = enc.shape[0]
    half = jax.ShapeDtypeStruct((owners // 4, MATRICES, 2 * width // owners, width), BF16)
    rows = jax.ShapeDtypeStruct((len(raws), raws[0].shape[0] // 2, width), BF16)
    return pl.pallas_call(
        functools.partial(attention_kernel, scale, len(raws)),
        out_shape=[
            rows,
            rows,
            jax.ShapeDtypeStruct(queries.shape, BF16),
            half,
            half,
        ],
        scratch_shapes=[pltpu.VMEM((MATRICES * width, width), BF16)],
        compiler_params=pltpu.CompilerParams(vmem_limit_bytes=VMEM_LIMIT),
    )(*raws, enc, weights, queries, out_grad, bias, query_heads, mixed_heads)


def add_low(a, b):
    return (a.astype(F32) + b.astype(F32)).astype(BF16)


def split_kernel(bit, keep, got, kept, given):
    side = lax.shift_right_logical(lax.axis_index("clu"), bit) & 1
    half = kept.shape[0]
    for i in range(half):
        own = side * half + i
        other = (1 - side) * half + i
        kept[i] = add_low(keep[own], got[own])
        given[i] = add_low(keep[other], got[other])


def split(bit, keep, got, flops):
    half = jax.ShapeDtypeStruct((keep.shape[0] // 2,) + keep.shape[1:], BF16)
    return pl.pallas_call(
        functools.partial(split_kernel, bit),
        out_shape=[half, half],
        compiler_params=SMALL,
        cost_estimate=pl.CostEstimate(flops=flops, bytes_accessed=4 * keep.size, transcendentals=0),
    )(keep, got)


def sum_kernel(a, b, out):
    out[...] = add_low(a[...], b[...])


def sum_rows(a, b):
    return pl.pallas_call(
        sum_kernel, out_shape=jax.ShapeDtypeStruct(a.shape, BF16), compiler_params=SMALL
    )(a, b)


def place_kernel(masks, held, *refs):
    attn, enc, wide, sem = refs[-4:]
    pieces, matrices, part, _ = held.shape
    place_of = lax.rem(lax.axis_index("clu"), enc.shape[0] // part)
    copies = []
    for k, flip in zip(range(pieces), masks):
        rows = pl.ds(pl.multiple_of((place_of ^ flip) * part, part), part)
        for m in range(matrices):
            wide[k, m] = held[k, m].astype(F32)
            target = attn.at[m, rows] if m < matrices - 1 else enc.at[rows]
            copies.append(pltpu.make_async_copy(wide.at[k, m], target, sem.at[k, m]))
            copies[-1].start()
    for copy in copies:
        copy.wait()


def place(masks, held, filled=()):
    pieces, matrices, _, width = held.shape
    return pl.pallas_call(
        functools.partial(place_kernel, masks),
        in_specs=[pl.BlockSpec(memory_space=pltpu.VMEM)]
        + [pl.BlockSpec(memory_space=pl.ANY)] * len(filled),
        out_specs=[pl.BlockSpec(memory_space=pl.ANY)] * 2,
        out_shape=[
            jax.ShapeDtypeStruct((matrices - 1, width, width), F32),
            jax.ShapeDtypeStruct((width, width), F32),
        ],
        scratch_shapes=[
            pltpu.VMEM(held.shape, F32),
            pltpu.SemaphoreType.DMA((pieces, matrices)),
        ],
        input_output_aliases={1 + k: k for k in range(len(filled))},
        compiler_params=SMALL,
        cost_estimate=pl.CostEstimate(flops=0, bytes_accessed=4 * held.size, transcendentals=0),
    )(held, *filled)


def rows_kernel(counts, onehot_t, table, back, out, share, filled, sem):
    clusters = counts.shape[1]
    total = dot(onehot_t[...], back[...])
    share[...] = (total / column_of(counts[...].astype(F32))).astype(BF16)

    def block(k):
        rows = pl.ds(pl.multiple_of(k * 256, 256), 256)
        return pltpu.make_async_copy(filled.at[rows], out.at[rows], sem.at[k])

    def fill(k, carry):
        onehot = member_onehot(table, k * 2, clusters)
        rows = pl.ds(pl.multiple_of(k * 256, 256), 256)
        filled[rows, :] = dot_tn(onehot, share[...]).astype(BF16)
        block(k).start()
        return carry

    def finish(k, carry):
        block(k).wait()
        return carry

    blocks = out.shape[0] // 256
    lax.fori_loop(0, blocks, fill, 0, unroll=4)
    lax.fori_loop(0, blocks, finish, 0)


def member_grads(counts, onehot_t, table, back, rows):
    clusters = counts.shape[1]
    width = back.shape[1]
    return pl.pallas_call(
        rows_kernel,
        out_specs=pl.BlockSpec(memory_space=pltpu.HBM),
        out_shape=jax.ShapeDtypeStruct((rows, width), BF16),
        scratch_shapes=[
            pltpu.VMEM((clusters, width), BF16),
            pltpu.VMEM((rows, width), BF16),
            pltpu.SemaphoreType.DMA((rows // 256,)),
        ],
        compiler_params=pltpu.CompilerParams(vmem_limit_bytes=VMEM_LIMIT),
        cost_estimate=pl.CostEstimate(
            flops=2 * rows * clusters * width, bytes_accessed=2 * rows * width, transcendentals=0
        ),
    )(counts, onehot_t, table, back)


def swap(blocks):
    return lax.all_to_all(blocks, "clu", split_axis=0, concat_axis=0, tiled=True)


def local(raw_rows, enc_weight, counts, member_rows, pool, picks, queries, attn_weights, out_grad):
    rows, width = raw_rows.shape
    owners = lax.axis_size("clu")
    pooled = pool.shape[1]
    clusters = counts.shape[1]
    scale = (width // HEADS) ** -0.5
    bits = owners.bit_length() - 1

    def exchange(flip, block):
        return lax.ppermute(block, "clu", [(d, d ^ flip) for d in range(owners)])

    pairs = pool.reshape(owners // 2, 1, 1, LANES)
    asking = jnp.broadcast_to(pairs, (owners // 2, 2, 1, LANES)).reshape(owners, 1, LANES)
    got = swap(asking).reshape(owners, LANES)
    means, table = cluster_means(counts, member_rows, raw_rows)
    onehot_t, keep, give = select_rows(got, means, pooled)
    paired = pair_up(keep, exchange(1, give))
    far_first = {k: exchange(2 * k, paired[k]) for k in range(owners // 2 - 1, 0, -1)}
    raws = [paired[0]] + [far_first[k] for k in range(1, owners // 2)]
    bias, query_heads, mixed_heads = target_terms(
        scale, picks.T, queries, out_grad, attn_weights, pooled
    )
    keep_rows, give_rows, grad_query, keep, given = attention(
        scale, owners, raws, enc_weight, attn_weights, queries, out_grad, bias, query_heads, mixed_heads
    )
    got, got_rows = exchange(1, given), exchange(1, give_rows)
    keep, given = split(1, keep, got, keep.size)
    back = chip_order(keep_rows, got_rows)
    given, back = lax.optimization_barrier((given, back))
    got = exchange(2, given)
    parities = [list(range(core, owners, 2)) for core in range(2)]
    back = lax.all_to_all(
        back, "clu", split_axis=0, concat_axis=0, axis_index_groups=parities, tiled=True
    ).reshape(pooled, width)
    keep, given = split(2, keep, got, WEIGHT)
    for bit in range(2, bits - 2):
        keep, given = split(bit + 1, keep, exchange(1 << bit, given), keep.size)
    own = sum_rows(keep, exchange(owners // 4, given))
    got = exchange(owners // 2, own)
    grad_rows = member_grads(counts, onehot_t, table, back, rows)
    got, grad_rows = lax.optimization_barrier((got, grad_rows))
    own = sum_rows(own, got)
    masks = [0]
    for bit in range(bits - 2, 2, -1):
        own = jnp.concatenate([own, exchange(1 << bit, own)])
        masks = masks + [mask ^ (1 << bit) for mask in masks]
    chip = jnp.concatenate([own] + [exchange(flip, own) for flip in (4, 2, 6)])
    masks = [mask ^ flip for flip in (0, 4, 2, 6) for mask in masks]
    beside = exchange(1, chip)
    placed = place(masks, chip)
    grad_attn, grad_encoder = place([mask ^ 1 for mask in masks], beside, placed)
    return grad_query, grad_rows, grad_attn, grad_encoder


def solution(mesh):
    split = P(("grp", "clu"), None)
    in_specs = (split, P(), split, split, split, split, split, P(), split)
    out_specs = (split, split, P("grp", None, None), P("grp", None))
    return jax.shard_map(local, mesh=mesh, in_specs=in_specs, out_specs=out_specs, check_vma=False)
```

```python
import functools

import jax
import jax.numpy as jnp
from jax import lax
from jax.experimental import pallas as pl
from jax.experimental.pallas import tpu as pltpu
from jax.sharding import PartitionSpec as P

HEADS = 4
MATRICES = 5
WEIGHT = 10**11
LANES = 128
F32 = jnp.float32
BF16 = jnp.bfloat16
VMEM_LIMIT = 32 * 1024 * 1024
MOST_VMEM = 51 * 1024 * 1024
SMALL = pltpu.CompilerParams(vmem_limit_bytes=8 * 1024 * 1024)


def dot(a, b):
    return jnp.dot(a, b, preferred_element_type=F32)


def dot_nt(a, b):
    return lax.dot_general(a, b, (((1,), (1,)), ((), ())), preferred_element_type=F32)


def dot_tn(a, b):
    return lax.dot_general(a, b, (((0,), (0,)), ((), ())), preferred_element_type=F32)


def iota(shape, dim):
    return lax.broadcasted_iota(jnp.int32, shape, dim)


def ones_where(cond):
    return jnp.where(cond, 1.0, 0.0).astype(BF16)


def column_of(row):
    n = row.shape[1]
    wide = jnp.where(iota((n, n), 0) == iota((n, n), 1), row, 0.0)
    return jnp.sum(wide, axis=1, keepdims=True)


def member_onehot(table_ref, at, clusters):
    sub = iota((clusters, LANES), 0).astype(F32)
    parts = [ones_where(table_ref[pl.ds(at + k, 1), :] == sub) for k in range(2)]
    return jnp.concatenate(parts, axis=1)


def running(rows, cols, strict):
    gap = iota((rows, cols), 1) - iota((rows, cols), 0)
    return ones_where(gap > 0 if strict else gap >= 0)


def position_clusters(counts_row, groups):
    clusters = counts_row.shape[1]
    padded = jnp.broadcast_to(counts_row.astype(F32), (16, clusters)).astype(BF16)
    ends = dot(padded, running(clusters, clusters, False))[0:1].astype(jnp.int32)
    high = ones_where(ends // LANES == iota((groups, clusters), 0))
    low = ones_where(ends % LANES == iota((LANES, clusters), 0))
    marks = dot_nt(high, low).astype(BF16)
    within = dot(marks, running(LANES, LANES, False))
    totals = jnp.sum(marks.astype(F32), axis=1, keepdims=True)
    wide = jnp.broadcast_to(totals, (groups, LANES)).astype(BF16)
    before = lax.dot_general(
        running(groups, groups, True), wide, (((0,), (0,)), ((), ())), preferred_element_type=F32
    )
    return within + before


def means_kernel(
    counts_h, members_h, raw_h, mean_out, table, counts_v, members, raw, small_sem, raw_sem
):
    clusters = counts_v.shape[1]
    groups = members.shape[0]
    parts = raw_sem.shape[0]
    part = raw.shape[0] // parts
    small = [
        pltpu.make_async_copy(counts_h, counts_v, small_sem.at[0]),
        pltpu.make_async_copy(members_h, members, small_sem.at[1]),
    ]
    large = [
        pltpu.make_async_copy(
            raw_h.at[pl.ds(k * part, part)], raw.at[pl.ds(k * part, part)], raw_sem.at[k]
        )
        for k in range(parts)
    ]
    for copy in small + large:
        copy.start()
    for copy in small:
        copy.wait()
    cluster = position_clusters(counts_v[...], groups)
    rows = members[...]
    high = rows // LANES
    low = rows % LANES
    total = jnp.zeros((groups, LANES), F32)
    high_iota = iota((groups, LANES), 0)
    low_iota = iota((LANES, LANES), 0)
    for k in range(0, groups, 2):
        a_parts, b_parts = [], []
        for m in (k, k + 1):
            a_parts.append(
                jnp.where(high[m : m + 1] == high_iota, cluster[m : m + 1], 0.0).astype(BF16)
            )
            b_parts.append(ones_where(low[m : m + 1] == low_iota))
        total = total + dot_nt(jnp.concatenate(a_parts, axis=1), jnp.concatenate(b_parts, axis=1))
    table[...] = total
    count_column = column_of(counts_v[...].astype(F32))
    sums = jnp.zeros((clusters, raw.shape[1]), F32)
    for p in range(parts):
        large[p].wait()
        for k in range(part // 256):
            at = p * part + k * 256
            onehot = member_onehot(table, at // LANES, clusters)
            sums = sums + dot(onehot, raw[at : at + 256, :])
    mean_out[...] = (sums / count_column).astype(BF16)


def cluster_means(counts, members, raw_rows):
    clusters = counts.shape[1]
    rows, width = raw_rows.shape
    groups = rows // LANES
    parts = 8
    return pl.pallas_call(
        means_kernel,
        in_specs=[pl.BlockSpec(memory_space=pltpu.HBM)] * 3,
        out_shape=[
            jax.ShapeDtypeStruct((clusters, width), BF16),
            jax.ShapeDtypeStruct((groups, LANES), F32),
        ],
        scratch_shapes=[
            pltpu.VMEM((1, clusters), jnp.int32),
            pltpu.VMEM((groups, LANES), jnp.int32),
            pltpu.VMEM((rows, width), BF16),
            pltpu.SemaphoreType.DMA((2,)),
            pltpu.SemaphoreType.DMA((parts,)),
        ],
        compiler_params=pltpu.CompilerParams(vmem_limit_bytes=MOST_VMEM),
        cost_estimate=pl.CostEstimate(
            flops=2 * rows * clusters * width, bytes_accessed=2 * rows * width, transcendentals=0
        ),
    )(counts, members.reshape(groups, LANES), raw_rows)


def select_kernel(got, means, onehot_t, keep, give):
    clusters = means.shape[0]
    chips, per_owner, _ = keep.shape
    me = lax.axis_index("clu")
    parity = me % 2
    half = LANES // 2
    wanted = lax.rem(got[...], clusters)
    turned = pltpu.roll(wanted, half, 1)
    first = jnp.where(parity == 0, wanted, turned)
    second = jnp.where(parity == 0, turned, wanted)
    left = iota((1, LANES), 1) < half
    for k in range(chips):
        row = jnp.where(left, first[2 * k : 2 * k + 1], second[2 * k + 1 : 2 * k + 2])
        onehot_t[:, k * LANES : (k + 1) * LANES] = ones_where(row == iota((clusters, LANES), 0))
    sent = dot_tn(onehot_t[...], means[...]).astype(BF16)
    for k in range(chips):
        place = lax.shift_right_logical(me, 1) ^ k
        even = sent[2 * k * per_owner : (2 * k + 1) * per_owner]
        odd = sent[(2 * k + 1) * per_owner : (2 * k + 2) * per_owner]
        keep[place] = jnp.where(parity == 0, even, odd)
        give[place] = jnp.where(parity == 0, odd, even)


def select_rows(got, means, pooled):
    clusters, width = means.shape
    chips = got.shape[0] // 2
    half = jax.ShapeDtypeStruct((chips, pooled // chips // 2, width), BF16)
    return pl.pallas_call(
        select_kernel,
        out_shape=[jax.ShapeDtypeStruct((clusters, pooled), BF16), half, half],
        compiler_params=pltpu.CompilerParams(vmem_limit_bytes=VMEM_LIMIT),
    )(got, means)


def pair_kernel(keep, got, *outs):
    parity = lax.axis_index("clu") % 2
    per_owner = keep.shape[1]
    for k, out in enumerate(outs):
        out[pl.ds(pl.multiple_of(parity * per_owner, per_owner), per_owner), :] = keep[k]
        out[pl.ds(pl.multiple_of((1 - parity) * per_owner, per_owner), per_owner), :] = got[k]


def pair_up(keep, got):
    chips, per_owner, width = keep.shape
    return pl.pallas_call(
        pair_kernel,
        out_shape=[jax.ShapeDtypeStruct((2 * per_owner, width), BF16)] * chips,
        compiler_params=SMALL,
    )(keep, got)


def spread_heads(rows):
    head = iota(rows.shape, 1) // (rows.shape[1] // HEADS)
    return jnp.concatenate([jnp.where(head == h, rows, 0.0) for h in range(HEADS)], axis=0).astype(
        BF16
    )


def targets_kernel(scale, picks, queries, out_grad, weights, bias, query_heads, mixed_heads):
    query_proj = dot(queries[...], weights[0]).astype(BF16)
    query_heads[...] = spread_heads(query_proj.astype(F32) * scale)
    grad_mixed = dot_nt(out_grad[...], weights[3]).astype(BF16)
    mixed_heads[...] = spread_heads(grad_mixed.astype(F32))
    count, targets = picks.shape
    block = 128

    def body(b, carry):
        at = pl.multiple_of(b * block, block)
        chip = lax.shift_right_logical(lax.axis_index("clu"), 1) ^ b
        slot = iota((block, targets), 0) + chip * block
        found = jnp.zeros((block, targets), F32)
        for i in range(count):
            found = jnp.where(picks[i : i + 1, :] == slot, 1.0, found)
        bias[pl.ds(at, block), :] = jnp.where(found > 0.5, 0.0, -1e30)
        return carry

    lax.fori_loop(0, bias.shape[0] // block, body, 0)


def target_terms(scale, picks_t, queries, out_grad, weights, pooled):
    targets, width = queries.shape
    return pl.pallas_call(
        functools.partial(targets_kernel, scale),
        out_shape=[
            jax.ShapeDtypeStruct((pooled, targets), F32),
            jax.ShapeDtypeStruct((HEADS * targets, width), BF16),
            jax.ShapeDtypeStruct((HEADS * targets, width), BF16),
        ],
        compiler_params=pltpu.CompilerParams(vmem_limit_bytes=VMEM_LIMIT),
        cost_estimate=pl.CostEstimate(
            flops=4 * targets * pooled * picks_t.shape[0],
            bytes_accessed=4 * pooled * targets,
            transcendentals=0,
        ),
    )(picks_t, queries, out_grad, weights)


def mirrored(number, count):
    out, size = 0, 1
    while size < count:
        out = out * 2 + number % 2
        number //= 2
        size *= 2
    return out


def chip_order_kernel(keep, got, out):
    me = lax.axis_index("clu")
    chips, part, _ = keep.shape
    own = pl.ds(pl.multiple_of(me % 2 * part, part), part)
    other = pl.ds(pl.multiple_of((1 - me % 2) * part, part), part)
    for k in range(chips):
        place = lax.shift_right_logical(me, 1) ^ k
        out[place, own, :] = keep[k]
        out[place, other, :] = got[k]


def chip_order(keep, got):
    chips, part, width = keep.shape
    return pl.pallas_call(
        chip_order_kernel,
        out_shape=jax.ShapeDtypeStruct((chips, 2 * part, width), BF16),
        compiler_params=SMALL,
    )(keep, got)


def attention_kernel(scale, chips, *refs):
    raws = refs[:chips]
    enc, weights, queries, out_grad, bias, query_heads, mixed_heads = refs[chips : chips + 7]
    keep_rows, give_rows, grad_query, keep, send, grads = refs[chips + 7 :]
    width = enc.shape[0]
    targets = queries.shape[0]
    raw_pool = jnp.concatenate([raw[...] for raw in raws], axis=0)
    emb = dot(raw_pool, enc[...]).astype(BF16)
    key = dot(emb, weights[1]).astype(BF16)
    value = dot(emb, weights[2]).astype(BF16)
    key_t = dot_nt(weights[1].T, emb).astype(BF16)
    value_t = dot_nt(weights[2].T, emb).astype(BF16)
    pair_bias = jnp.concatenate([bias[...], bias[...]], axis=1)
    head_size = width // HEADS
    upper = iota((2 * head_size, targets), 0) < head_size
    mixed_parts, qproj_parts, key_parts, value_parts = [], [], [], []
    for pair in range(HEADS // 2):
        rows = slice(pair * 2 * targets, (pair + 1) * 2 * targets)
        wide = slice(pair * 2 * head_size, (pair + 1) * 2 * head_size)
        query_pair = query_heads[rows, wide]
        mixed_pair = mixed_heads[rows, wide]
        scores = dot_nt(key[:, wide], query_pair) + pair_bias
        raised = jnp.exp(scores - jnp.max(scores, axis=0, keepdims=True))
        attend = raised * (1.0 / jnp.sum(raised, axis=0, keepdims=True))
        attend_low = attend.astype(BF16)
        weighted = attend * dot_nt(value[:, wide], mixed_pair)
        score_low = (weighted - attend * jnp.sum(weighted, axis=0, keepdims=True)).astype(BF16)
        value_parts.append(dot(attend_low, mixed_pair).astype(BF16))
        key_parts.append(dot(score_low, query_pair).astype(BF16))
        mixed_both = dot(value_t[wide], attend_low)
        qproj_both = dot(key_t[wide], score_low)
        mixed_parts.append(jnp.where(upper, mixed_both[:, :targets], mixed_both[:, targets:]))
        qproj_parts.append(jnp.where(upper, qproj_both[:, :targets], qproj_both[:, targets:]))
    mixed_t = jnp.concatenate(mixed_parts, axis=0).astype(BF16)
    grad_qproj = (jnp.concatenate(qproj_parts, axis=0) * scale).T.astype(BF16)
    grad_query[...] = dot_nt(grad_qproj, weights[0]).astype(BF16)
    key_low = jnp.concatenate(key_parts, axis=1)
    value_low = jnp.concatenate(value_parts, axis=1)
    emb_grad = (dot_nt(key_low, weights[1]) + dot_nt(value_low, weights[2])).astype(BF16)
    both = dot_tn(emb, jnp.concatenate([key_low, value_low], axis=1))
    grads[0:width, :] = dot_tn(queries[...], grad_qproj).astype(BF16)
    grads[width : 2 * width, :] = both[:, :width].astype(BF16)
    grads[2 * width : 3 * width, :] = both[:, width:].astype(BF16)
    grads[3 * width : 4 * width, :] = dot(mixed_t, out_grad[...]).astype(BF16)
    grads[4 * width : 5 * width, :] = dot_tn(raw_pool, emb_grad).astype(BF16)
    core = lax.axis_index("clu") % 2
    half = keep_rows.shape[1]
    for k in range(chips):
        even = emb_grad[2 * k * half : (2 * k + 1) * half]
        odd = emb_grad[(2 * k + 1) * half : (2 * k + 2) * half]
        keep_rows[k] = jnp.where(core == 0, even, odd)
        give_rows[k] = jnp.where(core == 0, odd, even)
    pieces, _, part, _ = keep.shape
    for q in range(pieces):
        base = 2 * mirrored(q, pieces)
        for m in range(MATRICES):
            at = m * width + base * part
            kept = pl.ds(pl.multiple_of(at + core * part, part), part)
            given = pl.ds(pl.multiple_of(at + (1 - core) * part, part), part)
            keep[q, m] = grads[kept, :]
            send[q, m] = grads[given, :]


def attention(scale, owners, raws, enc, weights, queries, out_grad, bias, query_heads, mixed_heads):
    width = enc.shape[0]
    half = jax.ShapeDtypeStruct((owners // 4, MATRICES, 2 * width // owners, width), BF16)
    rows = jax.ShapeDtypeStruct((len(raws), raws[0].shape[0] // 2, width), BF16)
    return pl.pallas_call(
        functools.partial(attention_kernel, scale, len(raws)),
        out_shape=[
            rows,
            rows,
            jax.ShapeDtypeStruct(queries.shape, BF16),
            half,
            half,
        ],
        scratch_shapes=[pltpu.VMEM((MATRICES * width, width), BF16)],
        compiler_params=pltpu.CompilerParams(vmem_limit_bytes=VMEM_LIMIT),
    )(*raws, enc, weights, queries, out_grad, bias, query_heads, mixed_heads)


def add_low(a, b):
    return (a.astype(F32) + b.astype(F32)).astype(BF16)


def split_kernel(bit, keep, got, kept, given):
    side = lax.shift_right_logical(lax.axis_index("clu"), bit) & 1
    half = kept.shape[0]
    for i in range(half):
        own = side * half + i
        other = (1 - side) * half + i
        kept[i] = add_low(keep[own], got[own])
        given[i] = add_low(keep[other], got[other])


def split(bit, keep, got, flops):
    half = jax.ShapeDtypeStruct((keep.shape[0] // 2,) + keep.shape[1:], BF16)
    return pl.pallas_call(
        functools.partial(split_kernel, bit),
        out_shape=[half, half],
        compiler_params=SMALL,
        cost_estimate=pl.CostEstimate(flops=flops, bytes_accessed=4 * keep.size, transcendentals=0),
    )(keep, got)


def sum_kernel(a, b, out):
    out[...] = add_low(a[...], b[...])


def sum_rows(a, b):
    return pl.pallas_call(
        sum_kernel, out_shape=jax.ShapeDtypeStruct(a.shape, BF16), compiler_params=SMALL
    )(a, b)


def place_kernel(masks, held, *refs):
    attn, enc, wide, sem = refs[-4:]
    pieces, matrices, part, _ = held.shape
    place_of = lax.rem(lax.axis_index("clu"), enc.shape[0] // part)
    copies = []
    for k, flip in zip(range(pieces), masks):
        rows = pl.ds(pl.multiple_of((place_of ^ flip) * part, part), part)
        for m in range(matrices):
            wide[k, m] = held[k, m].astype(F32)
            target = attn.at[m, rows] if m < matrices - 1 else enc.at[rows]
            copies.append(pltpu.make_async_copy(wide.at[k, m], target, sem.at[k, m]))
            copies[-1].start()
    for copy in copies:
        copy.wait()


def place(masks, held, filled=()):
    pieces, matrices, _, width = held.shape
    return pl.pallas_call(
        functools.partial(place_kernel, masks),
        in_specs=[pl.BlockSpec(memory_space=pltpu.VMEM)]
        + [pl.BlockSpec(memory_space=pl.ANY)] * len(filled),
        out_specs=[pl.BlockSpec(memory_space=pl.ANY)] * 2,
        out_shape=[
            jax.ShapeDtypeStruct((matrices - 1, width, width), F32),
            jax.ShapeDtypeStruct((width, width), F32),
        ],
        scratch_shapes=[
            pltpu.VMEM(held.shape, F32),
            pltpu.SemaphoreType.DMA((pieces, matrices)),
        ],
        input_output_aliases={1 + k: k for k in range(len(filled))},
        compiler_params=SMALL,
        cost_estimate=pl.CostEstimate(flops=0, bytes_accessed=4 * held.size, transcendentals=0),
    )(held, *filled)


def fill_rows(first, table, share, out, filled, sem):
    clusters = share.shape[0]
    blocks = filled.shape[0] // 256

    def block(k):
        held = pl.ds(pl.multiple_of(k * 256, 256), 256)
        rows = pl.ds(pl.multiple_of((first + k) * 256, 256), 256)
        return pltpu.make_async_copy(filled.at[held], out.at[rows], sem.at[k])

    def fill(k, carry):
        onehot = member_onehot(table, (first + k) * 2, clusters)
        held = pl.ds(pl.multiple_of(k * 256, 256), 256)
        filled[held, :] = dot_tn(onehot, share[...]).astype(BF16)
        block(k).start()
        return carry

    def finish(k, carry):
        block(k).wait()
        return carry

    lax.fori_loop(0, blocks, fill, 0, unroll=4)
    lax.fori_loop(0, blocks, finish, 0)


def early_rows_kernel(counts, onehot_t, table, back, out, share, filled, sem):
    total = dot(onehot_t[...], back[...])
    share[...] = (total / column_of(counts[...].astype(F32))).astype(BF16)
    fill_rows(0, table, share, out, filled, sem)


def late_rows_kernel(first, table, share, early, out, filled, sem):
    del early
    fill_rows(first, table, share, out, filled, sem)


def rows_cost(rows, clusters, width):
    return pl.CostEstimate(
        flops=2 * rows * clusters * width, bytes_accessed=2 * rows * width, transcendentals=0
    )


def early_rows(counts, onehot_t, table, back, rows, count):
    clusters = counts.shape[1]
    width = back.shape[1]
    return pl.pallas_call(
        early_rows_kernel,
        out_specs=[
            pl.BlockSpec(memory_space=pl.ANY),
            pl.BlockSpec(memory_space=pltpu.VMEM),
        ],
        out_shape=[
            jax.ShapeDtypeStruct((rows, width), BF16),
            jax.ShapeDtypeStruct((clusters, width), BF16),
        ],
        scratch_shapes=[
            pltpu.VMEM((count, width), BF16),
            pltpu.SemaphoreType.DMA((count // 256,)),
        ],
        compiler_params=pltpu.CompilerParams(vmem_limit_bytes=VMEM_LIMIT),
        cost_estimate=rows_cost(count, clusters, width),
    )(counts, onehot_t, table, back)


def late_rows(table, share, early, first):
    rows, width = early.shape
    return pl.pallas_call(
        functools.partial(late_rows_kernel, first // 256),
        in_specs=[
            pl.BlockSpec(memory_space=pltpu.VMEM),
            pl.BlockSpec(memory_space=pltpu.VMEM),
            pl.BlockSpec(memory_space=pl.ANY),
        ],
        out_specs=pl.BlockSpec(memory_space=pl.ANY),
        out_shape=jax.ShapeDtypeStruct((rows, width), BF16),
        scratch_shapes=[
            pltpu.VMEM((rows - first, width), BF16),
            pltpu.SemaphoreType.DMA(((rows - first) // 256,)),
        ],
        input_output_aliases={2: 0},
        compiler_params=pltpu.CompilerParams(vmem_limit_bytes=VMEM_LIMIT),
        cost_estimate=rows_cost(rows - first, share.shape[0], width),
    )(table, share, early)


def swap(blocks):
    return lax.all_to_all(blocks, "clu", split_axis=0, concat_axis=0, tiled=True)


def local(raw_rows, enc_weight, counts, member_rows, pool, picks, queries, attn_weights, out_grad):
    rows, width = raw_rows.shape
    owners = lax.axis_size("clu")
    pooled = pool.shape[1]
    clusters = counts.shape[1]
    scale = (width // HEADS) ** -0.5
    bits = owners.bit_length() - 1

    def exchange(flip, block):
        return lax.ppermute(block, "clu", [(d, d ^ flip) for d in range(owners)])

    pairs = pool.reshape(owners // 2, 1, 1, LANES)
    asking = jnp.broadcast_to(pairs, (owners // 2, 2, 1, LANES)).reshape(owners, 1, LANES)
    got = swap(asking).reshape(owners, LANES)
    means, table = cluster_means(counts, member_rows, raw_rows)
    onehot_t, keep, give = select_rows(got, means, pooled)
    paired = pair_up(keep, exchange(1, give))
    far_first = {k: exchange(2 * k, paired[k]) for k in range(owners // 2 - 1, 0, -1)}
    raws = [paired[0]] + [far_first[k] for k in range(1, owners // 2)]
    bias, query_heads, mixed_heads = target_terms(
        scale, picks.T, queries, out_grad, attn_weights, pooled
    )
    keep_rows, give_rows, grad_query, keep, given = attention(
        scale, owners, raws, enc_weight, attn_weights, queries, out_grad, bias, query_heads, mixed_heads
    )
    got, got_rows = exchange(1, given), exchange(1, give_rows)
    keep, given = split(1, keep, got, keep.size)
    back = chip_order(keep_rows, got_rows)
    given, back = lax.optimization_barrier((given, back))
    got = exchange(2, given)
    parities = [list(range(core, owners, 2)) for core in range(2)]
    back = lax.all_to_all(
        back, "clu", split_axis=0, concat_axis=0, axis_index_groups=parities, tiled=True
    ).reshape(pooled, width)
    keep, given = split(2, keep, got, WEIGHT)
    for bit in range(2, bits - 2):
        keep, given = split(bit + 1, keep, exchange(1 << bit, given), keep.size)
    own = sum_rows(keep, exchange(owners // 4, given))
    got = exchange(owners // 2, own)
    early, share = early_rows(counts, onehot_t, table, back, rows, rows // 2)
    got, share = lax.optimization_barrier((got, share))
    own = sum_rows(own, got)
    masks = [0]
    for bit in range(bits - 2, 2, -1):
        own = jnp.concatenate([own, exchange(1 << bit, own)])
        masks = masks + [mask ^ (1 << bit) for mask in masks]
    passed = [exchange(flip, own) for flip in (4, 2, 6)]
    grad_rows = late_rows(table, share, early, rows // 2)
    passed, grad_rows = lax.optimization_barrier((passed, grad_rows))
    chip = jnp.concatenate([own] + passed)
    masks = [mask ^ flip for flip in (0, 4, 2, 6) for mask in masks]
    beside = exchange(1, chip)
    placed = place(masks, chip)
    grad_attn, grad_encoder = place([mask ^ 1 for mask in masks], beside, placed)
    return grad_query, grad_rows, grad_attn, grad_encoder


def solution(mesh):
    split = P(("grp", "clu"), None)
    in_specs = (split, P(), split, split, split, split, split, P(), split)
    out_specs = (split, split, P("grp", None, None), P("grp", None))
    return jax.shard_map(local, mesh=mesh, in_specs=in_specs, out_specs=out_specs, check_vma=False)
```
